32 devices in a mesh: gx: 4 (over y, core), gz: 4 (over z), ta: 2 (over x).
Axes of the slice: x: 2, y: 2, z: 4, core: 2. Of those that a mesh axis runs over, the one named last changes fastest.
Arguments:
- residual: bfloat16 [16, 2, 12, 8192], P(None, None, None, ('gx', 'gz', 'ta')), may hold values from -6 to 6
- null_vectors: bfloat16 [2, 24, 12, 8192], P(None, None, None, ('gx', 'gz', 'ta')), may hold values from -0.29882812 to 0.29882812
- clover_inverse: bfloat16 [2, 2, 6, 6, 8192], P(None, None, None, None, ('gx', 'gz', 'ta')), may hold values from -2.390625 to 2.390625
- coarse_op: float32 [32, 9, 2, 2304], P(('gx', 'gz', 'ta')), may hold values from -0.15 to 2.5
- vector_count: int32 [32], P(('gx', 'gz', 'ta')), may hold values from 12 to 24
Outputs:
- correction: bfloat16 [16, 2, 12, 8192], P(None, None, None, ('gx', 'gz', 'ta'))
The draws below stay inside these ranges and needn't reach their ends.
All inputs are finite; a program needn't handle non-finite values.
Results may differ from the reference program's by a relative error of at most 0.0029.
Values sent between devices are 32-bit elements; how exact they have to be, the bound alone decides.
No kernel may reach another device: no remote copies, remote signals or barrier semaphores. Data moves between devices by JAX's collectives and lax.ppermute only.
A program may use at most 64 MiB of HBM per device.

```python
import jax
import jax.numpy as jnp
from jax import lax

NVEC = 24
BS = 256
NRHS = 16
TBLK = 1
ITERS = 5
GY = 2
PX = 2
CBLOCKS = 32
SITES = 8192
N_GZ = 4
N_TA = 2


def draw_coarse_op(key, part):
    key = jax.random.fold_in(key, 7)
    first_key, second_key = jax.random.split(key)
    dims_all = (CBLOCKS, 9, 2, 4 * NVEC * NVEC)
    noises = jnp.clip(jax.random.normal(first_key, dims_all, jnp.float32), -4.0, 4.0)
    levels = jax.random.uniform(second_key, dims_all, jnp.float32, 1.0, 2.0)
    link_id = lax.broadcasted_iota(jnp.int32, dims_all, 1)
    re_im = lax.broadcasted_iota(jnp.int32, dims_all, 2)
    entry = lax.broadcasted_iota(jnp.int32, dims_all, 3)
    centre = (link_id == 0) & (re_im == 0) & (entry % (2 * NVEC + 1) == 0)
    spread = jnp.where(link_id == 0, 0.03, 0.035)
    return jnp.where(centre, levels, spread * noises)


def plant(values, own_key, low, top_value):
    longest = values.shape.index(max(values.shape))
    spots = []
    for shift in (0, 1):
        where = [jax.random.randint(jax.random.fold_in(own_key, axis), (), 0, length) for axis, length in enumerate(values.shape)]
        where[longest] = (where[longest] + shift) % values.shape[longest]
        spots.append(tuple(where))
    return values.at[spots[0]].set(low).at[spots[1]].set(top_value)


def level_of(key, extent, shards, smallest, top_value):
    gain = 1.0
    for dim, blocks in shards:
        heights = jax.random.uniform(jax.random.fold_in(jax.random.fold_in(key, 6), dim), (blocks,), jnp.float32, smallest / len(shards), top_value / len(shards))
        gain = gain * jnp.repeat(jnp.exp(heights), extent[dim] // blocks).reshape((-1,) + (1,) * (len(extent) - 1 - dim))
    return gain


def centred(own_key, shape, deviation, most, shards=(), kind=jnp.bfloat16):
    gain = level_of(own_key, shape, shards, -0.22, 0.18) if shards else 1.0
    array = jax.random.normal(own_key, shape, jnp.float32) * deviation * gain
    return jnp.minimum(jnp.maximum(array, -most), most).astype(kind)


def setup_inputs(seed: int = 0) -> dict:
    streams_of = jax.random.split(jax.random.key(seed), 6)
    residual = centred(streams_of[0], (NRHS, 2, 12, SITES), 1.0, 6.0, ((3, 32),))
    null_vectors = centred(streams_of[1], (2, NVEC, 12, SITES), 0.05, 0.29882812, ((3, 32),))
    clover_inverse = centred(streams_of[2], (2, 2, 6, 6, SITES), 0.4, 2.390625, ((4, 32),))
    coarse_op = draw_coarse_op(jax.random.fold_in(streams_of[5], 71), 0)
    vector_count = plant(jax.random.randint(streams_of[4], (CBLOCKS,), NVEC // 2, NVEC + 1), jax.random.fold_in(streams_of[4], 1), NVEC // 2, NVEC).astype(jnp.int32)
    return dict(residual=residual, null_vectors=null_vectors, clover_inverse=clover_inverse, coarse_op=coarse_op, vector_count=vector_count)


omega_step = 0.5
exact = lax.Precision.HIGHEST


def complex_mul(matrix, vector):
    def product(left, right):
        return jnp.einsum("bij,bjr->bir", left, right, precision=exact)
    real_part = product(matrix[:, 0], vector[:, 0]) - product(matrix[:, 1], vector[:, 1])
    imag_part = product(matrix[:, 0], vector[:, 1]) + product(matrix[:, 1], vector[:, 0])
    return jnp.stack([real_part, imag_part], 1)


def coarse_apply(operator, vector):
    coarse_dim = 2 * NVEC
    lattice = vector.reshape(PX, GY, N_GZ, N_TA * TBLK, 2, coarse_dim, NRHS)
    moved = [lattice,
             jnp.roll(lattice, -1, 0), jnp.roll(lattice, 1, 0),
             jnp.roll(lattice, -1, 1), jnp.roll(lattice, 1, 1),
             jnp.roll(lattice, -1, 2), jnp.roll(lattice, 1, 2),
             jnp.roll(lattice, -1, 3), jnp.roll(lattice, 1, 3)]
    summed = jnp.zeros((CBLOCKS, 2, coarse_dim, NRHS), jnp.float32)
    for link_id in range(9):
        summed = summed + complex_mul(operator[:, link_id], moved[link_id].reshape(CBLOCKS, 2, coarse_dim, NRHS))
    return summed


def reference(residual, null_vectors, clover_inverse, coarse_op, vector_count):
    coarse_dim = 2 * NVEC
    per_group = TBLK * N_TA * N_GZ
    groups = CBLOCKS // per_group
    width_sites = per_group * BS
    in_use = (jnp.arange(NVEC, dtype=jnp.int32)[None, :] < vector_count[:, None]).astype(jnp.float32)
    in_use = in_use[:, None, None, :, None]

    def restrict_group(index, rc_all):
        start = (index * width_sites).astype(jnp.int32)
        fine_rows = lax.dynamic_slice_in_dim(residual, start, width_sites, 3).astype(jnp.float32)
        fine_rows = fine_rows.reshape(NRHS, 2, 2, 6, per_group, BS)
        vectors = lax.dynamic_slice_in_dim(null_vectors, start, width_sites, 3).astype(jnp.float32)
        vectors = vectors.reshape(2, NVEC, 2, 6, per_group, BS)

        def contract(left, right):
            return jnp.einsum("kxcbw,rxcbw->bxkr", left, right, precision=exact)
        real_part = contract(vectors[0], fine_rows[:, 0]) + contract(vectors[1], fine_rows[:, 1])
        imag_part = contract(vectors[0], fine_rows[:, 1]) - contract(vectors[1], fine_rows[:, 0])
        block_rows = jnp.stack([real_part, imag_part], 1)
        return lax.dynamic_update_slice_in_dim(rc_all, block_rows, (index * per_group).astype(jnp.int32), 0)

    rc_all = jnp.zeros((CBLOCKS, 2, 2, NVEC, NRHS), jnp.float32)
    rc_all = lax.fori_loop(jnp.int32(0), jnp.int32(groups), restrict_group, rc_all)
    restricted = (rc_all * in_use).reshape(CBLOCKS, 2, coarse_dim, NRHS)

    operator = coarse_op.reshape(CBLOCKS, 9, 2, coarse_dim, coarse_dim)
    coarse = jnp.zeros_like(restricted)
    for sweep_id in range(ITERS):
        coarse = coarse + omega_step * (restricted - coarse_apply(operator, coarse))
    coarse_rounded = (coarse.reshape(CBLOCKS, 2, 2, NVEC, NRHS) * in_use).astype(jnp.bfloat16)

    def extend_group(index, output):
        start = (index * width_sites).astype(jnp.int32)
        fine_rows = lax.dynamic_slice_in_dim(residual, start, width_sites, 3).astype(jnp.float32)
        fine_rows = fine_rows.reshape(NRHS, 2, 2, 6, width_sites)
        vectors = lax.dynamic_slice_in_dim(null_vectors, start, width_sites, 3).astype(jnp.float32)
        vectors = vectors.reshape(2, NVEC, 2, 6, per_group, BS)
        clover = lax.dynamic_slice_in_dim(clover_inverse, start, width_sites, 4).astype(jnp.float32)
        coarse_rows = lax.dynamic_slice_in_dim(coarse_rounded, (index * per_group).astype(jnp.int32), per_group, 0)
        coarse_rows = coarse_rows.astype(jnp.float32)

        def spread_out(left, right):
            return jnp.einsum("kxcbw,bxkr->rxcbw", left, right, precision=exact)

        def local_apply(left, right):
            return jnp.einsum("xabs,rxbs->rxas", left, right, precision=exact)
        lift_real = spread_out(vectors[0], coarse_rows[:, 0]) - spread_out(vectors[1], coarse_rows[:, 1])
        lift_imag = spread_out(vectors[0], coarse_rows[:, 1]) + spread_out(vectors[1], coarse_rows[:, 0])
        local_real = local_apply(clover[0], fine_rows[:, 0]) - local_apply(clover[1], fine_rows[:, 1])
        local_imag = local_apply(clover[0], fine_rows[:, 1]) + local_apply(clover[1], fine_rows[:, 0])
        result = jnp.stack([local_real + lift_real.reshape(NRHS, 2, 6, width_sites),
                            local_imag + lift_imag.reshape(NRHS, 2, 6, width_sites)], 1)
        result = result.reshape(NRHS, 2, 12, width_sites).astype(jnp.bfloat16)
        return lax.dynamic_update_slice_in_dim(output, result, start, 3)

    output = jnp.zeros((NRHS, 2, 12, SITES), jnp.bfloat16)
    return lax.fori_loop(jnp.int32(0), jnp.int32(groups), extend_group, output)
```

```python
import jax
import jax.numpy as jnp
from jax import lax
from jax.sharding import PartitionSpec as P

ITERS = 5


omega_step = 0.5
exact = lax.Precision.HIGHEST


def routes():
    total = lax.axis_size("gx")
    plane_y = min(8, total // 2)
    plane_x = total // plane_y
    links = []
    for step in (1, -1):
        links.append(
            ("gx", tuple(((g // plane_y + step) % plane_x) * plane_y + g % plane_y for g in range(total)))
        )
    for step in (1, -1):
        links.append(
            ("gx", tuple((g // plane_y) * plane_y + (g % plane_y + step) % plane_y for g in range(total)))
        )
    for axis in ("gz", "ta"):
        count = lax.axis_size(axis)
        for step in (1, -1):
            links.append((axis, tuple((i + step) % count for i in range(count))))
    return links


def fetch(block, link):
    axis, sources = link
    return lax.ppermute(block, axis, [(source, i) for i, source in enumerate(sources)])


def body(residual, null_vectors, clover_inverse, coarse_op, vector_count):
    rhs_count = residual.shape[0]
    vec_total = null_vectors.shape[1]
    coarse_dim = 2 * vec_total
    sites = residual.shape[3]
    in_use = (lax.iota(jnp.int32, vec_total)[None, :] < vector_count[:, None]).astype(jnp.float32)[0]
    used = jnp.tile(in_use, 4)

    fine_rows = residual.transpose(2, 1, 0, 3).reshape(2, 6, 2 * rhs_count, sites)
    vectors = null_vectors.transpose(2, 0, 1, 3).reshape(2, 6, 2 * vec_total, sites)
    product = jnp.einsum("xcrs,xcks->xrk", fine_rows, vectors, preferred_element_type=jnp.float32)
    product = product.reshape(2, 2, rhs_count, 2, vec_total)
    real_part = product[:, 0, :, 0] + product[:, 1, :, 1]
    imag_part = product[:, 1, :, 0] - product[:, 0, :, 1]
    restricted = jnp.stack([real_part, imag_part]).transpose(2, 0, 1, 3)
    half = omega_step * (restricted.reshape(rhs_count, 2 * coarse_dim) * used)

    operator = coarse_op.reshape(9, 2, coarse_dim, coarse_dim)
    grouped = {}
    for link_id, link in enumerate(routes()):
        grouped.setdefault(link, []).append(operator[link_id + 1])
    order = sorted(grouped, key=lambda link: ("gz", "ta", "gx").index(link[0]))

    def real_form(matrix):
        upper = jnp.concatenate([matrix[0], -matrix[1]], 1)
        lower = jnp.concatenate([matrix[1], matrix[0]], 1)
        return omega_step * jnp.concatenate([upper, lower], 0)

    own = jnp.eye(2 * coarse_dim, dtype=jnp.float32) - real_form(operator[0])
    around = jnp.concatenate([-real_form(sum(grouped[link])) for link in order], 1)

    def apply(vector, matrix):
        return lax.dot_general(vector, matrix, (((1,), (1,)), ((), ())), precision=exact)

    coarse = half
    for sweep_id in range(ITERS - 1):
        moved = [fetch(coarse, link) for link in order]
        kept = half + apply(coarse, own)
        coarse = kept + apply(jnp.concatenate(moved, 1), around)

    rounded = (coarse * used).reshape(rhs_count, 2, 2, vec_total)
    real_rows = jnp.stack([rounded[:, 0], -rounded[:, 1]], 1)
    imag_rows = jnp.stack([rounded[:, 1], rounded[:, 0]], 1)
    weights = jnp.stack([real_rows, imag_rows]).transpose(3, 0, 1, 2, 4)
    weights = weights.reshape(2, 2 * rhs_count, 2 * vec_total).astype(jnp.bfloat16)
    lift = jnp.einsum("xrk,xcks->xcrs", weights, vectors, preferred_element_type=jnp.float32)

    rows = residual.reshape(rhs_count, 2, 2, 6, sites).astype(jnp.float32)
    clover = clover_inverse.astype(jnp.float32)

    def local_apply(left, right):
        return sum(left[:, :, b][None] * right[:, :, b][:, :, None] for b in range(6))

    local_real = local_apply(clover[0], rows[:, 0]) - local_apply(clover[1], rows[:, 1])
    local_imag = local_apply(clover[0], rows[:, 1]) + local_apply(clover[1], rows[:, 0])
    lift = lift.reshape(2, 6, 2, rhs_count, sites).transpose(3, 2, 0, 1, 4)
    result = jnp.stack([local_real, local_imag], 1) + lift
    return result.reshape(rhs_count, 2, 12, sites).astype(jnp.bfloat16)


def solution(mesh):
    in_specs = (
        P(None, None, None, ("gx", "gz", "ta")),
        P(None, None, None, ("gx", "gz", "ta")),
        P(None, None, None, None, ("gx", "gz", "ta")),
        P(("gx", "gz", "ta"), None, None, None),
        P(("gx", "gz", "ta")),
    )
    out_specs = P(None, None, None, ("gx", "gz", "ta"))
    return jax.shard_map(body, mesh=mesh, in_specs=in_specs, out_specs=out_specs, check_vma=False)
```

```python
import jax
import jax.numpy as jnp
from jax import lax
from jax.sharding import PartitionSpec as P

ITERS = 5


omega_step = 0.5
exact = lax.Precision.HIGHEST


def routes():
    total = lax.axis_size("gx")
    plane_y = min(8, total // 2)
    plane_x = total // plane_y

    def ring(count):
        up = [(i + 1) % count for i in range(count)]
        down = [(i - 1) % count for i in range(count)]
        if count % 2:
            return up, down, False
        even = [(up if i % 2 == 0 else down)[i] for i in range(count)]
        odd = [(down if i % 2 == 0 else up)[i] for i in range(count)]
        return even, odd, True

    links = []
    first, second, paired = ring(plane_x)
    links.append(
        [("gx", tuple(way[g // plane_y] * plane_y + g % plane_y for g in range(total))) for way in (first, second)]
        + [paired, lax.axis_index("gx") // plane_y]
    )
    first, second, paired = ring(plane_y)
    links.append(
        [("gx", tuple((g // plane_y) * plane_y + way[g % plane_y] for g in range(total))) for way in (first, second)]
        + [paired, lax.axis_index("gx") % plane_y]
    )
    for axis in ("gz", "ta"):
        first, second, paired = ring(lax.axis_size(axis))
        links.append([(axis, tuple(first)), (axis, tuple(second)), paired, lax.axis_index(axis)])
    return links


def fetch(block, link):
    axis, sources = link
    return lax.ppermute(block, axis, [(source, i) for i, source in enumerate(sources)])


def body(residual, null_vectors, clover_inverse, coarse_op, vector_count):
    rhs_count = residual.shape[0]
    vec_total = null_vectors.shape[1]
    coarse_dim = 2 * vec_total
    sites = residual.shape[3]
    in_use = (lax.iota(jnp.int32, vec_total)[None, :] < vector_count[:, None]).astype(jnp.float32)[0]
    used = jnp.tile(in_use, 4)

    fine_rows = residual.transpose(2, 1, 0, 3).reshape(2, 6, 2 * rhs_count, sites)
    vectors = null_vectors.transpose(2, 0, 1, 3).reshape(2, 6, 2 * vec_total, sites)
    product = jnp.einsum("xcrs,xcks->xrk", fine_rows, vectors, preferred_element_type=jnp.float32)
    product = product.reshape(2, 2, rhs_count, 2, vec_total)
    real_part = product[:, 0, :, 0] + product[:, 1, :, 1]
    imag_part = product[:, 1, :, 0] - product[:, 0, :, 1]
    restricted = jnp.stack([real_part, imag_part]).transpose(2, 0, 1, 3)
    half = omega_step * (restricted.reshape(rhs_count, 2 * coarse_dim) * used)

    operator = coarse_op.reshape(9, 2, coarse_dim, coarse_dim)
    grouped = {}
    for way, (first, second, paired, place) in enumerate(routes()):
        plus, minus = operator[2 * way + 1], operator[2 * way + 2]
        if first == second:
            grouped[first] = plus + minus
        else:
            swap = (place % 2 == 1) & paired
            grouped[first] = jnp.where(swap, minus, plus)
            grouped[second] = jnp.where(swap, plus, minus)

    def reach(link):
        axis, sources = link
        return ("gz", "ta", "gx").index(axis), -max(abs(source - i) for i, source in enumerate(sources))

    order = sorted(grouped, key=reach)

    def real_form(matrix):
        upper = jnp.concatenate([matrix[0], -matrix[1]], 1)
        lower = jnp.concatenate([matrix[1], matrix[0]], 1)
        return omega_step * jnp.concatenate([upper, lower], 0)

    own = jnp.eye(2 * coarse_dim, dtype=jnp.float32) - real_form(operator[0])
    around = jnp.concatenate([-real_form(grouped[link]) for link in order], 1)

    def apply(vector, matrix):
        return lax.dot_general(vector, matrix, (((1,), (1,)), ((), ())), precision=exact)

    coarse = half
    for sweep_id in range(ITERS - 1):
        moved = [fetch(coarse, link) for link in order]
        kept = half + apply(coarse, own)
        coarse = kept + apply(jnp.concatenate(moved, 1), around)

    rounded = (coarse * used).reshape(rhs_count, 2, 2, vec_total)
    real_rows = jnp.stack([rounded[:, 0], -rounded[:, 1]], 1)
    imag_rows = jnp.stack([rounded[:, 1], rounded[:, 0]], 1)
    weights = jnp.stack([real_rows, imag_rows]).transpose(3, 0, 1, 2, 4)
    weights = weights.reshape(2, 2 * rhs_count, 2 * vec_total).astype(jnp.bfloat16)
    lift = jnp.einsum("xrk,xcks->xcrs", weights, vectors, preferred_element_type=jnp.float32)

    rows = residual.reshape(rhs_count, 2, 2, 6, sites).astype(jnp.float32)
    clover = clover_inverse.astype(jnp.float32)

    def local_apply(left, right):
        return sum(left[:, :, b][None] * right[:, :, b][:, :, None] for b in range(6))

    local_real = local_apply(clover[0], rows[:, 0]) - local_apply(clover[1], rows[:, 1])
    local_imag = local_apply(clover[0], rows[:, 1]) + local_apply(clover[1], rows[:, 0])
    lift = lift.reshape(2, 6, 2, rhs_count, sites).transpose(3, 2, 0, 1, 4)
    result = jnp.stack([local_real, local_imag], 1) + lift
    return result.reshape(rhs_count, 2, 12, sites).astype(jnp.bfloat16)


def solution(mesh):
    in_specs = (
        P(None, None, None, ("gx", "gz", "ta")),
        P(None, None, None, ("gx", "gz", "ta")),
        P(None, None, None, None, ("gx", "gz", "ta")),
        P(("gx", "gz", "ta"), None, None, None),
        P(("gx", "gz", "ta")),
    )
    out_specs = P(None, None, None, ("gx", "gz", "ta"))
    return jax.shard_map(body, mesh=mesh, in_specs=in_specs, out_specs=out_specs, check_vma=False)
```

```python
import jax
import jax.numpy as jnp
from jax import lax
from jax.sharding import PartitionSpec as P

ITERS = 5


omega_step = 0.5
exact = lax.Precision.HIGHEST


def routes():
    total = lax.axis_size("gx")
    plane_y = min(8, total // 2)
    plane_x = total // plane_y

    def ring(count):
        up = [(i + 1) % count for i in range(count)]
        down = [(i - 1) % count for i in range(count)]
        if count % 2:
            return up, down, False
        even = [(up if i % 2 == 0 else down)[i] for i in range(count)]
        odd = [(down if i % 2 == 0 else up)[i] for i in range(count)]
        return even, odd, True

    links = []
    first, second, paired = ring(plane_x)
    links.append(
        [("gx", tuple(way[g // plane_y] * plane_y + g % plane_y for g in range(total))) for way in (first, second)]
        + [paired, lax.axis_index("gx") // plane_y]
    )
    first, second, paired = ring(plane_y)
    links.append(
        [("gx", tuple((g // plane_y) * plane_y + way[g % plane_y] for g in range(total))) for way in (first, second)]
        + [paired, lax.axis_index("gx") % plane_y]
    )
    for axis in ("gz", "ta"):
        first, second, paired = ring(lax.axis_size(axis))
        links.append([(axis, tuple(first)), (axis, tuple(second)), paired, lax.axis_index(axis)])
    return links


def fetch(block, link):
    axis, sources = link
    return lax.ppermute(block, axis, [(source, i) for i, source in enumerate(sources)])


def fetch_all(block, order):
    axes = ("gx", "gz", "ta")
    everything = lax.all_gather(block, axes)
    moved = []
    for axis, sources in order:
        position = 0
        for name in axes:
            place = lax.axis_index(name)
            if name == axis:
                place = jnp.asarray(sources, jnp.int32)[place]
            position = position * lax.axis_size(name) + place
        moved.append(lax.dynamic_index_in_dim(everything, position, 0, keepdims=False))
    return moved


def body(residual, null_vectors, clover_inverse, coarse_op, vector_count):
    rhs_count = residual.shape[0]
    vec_total = null_vectors.shape[1]
    coarse_dim = 2 * vec_total
    sites = residual.shape[3]
    in_use = (lax.iota(jnp.int32, vec_total)[None, :] < vector_count[:, None]).astype(jnp.float32)[0]
    used = jnp.tile(in_use, 4)

    fine_rows = residual.transpose(2, 1, 0, 3).reshape(2, 6, 2 * rhs_count, sites)
    vectors = null_vectors.transpose(2, 0, 1, 3).reshape(2, 6, 2 * vec_total, sites)
    product = jnp.einsum("xcrs,xcks->xrk", fine_rows, vectors, preferred_element_type=jnp.float32)
    product = product.reshape(2, 2, rhs_count, 2, vec_total)
    real_part = product[:, 0, :, 0] + product[:, 1, :, 1]
    imag_part = product[:, 1, :, 0] - product[:, 0, :, 1]
    restricted = jnp.stack([real_part, imag_part]).transpose(2, 0, 1, 3)
    half = omega_step * (restricted.reshape(rhs_count, 2 * coarse_dim) * used)

    operator = coarse_op.reshape(9, 2, coarse_dim, coarse_dim)
    grouped = {}
    for way, (first, second, paired, place) in enumerate(routes()):
        plus, minus = operator[2 * way + 1], operator[2 * way + 2]
        if first == second:
            grouped[first] = plus + minus
        else:
            swap = (place % 2 == 1) & paired
            grouped[first] = jnp.where(swap, minus, plus)
            grouped[second] = jnp.where(swap, plus, minus)

    def reach(link):
        axis, sources = link
        return ("gz", "ta", "gx").index(axis), -max(abs(source - i) for i, source in enumerate(sources))

    order = sorted(grouped, key=reach)

    def real_form(matrix):
        upper = jnp.concatenate([matrix[0], -matrix[1]], 1)
        lower = jnp.concatenate([matrix[1], matrix[0]], 1)
        return omega_step * jnp.concatenate([upper, lower], 0)

    own = jnp.eye(2 * coarse_dim, dtype=jnp.float32) - real_form(operator[0])
    around = jnp.concatenate([-real_form(grouped[link]) for link in order], 1)

    def apply(vector, matrix):
        return lax.dot_general(vector, matrix, (((1,), (1,)), ((), ())), precision=exact)

    coarse = half
    for sweep_id in range(ITERS - 1):
        moved = fetch_all(coarse, order)
        kept = half + apply(coarse, own)
        coarse = kept + apply(jnp.concatenate(moved, 1), around)

    rounded = (coarse * used).reshape(rhs_count, 2, 2, vec_total)
    real_rows = jnp.stack([rounded[:, 0], -rounded[:, 1]], 1)
    imag_rows = jnp.stack([rounded[:, 1], rounded[:, 0]], 1)
    weights = jnp.stack([real_rows, imag_rows]).transpose(3, 0, 1, 2, 4)
    weights = weights.reshape(2, 2 * rhs_count, 2 * vec_total).astype(jnp.bfloat16)
    lift = jnp.einsum("xrk,xcks->xcrs", weights, vectors, preferred_element_type=jnp.float32)

    rows = residual.reshape(rhs_count, 2, 2, 6, sites).astype(jnp.float32)
    clover = clover_inverse.astype(jnp.float32)

    def local_apply(left, right):
        return sum(left[:, :, b][None] * right[:, :, b][:, :, None] for b in range(6))

    local_real = local_apply(clover[0], rows[:, 0]) - local_apply(clover[1], rows[:, 1])
    local_imag = local_apply(clover[0], rows[:, 1]) + local_apply(clover[1], rows[:, 0])
    lift = lift.reshape(2, 6, 2, rhs_count, sites).transpose(3, 2, 0, 1, 4)
    result = jnp.stack([local_real, local_imag], 1) + lift
    return result.reshape(rhs_count, 2, 12, sites).astype(jnp.bfloat16)


def solution(mesh):
    in_specs = (
        P(None, None, None, ("gx", "gz", "ta")),
        P(None, None, None, ("gx", "gz", "ta")),
        P(None, None, None, None, ("gx", "gz", "ta")),
        P(("gx", "gz", "ta"), None, None, None),
        P(("gx", "gz", "ta")),
    )
    out_specs = P(None, None, None, ("gx", "gz", "ta"))
    return jax.shard_map(body, mesh=mesh, in_specs=in_specs, out_specs=out_specs, check_vma=False)
```

```python
import jax
import jax.numpy as jnp
from jax import lax
from jax.sharding import PartitionSpec as P

ITERS = 5


omega_step = 0.5
exact = lax.Precision.HIGHEST


def routes():
    total = lax.axis_size("gx")
    plane_y = min(8, total // 2)
    plane_x = total // plane_y

    def ring(count):
        up = [(i + 1) % count for i in range(count)]
        down = [(i - 1) % count for i in range(count)]
        if count % 2:
            return up, down, False
        even = [(up if i % 2 == 0 else down)[i] for i in range(count)]
        odd = [(down if i % 2 == 0 else up)[i] for i in range(count)]
        return even, odd, True

    links = []
    first, second, paired = ring(plane_x)
    links.append(
        [("gx", tuple(way[g // plane_y] * plane_y + g % plane_y for g in range(total))) for way in (first, second)]
        + [paired, lax.axis_index("gx") // plane_y]
    )
    first, second, paired = ring(plane_y)
    links.append(
        [("gx", tuple((g // plane_y) * plane_y + way[g % plane_y] for g in range(total))) for way in (first, second)]
        + [paired, lax.axis_index("gx") % plane_y]
    )
    for axis in ("gz", "ta"):
        first, second, paired = ring(lax.axis_size(axis))
        links.append([(axis, tuple(first)), (axis, tuple(second)), paired, lax.axis_index(axis)])
    return links


def fetch(block, link):
    axis, sources = link
    return lax.ppermute(block, axis, [(source, i) for i, source in enumerate(sources)])


def fetch_all(block, order):
    axes = ("gx", "gz", "ta")
    count = 1
    for name in axes:
        count *= lax.axis_size(name)
    everything = lax.all_to_all(jnp.broadcast_to(block, (count,) + block.shape), axes, 0, 0)
    moved = []
    for axis, sources in order:
        position = 0
        for name in axes:
            place = lax.axis_index(name)
            if name == axis:
                place = jnp.asarray(sources, jnp.int32)[place]
            position = position * lax.axis_size(name) + place
        moved.append(lax.dynamic_index_in_dim(everything, position, 0, keepdims=False))
    return moved


def body(residual, null_vectors, clover_inverse, coarse_op, vector_count):
    rhs_count = residual.shape[0]
    vec_total = null_vectors.shape[1]
    coarse_dim = 2 * vec_total
    sites = residual.shape[3]
    in_use = (lax.iota(jnp.int32, vec_total)[None, :] < vector_count[:, None]).astype(jnp.float32)[0]
    used = jnp.tile(in_use, 4)

    fine_rows = residual.transpose(2, 1, 0, 3).reshape(2, 6, 2 * rhs_count, sites)
    vectors = null_vectors.transpose(2, 0, 1, 3).reshape(2, 6, 2 * vec_total, sites)
    product = jnp.einsum("xcrs,xcks->xrk", fine_rows, vectors, preferred_element_type=jnp.float32)
    product = product.reshape(2, 2, rhs_count, 2, vec_total)
    real_part = product[:, 0, :, 0] + product[:, 1, :, 1]
    imag_part = product[:, 1, :, 0] - product[:, 0, :, 1]
    restricted = jnp.stack([real_part, imag_part]).transpose(2, 0, 1, 3)
    half = omega_step * (restricted.reshape(rhs_count, 2 * coarse_dim) * used)

    operator = coarse_op.reshape(9, 2, coarse_dim, coarse_dim)
    grouped = {}
    for way, (first, second, paired, place) in enumerate(routes()):
        plus, minus = operator[2 * way + 1], operator[2 * way + 2]
        if first == second:
            grouped[first] = plus + minus
        else:
            swap = (place % 2 == 1) & paired
            grouped[first] = jnp.where(swap, minus, plus)
            grouped[second] = jnp.where(swap, plus, minus)

    def reach(link):
        axis, sources = link
        return ("gz", "ta", "gx").index(axis), -max(abs(source - i) for i, source in enumerate(sources))

    order = sorted(grouped, key=reach)

    def real_form(matrix):
        upper = jnp.concatenate([matrix[0], -matrix[1]], 1)
        lower = jnp.concatenate([matrix[1], matrix[0]], 1)
        return omega_step * jnp.concatenate([upper, lower], 0)

    own = jnp.eye(2 * coarse_dim, dtype=jnp.float32) - real_form(operator[0])
    around = jnp.concatenate([-real_form(grouped[link]) for link in order], 1)

    def apply(vector, matrix):
        return lax.dot_general(vector, matrix, (((1,), (1,)), ((), ())), precision=exact)

    coarse = half
    for sweep_id in range(ITERS - 1):
        moved = fetch_all(coarse, order)
        kept = half + apply(coarse, own)
        coarse = kept + apply(jnp.concatenate(moved, 1), around)

    rounded = (coarse * used).reshape(rhs_count, 2, 2, vec_total)
    real_rows = jnp.stack([rounded[:, 0], -rounded[:, 1]], 1)
    imag_rows = jnp.stack([rounded[:, 1], rounded[:, 0]], 1)
    weights = jnp.stack([real_rows, imag_rows]).transpose(3, 0, 1, 2, 4)
    weights = weights.reshape(2, 2 * rhs_count, 2 * vec_total).astype(jnp.bfloat16)
    lift = jnp.einsum("xrk,xcks->xcrs", weights, vectors, preferred_element_type=jnp.float32)

    rows = residual.reshape(rhs_count, 2, 2, 6, sites).astype(jnp.float32)
    clover = clover_inverse.astype(jnp.float32)

    def local_apply(left, right):
        return sum(left[:, :, b][None] * right[:, :, b][:, :, None] for b in range(6))

    local_real = local_apply(clover[0], rows[:, 0]) - local_apply(clover[1], rows[:, 1])
    local_imag = local_apply(clover[0], rows[:, 1]) + local_apply(clover[1], rows[:, 0])
    lift = lift.reshape(2, 6, 2, rhs_count, sites).transpose(3, 2, 0, 1, 4)
    result = jnp.stack([local_real, local_imag], 1) + lift
    return result.reshape(rhs_count, 2, 12, sites).astype(jnp.bfloat16)


def solution(mesh):
    in_specs = (
        P(None, None, None, ("gx", "gz", "ta")),
        P(None, None, None, ("gx", "gz", "ta")),
        P(None, None, None, None, ("gx", "gz", "ta")),
        P(("gx", "gz", "ta"), None, None, None),
        P(("gx", "gz", "ta")),
    )
    out_specs = P(None, None, None, ("gx", "gz", "ta"))
    return jax.shard_map(body, mesh=mesh, in_specs=in_specs, out_specs=out_specs, check_vma=False)
```

```python
import jax
import jax.numpy as jnp
from jax import lax
from jax.experimental import pallas as pl
from jax.experimental.pallas import tpu as pltpu
from jax.sharding import PartitionSpec as P

ITERS = 5


omega_step = 0.5
exact = lax.Precision.HIGHEST


def routes():
    total = lax.axis_size("gx")
    plane_y = min(8, total // 2)
    plane_x = total // plane_y

    def ring(count):
        up = [(i + 1) % count for i in range(count)]
        down = [(i - 1) % count for i in range(count)]
        if count % 2:
            return up, down, False
        even = [(up if i % 2 == 0 else down)[i] for i in range(count)]
        odd = [(down if i % 2 == 0 else up)[i] for i in range(count)]
        return even, odd, True

    links = []
    first, second, paired = ring(plane_x)
    links.append(
        [("gx", tuple(way[g // plane_y] * plane_y + g % plane_y for g in range(total))) for way in (first, second)]
        + [paired, lax.axis_index("gx") // plane_y]
    )
    first, second, paired = ring(plane_y)
    links.append(
        [("gx", tuple((g // plane_y) * plane_y + way[g % plane_y] for g in range(total))) for way in (first, second)]
        + [paired, lax.axis_index("gx") % plane_y]
    )
    for axis in ("gz", "ta"):
        first, second, paired = ring(lax.axis_size(axis))
        links.append([(axis, tuple(first)), (axis, tuple(second)), paired, lax.axis_index(axis)])
    return links


def fetch(block, link):
    axis, sources = link
    return lax.ppermute(block, axis, [(source, i) for i, source in enumerate(sources)])


def restrict_kernel(count_hbm, rows_hbm, vectors_hbm, out_ref, count_ref, rows_ref, vectors_ref, scratch, sems):
    rhs, parts, _, sites = rows_ref.shape
    vecs = vectors_ref.shape[2]
    half = parts // 2
    copies = []
    for chi in range(2):
        span = pl.ds(half * chi, half)
        copies.append(
            [
                pltpu.make_async_copy(rows_hbm.at[:, span], rows_ref.at[:, span], sems.at[2 * chi]),
                pltpu.make_async_copy(vectors_hbm.at[:, span], vectors_ref.at[:, span], sems.at[2 * chi + 1]),
            ]
        )
    count_copy = pltpu.make_async_copy(count_hbm, count_ref, sems.at[4])
    for copy in copies[0] + [count_copy] + copies[1]:
        copy.start()
    for chi in range(2):
        for copy in copies[chi]:
            copy.wait()
        total = jnp.zeros((2 * rhs, 2 * vecs), jnp.float32)
        for c in range(half * chi, half * chi + half):
            rows = rows_ref[:, c].reshape(2 * rhs, sites)
            vectors = jnp.concatenate([vectors_ref[0, c], vectors_ref[1, c]], 0)
            total += lax.dot_general(
                rows, vectors, (((1,), (1,)), ((), ())), preferred_element_type=jnp.float32
            )
        scratch[chi, :, : 2 * vecs] = total
    count_copy.wait()
    real, imag = [], []
    for chi in range(2):
        even = scratch[chi, pl.ds(0, rhs, stride=2), :]
        odd = scratch[chi, pl.ds(1, rhs, stride=2), :]
        real.append(even[:, :vecs] + odd[:, vecs : 2 * vecs])
        imag.append(odd[:, :vecs] - even[:, vecs : 2 * vecs])
    lane = lax.broadcasted_iota(jnp.int32, (rhs, vecs), 1)
    keep = jnp.where(lane < count_ref[0], omega_step, 0.0)
    out_ref[...] = jnp.concatenate([part * keep for part in real + imag], 1)


def local_kernel(rows_ref, clover_ref, out_ref):
    rhs, parts, _, sites = rows_ref.shape
    half = parts // 2
    row = lax.broadcasted_iota(jnp.int32, (2 * rhs, 2 * rhs), 0)
    col = lax.broadcasted_iota(jnp.int32, (2 * rhs, 2 * rhs), 1)
    turn = jnp.where((row % 2 == 0) & (col == row + 1), -1.0, 0.0)
    turn = jnp.where((row % 2 == 1) & (col == row - 1), 1.0, turn).astype(jnp.bfloat16)
    for chi in range(2):
        for start in range(0, sites, 128):
            lanes = slice(start, start + 128)
            plain, turned = [], []
            for b in range(half):
                rows = rows_ref[:, half * chi + b, :, lanes].reshape(2 * rhs, 128)
                plain.append(rows.astype(jnp.float32))
                turned.append(jnp.dot(turn, rows, preferred_element_type=jnp.float32))
            for a in range(half):
                total = jnp.zeros((2 * rhs, 128), jnp.float32)
                for b in range(half):
                    real = clover_ref[0, a, b, :, lanes].astype(jnp.float32)[chi : chi + 1]
                    imag = clover_ref[1, a, b, :, lanes].astype(jnp.float32)[chi : chi + 1]
                    total += real * plain[b] + imag * turned[b]
                out_ref[half * chi + a, :, lanes] = total


def extend_kernel(count_ref, coarse_ref, vectors_ref, local_ref, out_ref, scratch):
    rhs, parts, _, sites = out_ref.shape
    vecs = vectors_ref.shape[2]
    half = parts // 2
    lane = lax.broadcasted_iota(jnp.int32, (rhs, vecs), 1)
    keep = lane < count_ref[...]
    pieces = [jnp.where(keep, coarse_ref[:, p * vecs : p * vecs + vecs], 0.0) for p in range(4)]
    for chi in range(2):
        real, imag = pieces[chi], pieces[2 + chi]
        scratch[chi, pl.ds(0, rhs, stride=2), : 2 * vecs] = jnp.concatenate([real, -imag], 1)
        scratch[chi, pl.ds(1, rhs, stride=2), : 2 * vecs] = jnp.concatenate([imag, real], 1)
        weights = scratch[chi, :, : 2 * vecs].astype(jnp.bfloat16)
        for c in range(half * chi, half * chi + half):
            vectors = jnp.concatenate([vectors_ref[0, c], vectors_ref[1, c]], 0)
            lift = jnp.dot(weights, vectors, preferred_element_type=jnp.float32)
            total = (local_ref[c] + lift).astype(jnp.bfloat16)
            out_ref[:, c] = total.reshape(rhs, 2, sites)


in_hbm = pl.BlockSpec(memory_space=pltpu.HBM)
in_vmem = pl.BlockSpec(memory_space=pltpu.VMEM)


def body(residual, null_vectors, clover_inverse, coarse_op, vector_count):
    rhs_count = residual.shape[0]
    vec_total = null_vectors.shape[1]
    coarse_dim = 2 * vec_total
    parts = residual.shape[2]
    sites = residual.shape[3]
    count = vector_count.reshape(1, 1)
    rows = residual.transpose(0, 2, 1, 3)
    vectors = null_vectors.transpose(0, 2, 1, 3)
    clover = clover_inverse.transpose(0, 2, 3, 1, 4)

    half = pl.pallas_call(
        restrict_kernel,
        out_shape=jax.ShapeDtypeStruct((rhs_count, 2 * coarse_dim), jnp.float32),
        in_specs=[in_hbm] * 3,
        out_specs=in_vmem,
        scratch_shapes=[
            pltpu.SMEM((1,), jnp.int32),
            pltpu.VMEM(rows.shape, rows.dtype),
            pltpu.VMEM(vectors.shape, vectors.dtype),
            pltpu.VMEM((2, 2 * rhs_count, 128), jnp.float32),
            pltpu.SemaphoreType.DMA((5,)),
        ],
        cost_estimate=pl.CostEstimate(flops=10**7, bytes_accessed=5 * 10**5, transcendentals=0),
    )(vector_count, rows, vectors)

    operator = coarse_op.reshape(9, 2, coarse_dim, coarse_dim)
    grouped = {}
    for way, (first, second, paired, place) in enumerate(routes()):
        plus, minus = operator[2 * way + 1], operator[2 * way + 2]
        if first == second:
            grouped[first] = plus + minus
        else:
            swap = (place % 2 == 1) & paired
            grouped[first] = jnp.where(swap, minus, plus)
            grouped[second] = jnp.where(swap, plus, minus)

    def reach(link):
        axis, sources = link
        return ("gz", "ta", "gx").index(axis), -max(abs(source - i) for i, source in enumerate(sources))

    order = sorted(grouped, key=reach)

    def real_form(matrix):
        upper = jnp.concatenate([matrix[0], -matrix[1]], 1)
        lower = jnp.concatenate([matrix[1], matrix[0]], 1)
        return omega_step * jnp.concatenate([upper, lower], 0)

    own = jnp.eye(2 * coarse_dim, dtype=jnp.float32) - real_form(operator[0])
    around = jnp.concatenate([-real_form(grouped[link]) for link in order], 1)

    def apply(vector, matrix):
        return lax.dot_general(vector, matrix, (((1,), (1,)), ((), ())), precision=exact)

    coarse = half
    for sweep_id in range(ITERS - 1):
        moved = [fetch(coarse, link) for link in order]
        kept = half + apply(coarse, own)
        if sweep_id == 1:
            held_rows, held_clover, _ = lax.optimization_barrier((rows, clover, coarse))
            local = pl.pallas_call(
                local_kernel,
                out_shape=jax.ShapeDtypeStruct((parts, 2 * rhs_count, sites), jnp.float32),
                in_specs=[in_vmem] * 2,
                out_specs=in_vmem,
                cost_estimate=pl.CostEstimate(flops=10**7, bytes_accessed=10**6, transcendentals=0),
            )(held_rows, held_clover)
        coarse = kept + apply(jnp.concatenate(moved, 1), around)

    result = pl.pallas_call(
        extend_kernel,
        out_shape=jax.ShapeDtypeStruct((rhs_count, parts, 2, sites), jnp.bfloat16),
        in_specs=[in_vmem] * 4,
        out_specs=in_vmem,
        scratch_shapes=[pltpu.VMEM((2, 2 * rhs_count, 128), jnp.float32)],
        cost_estimate=pl.CostEstimate(flops=10**7, bytes_accessed=10**6, transcendentals=0),
    )(count, coarse, vectors, local)
    return result.transpose(0, 2, 1, 3)


def solution(mesh):
    in_specs = (
        P(None, None, None, ("gx", "gz", "ta")),
        P(None, None, None, ("gx", "gz", "ta")),
        P(None, None, None, None, ("gx", "gz", "ta")),
        P(("gx", "gz", "ta"), None, None, None),
        P(("gx", "gz", "ta")),
    )
    out_specs = P(None, None, None, ("gx", "gz", "ta"))
    return jax.shard_map(body, mesh=mesh, in_specs=in_specs, out_specs=out_specs, check_vma=False)
```

```python
import jax
import jax.numpy as jnp
from jax import lax
from jax.sharding import PartitionSpec as P

ITERS = 5


omega_step = 0.5
exact = lax.Precision.HIGHEST


def routes():
    total = lax.axis_size("gx")
    plane_y = min(8, total // 2)
    plane_x = total // plane_y

    def ring(count):
        up = [(i + 1) % count for i in range(count)]
        down = [(i - 1) % count for i in range(count)]
        if count % 2:
            return up, down, False
        even = [(up if i % 2 == 0 else down)[i] for i in range(count)]
        odd = [(down if i % 2 == 0 else up)[i] for i in range(count)]
        return even, odd, True

    links = []
    first, second, paired = ring(plane_x)
    links.append(
        [("gx", tuple(way[g // plane_y] * plane_y + g % plane_y for g in range(total))) for way in (first, second)]
        + [paired, lax.axis_index("gx") // plane_y]
    )
    first, second, paired = ring(plane_y)
    links.append(
        [("gx", tuple((g // plane_y) * plane_y + way[g % plane_y] for g in range(total))) for way in (first, second)]
        + [paired, lax.axis_index("gx") % plane_y]
    )
    for axis in ("gz", "ta"):
        first, second, paired = ring(lax.axis_size(axis))
        links.append([(axis, tuple(first)), (axis, tuple(second)), paired, lax.axis_index(axis)])
    return links


def fetch(block, link):
    axis, sources = link
    return lax.ppermute(block, axis, [(source, i) for i, source in enumerate(sources)])


def local_term(residual, clover_inverse):
    rhs_count, _, _, sites = residual.shape
    rows = residual.reshape(rhs_count, 2, 2, 6, sites).astype(jnp.float32)
    clover = clover_inverse.astype(jnp.float32)

    def local_apply(left, right):
        return sum(left[:, :, b][None] * right[:, :, b][:, :, None] for b in range(6))

    local_real = local_apply(clover[0], rows[:, 0]) - local_apply(clover[1], rows[:, 1])
    local_imag = local_apply(clover[0], rows[:, 1]) + local_apply(clover[1], rows[:, 0])
    return local_real, local_imag


def body(residual, null_vectors, clover_inverse, coarse_op, vector_count):
    rhs_count = residual.shape[0]
    vec_total = null_vectors.shape[1]
    coarse_dim = 2 * vec_total
    sites = residual.shape[3]
    in_use = (lax.iota(jnp.int32, vec_total)[None, :] < vector_count[:, None]).astype(jnp.float32)[0]
    used = jnp.tile(in_use, 4)

    parts = residual.transpose(1, 2, 0, 3).reshape(2, 2, 6, rhs_count, sites)
    fine_rows = jnp.stack(
        [jnp.concatenate([parts[0], parts[1]], 2), jnp.concatenate([parts[1], -parts[0]], 2)]
    )
    vectors = null_vectors.transpose(0, 2, 1, 3).reshape(2, 2, 6, vec_total, sites)
    product = jnp.einsum("pxcrs,pxcks->xrk", fine_rows, vectors, preferred_element_type=jnp.float32)
    pieces = [product[chi, part * rhs_count : (part + 1) * rhs_count] for part in range(2) for chi in range(2)]
    half = omega_step * (jnp.concatenate(pieces, 1) * used)

    operator = coarse_op.reshape(9, 2, coarse_dim, coarse_dim)
    grouped = {}
    for way, (first, second, paired, place) in enumerate(routes()):
        plus, minus = operator[2 * way + 1], operator[2 * way + 2]
        if first == second:
            grouped[first] = plus + minus
        else:
            swap = (place % 2 == 1) & paired
            grouped[first] = jnp.where(swap, minus, plus)
            grouped[second] = jnp.where(swap, plus, minus)

    def reach(link):
        axis, sources = link
        return ("gz", "ta", "gx").index(axis), -max(abs(source - i) for i, source in enumerate(sources))

    order = sorted(grouped, key=reach)

    def real_form(matrix):
        upper = jnp.concatenate([matrix[0], -matrix[1]], 1)
        lower = jnp.concatenate([matrix[1], matrix[0]], 1)
        return omega_step * jnp.concatenate([upper, lower], 0)

    own = jnp.eye(2 * coarse_dim, dtype=jnp.float32) - real_form(operator[0])
    around = jnp.concatenate([-real_form(grouped[link]) for link in order], 1)

    def apply(vector, matrix):
        return lax.dot_general(vector, matrix, (((1,), (1,)), ((), ())), precision=exact)

    coarse = half
    for sweep_id in range(ITERS - 1):
        moved = [fetch(coarse, link) for link in order]
        kept = half + apply(coarse, own)
        if sweep_id == 1:
            rows, clover, _ = lax.optimization_barrier((residual, clover_inverse, coarse))
            local_real, local_imag = local_term(rows, clover)
        coarse = kept + apply(jnp.concatenate(moved, 1), around)

    rounded = coarse * used
    cut = [rounded[:, p * vec_total : (p + 1) * vec_total] for p in range(4)]
    by_real = jnp.stack([jnp.concatenate([cut[chi], cut[2 + chi]], 0) for chi in range(2)])
    by_imag = jnp.stack([jnp.concatenate([-cut[2 + chi], cut[chi]], 0) for chi in range(2)])
    weights = jnp.stack([by_real, by_imag]).astype(jnp.bfloat16)
    lift = jnp.einsum("pxrk,pxcks->xcrs", weights, vectors, preferred_element_type=jnp.float32)
    lift = lift.reshape(2, 6, 2, rhs_count, sites).transpose(3, 2, 0, 1, 4)
    result = jnp.stack([local_real, local_imag], 1) + lift
    return result.reshape(rhs_count, 2, 12, sites).astype(jnp.bfloat16)


def solution(mesh):
    in_specs = (
        P(None, None, None, ("gx", "gz", "ta")),
        P(None, None, None, ("gx", "gz", "ta")),
        P(None, None, None, None, ("gx", "gz", "ta")),
        P(("gx", "gz", "ta"), None, None, None),
        P(("gx", "gz", "ta")),
    )
    out_specs = P(None, None, None, ("gx", "gz", "ta"))
    return jax.shard_map(body, mesh=mesh, in_specs=in_specs, out_specs=out_specs, check_vma=False)
```

```python
import jax
import jax.numpy as jnp
from jax import lax
from jax.sharding import PartitionSpec as P

ITERS = 5


omega_step = 0.5
exact = lax.Precision.HIGHEST


def routes():
    total = lax.axis_size("gx")
    plane_y = min(8, total // 2)
    plane_x = total // plane_y

    def ring(count):
        up = [(i + 1) % count for i in range(count)]
        down = [(i - 1) % count for i in range(count)]
        if count % 2:
            return up, down, False
        even = [(up if i % 2 == 0 else down)[i] for i in range(count)]
        odd = [(down if i % 2 == 0 else up)[i] for i in range(count)]
        return even, odd, True

    links = []
    first, second, paired = ring(plane_x)
    links.append(
        [("gx", tuple(way[g // plane_y] * plane_y + g % plane_y for g in range(total))) for way in (first, second)]
        + [paired, lax.axis_index("gx") // plane_y]
    )
    first, second, paired = ring(plane_y)
    links.append(
        [("gx", tuple((g // plane_y) * plane_y + way[g % plane_y] for g in range(total))) for way in (first, second)]
        + [paired, lax.axis_index("gx") % plane_y]
    )
    for axis in ("gz", "ta"):
        first, second, paired = ring(lax.axis_size(axis))
        links.append([(axis, tuple(first)), (axis, tuple(second)), paired, lax.axis_index(axis)])
    return links


def fetch(block, link):
    axis, sources = link
    return lax.ppermute(block, axis, [(source, i) for i, source in enumerate(sources)])


def local_term(residual, clover_inverse):
    rhs_count, _, _, sites = residual.shape
    rows = residual.reshape(rhs_count, 2, 2, 6, sites).astype(jnp.float32)
    clover = clover_inverse.astype(jnp.float32)

    def local_apply(left, right):
        return sum(left[:, :, b][None] * right[:, :, b][:, :, None] for b in range(6))

    local_real = local_apply(clover[0], rows[:, 0]) - local_apply(clover[1], rows[:, 1])
    local_imag = local_apply(clover[0], rows[:, 1]) + local_apply(clover[1], rows[:, 0])
    return local_real, local_imag


def body(residual, null_vectors, clover_inverse, coarse_op, vector_count):
    rhs_count = residual.shape[0]
    vec_total = null_vectors.shape[1]
    coarse_dim = 2 * vec_total
    sites = residual.shape[3]
    in_use = (lax.iota(jnp.int32, vec_total)[None, :] < vector_count[:, None]).astype(jnp.float32)[0]
    used = jnp.tile(in_use, 4)
    used, fine = lax.optimization_barrier((used, residual))

    parts = fine.transpose(1, 2, 0, 3).reshape(2, 2, 6, rhs_count, sites)
    fine_rows = jnp.stack(
        [jnp.concatenate([parts[0], parts[1]], 2), jnp.concatenate([parts[1], -parts[0]], 2)]
    )
    vectors = null_vectors.transpose(0, 2, 1, 3).reshape(2, 2, 6, vec_total, sites)
    product = jnp.einsum("pxcrs,pxcks->xrk", fine_rows, vectors, preferred_element_type=jnp.float32)
    pieces = [product[chi, part * rhs_count : (part + 1) * rhs_count] for part in range(2) for chi in range(2)]
    half = omega_step * (jnp.concatenate(pieces, 1) * used)

    operator = coarse_op.reshape(9, 2, coarse_dim, coarse_dim)
    grouped = {}
    for way, (first, second, paired, place) in enumerate(routes()):
        plus, minus = operator[2 * way + 1], operator[2 * way + 2]
        if first == second:
            grouped[first] = plus + minus
        else:
            swap = (place % 2 == 1) & paired
            grouped[first] = jnp.where(swap, minus, plus)
            grouped[second] = jnp.where(swap, plus, minus)

    def reach(link):
        axis, sources = link
        return ("gz", "ta", "gx").index(axis), -max(abs(source - i) for i, source in enumerate(sources))

    order = sorted(grouped, key=reach)

    def real_form(matrix):
        upper = jnp.concatenate([matrix[0], -matrix[1]], 1)
        lower = jnp.concatenate([matrix[1], matrix[0]], 1)
        return omega_step * jnp.concatenate([upper, lower], 0)

    own = jnp.eye(2 * coarse_dim, dtype=jnp.float32) - real_form(operator[0])
    around = jnp.concatenate([-real_form(grouped[link]) for link in order], 1)

    def apply(vector, matrix):
        return lax.dot_general(vector, matrix, (((1,), (1,)), ((), ())), precision=exact)

    coarse = half
    for sweep_id in range(ITERS - 1):
        moved = [fetch(coarse, link) for link in order]
        kept = half + apply(coarse, own)
        if sweep_id == 1:
            rows, clover, kept = lax.optimization_barrier((residual, clover_inverse, kept))
            local_real, local_imag = local_term(rows, clover)
        coarse = kept + apply(jnp.concatenate(moved, 1), around)

    rounded = coarse * used
    cut = [rounded[:, p * vec_total : (p + 1) * vec_total] for p in range(4)]
    by_real = jnp.stack([jnp.concatenate([cut[chi], cut[2 + chi]], 0) for chi in range(2)])
    by_imag = jnp.stack([jnp.concatenate([-cut[2 + chi], cut[chi]], 0) for chi in range(2)])
    weights = jnp.stack([by_real, by_imag]).astype(jnp.bfloat16)
    lift = jnp.einsum("pxrk,pxcks->xcrs", weights, vectors, preferred_element_type=jnp.float32)
    lift = lift.reshape(2, 6, 2, rhs_count, sites).transpose(3, 2, 0, 1, 4)
    result = jnp.stack([local_real, local_imag], 1) + lift
    return result.reshape(rhs_count, 2, 12, sites).astype(jnp.bfloat16)


def solution(mesh):
    in_specs = (
        P(None, None, None, ("gx", "gz", "ta")),
        P(None, None, None, ("gx", "gz", "ta")),
        P(None, None, None, None, ("gx", "gz", "ta")),
        P(("gx", "gz", "ta"), None, None, None),
        P(("gx", "gz", "ta")),
    )
    out_specs = P(None, None, None, ("gx", "gz", "ta"))
    return jax.shard_map(body, mesh=mesh, in_specs=in_specs, out_specs=out_specs, check_vma=False)
```

```python
import jax
import jax.numpy as jnp
from jax import lax
from jax.sharding import PartitionSpec as P

ITERS = 5


omega_step = 0.5
exact = lax.Precision.HIGHEST


def routes():
    total = lax.axis_size("gx")
    plane_y = min(8, total // 2)
    plane_x = total // plane_y

    def ring(count):
        up = [(i + 1) % count for i in range(count)]
        down = [(i - 1) % count for i in range(count)]
        if count % 2:
            return up, down, False
        even = [(up if i % 2 == 0 else down)[i] for i in range(count)]
        odd = [(down if i % 2 == 0 else up)[i] for i in range(count)]
        return even, odd, True

    links = []
    first, second, paired = ring(plane_x)
    links.append(
        [("gx", tuple(way[g // plane_y] * plane_y + g % plane_y for g in range(total))) for way in (first, second)]
        + [paired, lax.axis_index("gx") // plane_y]
    )
    first, second, paired = ring(plane_y)
    links.append(
        [("gx", tuple((g // plane_y) * plane_y + way[g % plane_y] for g in range(total))) for way in (first, second)]
        + [paired, lax.axis_index("gx") % plane_y]
    )
    first, second, paired = ring(lax.axis_size("ta"))
    links.append([("ta", tuple(first)), ("ta", tuple(second)), paired, lax.axis_index("ta")])
    return links


def fetch(block, link):
    axis, sources = link
    return lax.ppermute(block, axis, [(source, i) for i, source in enumerate(sources)])


def local_term(residual, clover_inverse):
    rhs_count, _, _, sites = residual.shape
    rows = residual.reshape(rhs_count, 2, 2, 6, sites).astype(jnp.float32)
    clover = clover_inverse.astype(jnp.float32)

    def local_apply(left, right):
        return sum(left[:, :, b][None] * right[:, :, b][:, :, None] for b in range(6))

    local_real = local_apply(clover[0], rows[:, 0]) - local_apply(clover[1], rows[:, 1])
    local_imag = local_apply(clover[0], rows[:, 1]) + local_apply(clover[1], rows[:, 0])
    return local_real, local_imag


def body(residual, null_vectors, clover_inverse, coarse_op, vector_count):
    rhs_count = residual.shape[0]
    vec_total = null_vectors.shape[1]
    coarse_dim = 2 * vec_total
    sites = residual.shape[3]
    in_use = (lax.iota(jnp.int32, vec_total)[None, :] < vector_count[:, None]).astype(jnp.float32)[0]
    used = jnp.tile(in_use, 4)
    used, fine = lax.optimization_barrier((used, residual))

    parts = fine.transpose(1, 2, 0, 3).reshape(2, 2, 6, rhs_count, sites)
    fine_rows = jnp.stack(
        [jnp.concatenate([parts[0], parts[1]], 2), jnp.concatenate([parts[1], -parts[0]], 2)]
    )
    vectors = null_vectors.transpose(0, 2, 1, 3).reshape(2, 2, 6, vec_total, sites)
    product = jnp.einsum("pxcrs,pxcks->xrk", fine_rows, vectors, preferred_element_type=jnp.float32)
    pieces = [product[chi, part * rhs_count : (part + 1) * rhs_count] for part in range(2) for chi in range(2)]
    half = omega_step * (jnp.concatenate(pieces, 1) * used)

    operator = coarse_op.reshape(9, 2, coarse_dim, coarse_dim)
    grouped = {}
    for way, (first, second, paired, place) in zip((0, 1, 3), routes()):
        plus, minus = operator[2 * way + 1], operator[2 * way + 2]
        if first == second:
            grouped[first] = plus + minus
        else:
            swap = (place % 2 == 1) & paired
            grouped[first] = jnp.where(swap, minus, plus)
            grouped[second] = jnp.where(swap, plus, minus)
    order = sorted(grouped, key=lambda link: ("ta", "gx").index(link[0]))

    depth = lax.axis_size("gz")
    place = lax.axis_index("gz")
    column = []
    for source in range(depth):
        above = jnp.where(source == (place + 1) % depth, 1.0, 0.0)
        below = jnp.where(source == (place + depth - 1) % depth, 1.0, 0.0)
        column.append(above * operator[5] + below * operator[6])

    def real_form(matrix):
        upper = jnp.concatenate([matrix[0], -matrix[1]], 1)
        lower = jnp.concatenate([matrix[1], matrix[0]], 1)
        return omega_step * jnp.concatenate([upper, lower], 0)

    own = jnp.eye(2 * coarse_dim, dtype=jnp.float32) - real_form(operator[0])
    around = jnp.concatenate([-real_form(part) for part in column + [grouped[link] for link in order]], 1)

    def apply(vector, matrix):
        return lax.dot_general(vector, matrix, (((1,), (1,)), ((), ())), precision=exact)

    coarse = half
    for sweep_id in range(ITERS - 1):
        line = lax.all_to_all(jnp.broadcast_to(coarse, (depth,) + coarse.shape), "gz", 0, 0)
        moved = [line[source] for source in range(depth)] + [fetch(coarse, link) for link in order]
        kept = half + apply(coarse, own)
        if sweep_id == 1:
            rows, clover, kept = lax.optimization_barrier((residual, clover_inverse, kept))
            local_real, local_imag = local_term(rows, clover)
        coarse = kept + apply(jnp.concatenate(moved, 1), around)

    rounded = coarse * used
    cut = [rounded[:, p * vec_total : (p + 1) * vec_total] for p in range(4)]
    by_real = jnp.stack([jnp.concatenate([cut[chi], cut[2 + chi]], 0) for chi in range(2)])
    by_imag = jnp.stack([jnp.concatenate([-cut[2 + chi], cut[chi]], 0) for chi in range(2)])
    weights = jnp.stack([by_real, by_imag]).astype(jnp.bfloat16)
    lift = jnp.einsum("pxrk,pxcks->xcrs", weights, vectors, preferred_element_type=jnp.float32)
    lift = lift.reshape(2, 6, 2, rhs_count, sites).transpose(3, 2, 0, 1, 4)
    result = jnp.stack([local_real, local_imag], 1) + lift
    return result.reshape(rhs_count, 2, 12, sites).astype(jnp.bfloat16)


def solution(mesh):
    in_specs = (
        P(None, None, None, ("gx", "gz", "ta")),
        P(None, None, None, ("gx", "gz", "ta")),
        P(None, None, None, None, ("gx", "gz", "ta")),
        P(("gx", "gz", "ta"), None, None, None),
        P(("gx", "gz", "ta")),
    )
    out_specs = P(None, None, None, ("gx", "gz", "ta"))
    return jax.shard_map(body, mesh=mesh, in_specs=in_specs, out_specs=out_specs, check_vma=False)
```

```python
import jax
import jax.numpy as jnp
from jax import lax
from jax.sharding import PartitionSpec as P

ITERS = 5


omega_step = 0.5
exact = lax.Precision.HIGHEST


axes = ("gx", "gz", "ta")


def plan():
    total, depth, slabs = (lax.axis_size(axis) for axis in axes)
    plane_y = min(8, total // 2)
    extents = (total // plane_y, plane_y, depth, slabs)
    count = total * depth * slabs

    def coordinates(device):
        group, rest = divmod(device, depth * slabs)
        return [group // plane_y, group % plane_y, rest // slabs, rest % slabs]

    def device_at(x, y, z, t):
        return ((x * plane_y + y) * depth + z) * slabs + t

    places = [coordinates(device) for device in range(count)]
    parity = [sum(place) % 2 for place in places]
    links = []
    for dim, extent in enumerate(extents):
        for first in (0, 1):
            sources, plus = [], []
            for place in places:
                step = 1 if extent % 2 or place[dim] % 2 == 0 else -1
                step = -step if first == 0 else step
                moved = list(place)
                moved[dim] = (place[dim] + step) % extent
                sources.append(device_at(*moved))
                plus.append(step == 1)
            links.append((dim, sources, plus, extent == 2, extent % 2 == 0))
            if extent == 2:
                break
    return links, parity


def fetch(block, sources, senders):
    pairs = [(source, i) for i, source in enumerate(sources) if senders(source)]
    return lax.ppermute(block, axes, pairs)


def exchange(block, links, parity, odd):
    split = [i for i, (dim, _, _, _, paired) in enumerate(links) if paired and dim in (0, 3)]
    along_z = [i for i, link in enumerate(links) if link[0] == 2]
    split += [i for i in along_z[1:] if links[i][4]]
    middle = [i for i in range(len(links)) if i not in split and links[i][0] != 1]
    last = [i for i in range(len(links)) if links[i][0] == 1]

    def send(block, chosen, senders):
        return [fetch(block, links[i][1], senders) for i in chosen]

    from_odd = send(block, split, lambda device: parity[device] == 1)
    got = dict(zip(middle, send(block, middle, lambda device: True)))
    block, from_odd = lax.optimization_barrier((block, from_odd))
    from_even = send(block, split, lambda device: parity[device] == 0)
    got.update(zip(last, send(block, last, lambda device: True)))
    for i, first, second in zip(split, from_odd, from_even):
        got[i] = jnp.where(odd, second, first)
    return [got[i] for i in range(len(links))]


def local_term(residual, clover_inverse):
    rhs_count, _, _, sites = residual.shape
    rows = residual.reshape(rhs_count, 2, 2, 6, sites).astype(jnp.float32)
    clover = clover_inverse.astype(jnp.float32)

    def local_apply(left, right):
        return sum(left[:, :, b][None] * right[:, :, b][:, :, None] for b in range(6))

    local_real = local_apply(clover[0], rows[:, 0]) - local_apply(clover[1], rows[:, 1])
    local_imag = local_apply(clover[0], rows[:, 1]) + local_apply(clover[1], rows[:, 0])
    return local_real, local_imag


def body(residual, null_vectors, clover_inverse, coarse_op, vector_count):
    rhs_count = residual.shape[0]
    vec_total = null_vectors.shape[1]
    coarse_dim = 2 * vec_total
    sites = residual.shape[3]
    in_use = (lax.iota(jnp.int32, vec_total)[None, :] < vector_count[:, None]).astype(jnp.float32)[0]
    used = jnp.tile(in_use, 4)
    used, fine = lax.optimization_barrier((used, residual))

    parts = fine.transpose(1, 2, 0, 3).reshape(2, 2, 6, rhs_count, sites)
    fine_rows = jnp.stack(
        [jnp.concatenate([parts[0], parts[1]], 2), jnp.concatenate([parts[1], -parts[0]], 2)]
    )
    vectors = null_vectors.transpose(0, 2, 1, 3).reshape(2, 2, 6, vec_total, sites)
    product = jnp.einsum("pxcrs,pxcks->xrk", fine_rows, vectors, preferred_element_type=jnp.float32)
    pieces = [product[chi, part * rhs_count : (part + 1) * rhs_count] for part in range(2) for chi in range(2)]
    half = omega_step * (jnp.concatenate(pieces, 1) * used)

    operator = coarse_op.reshape(9, 2, coarse_dim, coarse_dim)
    links, parity = plan()
    me = (lax.axis_index("gx") * lax.axis_size("gz") + lax.axis_index("gz")) * lax.axis_size("ta")
    me = me + lax.axis_index("ta")
    odd = jnp.asarray(parity, jnp.int32)[me] == 1
    reached = []
    for dim, _, plus, merged, _ in links:
        above, below = operator[2 * dim + 1], operator[2 * dim + 2]
        if merged:
            reached.append(above + below)
        else:
            reached.append(jnp.where(jnp.asarray(plus)[me], above, below))

    def real_form(matrix):
        upper = jnp.concatenate([matrix[0], -matrix[1]], 1)
        lower = jnp.concatenate([matrix[1], matrix[0]], 1)
        return omega_step * jnp.concatenate([upper, lower], 0)

    own = jnp.eye(2 * coarse_dim, dtype=jnp.float32) - real_form(operator[0])
    around = jnp.concatenate([-real_form(part) for part in reached], 1)

    def apply(vector, matrix):
        return lax.dot_general(vector, matrix, (((1,), (1,)), ((), ())), precision=exact)

    coarse = half
    for sweep_id in range(ITERS - 1):
        moved = exchange(coarse, links, parity, odd)
        kept = half + apply(coarse, own)
        if sweep_id == 1:
            rows, clover, kept = lax.optimization_barrier((residual, clover_inverse, kept))
            local_real, local_imag = local_term(rows, clover)
        coarse = kept + apply(jnp.concatenate(moved, 1), around)

    rounded = coarse * used
    cut = [rounded[:, p * vec_total : (p + 1) * vec_total] for p in range(4)]
    by_real = jnp.stack([jnp.concatenate([cut[chi], cut[2 + chi]], 0) for chi in range(2)])
    by_imag = jnp.stack([jnp.concatenate([-cut[2 + chi], cut[chi]], 0) for chi in range(2)])
    weights = jnp.stack([by_real, by_imag]).astype(jnp.bfloat16)
    lift = jnp.einsum("pxrk,pxcks->xcrs", weights, vectors, preferred_element_type=jnp.float32)
    lift = lift.reshape(2, 6, 2, rhs_count, sites).transpose(3, 2, 0, 1, 4)
    result = jnp.stack([local_real, local_imag], 1) + lift
    return result.reshape(rhs_count, 2, 12, sites).astype(jnp.bfloat16)


def solution(mesh):
    in_specs = (
        P(None, None, None, ("gx", "gz", "ta")),
        P(None, None, None, ("gx", "gz", "ta")),
        P(None, None, None, None, ("gx", "gz", "ta")),
        P(("gx", "gz", "ta"), None, None, None),
        P(("gx", "gz", "ta")),
    )
    out_specs = P(None, None, None, ("gx", "gz", "ta"))
    return jax.shard_map(body, mesh=mesh, in_specs=in_specs, out_specs=out_specs, check_vma=False)
```

```python
import jax
import jax.numpy as jnp
from jax import lax
from jax.sharding import PartitionSpec as P

ITERS = 5


omega_step = 0.5
exact = lax.Precision.HIGHEST
axes = ("gx", "gz", "ta")


def routes():
    total = lax.axis_size("gx")
    plane_y = min(8, total // 2)
    plane_x = total // plane_y

    def ring(count):
        up = [(i + 1) % count for i in range(count)]
        down = [(i - 1) % count for i in range(count)]
        if count % 2:
            return up, down, False
        even = [(up if i % 2 == 0 else down)[i] for i in range(count)]
        odd = [(down if i % 2 == 0 else up)[i] for i in range(count)]
        return even, odd, True

    links = []
    first, second, paired = ring(plane_x)
    links.append(
        [("gx", tuple(way[g // plane_y] * plane_y + g % plane_y for g in range(total))) for way in (first, second)]
        + [paired, lax.axis_index("gx") // plane_y]
    )
    first, second, paired = ring(plane_y)
    links.append(
        [("gx", tuple((g // plane_y) * plane_y + way[g % plane_y] for g in range(total))) for way in (first, second)]
        + [paired, lax.axis_index("gx") % plane_y]
    )
    for axis in ("gz", "ta"):
        first, second, paired = ring(lax.axis_size(axis))
        links.append([(axis, tuple(first)), (axis, tuple(second)), paired, lax.axis_index(axis)])
    return links


def fetch(block, link):
    axis, sources = link
    return lax.ppermute(block, axis, [(source, i) for i, source in enumerate(sources)])


def local_term(residual, clover_inverse):
    rhs_count, _, _, sites = residual.shape
    rows = residual.reshape(rhs_count, 2, 2, 6, sites).astype(jnp.float32)
    clover = clover_inverse.astype(jnp.float32)

    def local_apply(left, right):
        return sum(left[:, :, b][None] * right[:, :, b][:, :, None] for b in range(6))

    local_real = local_apply(clover[0], rows[:, 0]) - local_apply(clover[1], rows[:, 1])
    local_imag = local_apply(clover[0], rows[:, 1]) + local_apply(clover[1], rows[:, 0])
    return local_real, local_imag


def real_form(matrix, dim):
    matrix = matrix.reshape(2, dim, dim)
    upper = jnp.concatenate([matrix[0], -matrix[1]], 1)
    lower = jnp.concatenate([matrix[1], matrix[0]], 1)
    return omega_step * jnp.concatenate([upper, lower], 0)


def apply(vector, matrix):
    return lax.dot_general(vector, matrix, (((1,), (1,)), ((), ())), precision=exact)


def own_form(operator, dim):
    return jnp.eye(2 * dim, dtype=jnp.float32) - real_form(operator, dim)


def sweep_alone(half, operator, dim, held):
    grouped = {}
    for way, (first, second, paired, place) in enumerate(routes()):
        plus, minus = operator[2 * way + 1], operator[2 * way + 2]
        if first == second:
            grouped[first] = plus + minus
        else:
            swap = (place % 2 == 1) & paired
            grouped[first] = jnp.where(swap, minus, plus)
            grouped[second] = jnp.where(swap, plus, minus)

    def reach(link):
        axis, sources = link
        return ("gz", "ta", "gx").index(axis), -max(abs(source - i) for i, source in enumerate(sources))

    order = sorted(grouped, key=reach)
    own = own_form(operator[0], dim)
    around = jnp.concatenate([-real_form(grouped[link], dim) for link in order], 1)
    coarse = half
    for sweep_id in range(ITERS - 1):
        moved = [fetch(coarse, link) for link in order]
        kept = half + apply(coarse, own)
        if sweep_id == 1:
            rows, clover, kept = lax.optimization_barrier((*held, kept))
            local = local_term(rows, clover)
        coarse = kept + apply(jnp.concatenate(moved, 1), around)
    return coarse, local


def shares_chip():
    total, depth, slabs = (lax.axis_size(axis) for axis in axes)
    return total == 4 and depth == 4 and slabs == 2


def pair_routes():
    total, depth, slabs = (lax.axis_size(axis) for axis in axes)

    def device_at(group, level, slab):
        return (group * depth + level) * slabs + slab

    first, second, mate = [], [], []
    for group in range(total):
        for level in range(depth):
            for slab in range(slabs):
                step = 1 if level % 2 == 0 else -1
                if group % 2 == 0:
                    first.append(device_at(group, level, 1 - slab))
                    second.append(device_at(group ^ 2, level, slab))
                else:
                    first.append(device_at(group, (level - step) % depth, slab))
                    second.append(device_at(group, (level + step) % depth, slab))
                mate.append(device_at(group ^ 1, level, slab))
    return first, second, mate


def sweep_in_pairs(half, operator, dim, held):
    first, second, mate = pair_routes()

    def swap(block, sources):
        return lax.ppermute(block, axes, [(source, i) for i, source in enumerate(sources)])

    along_t_x = jnp.stack([operator[7] + operator[8], operator[1] + operator[2]])
    odd_level = lax.axis_index("gz") % 2 == 1
    along_z = jnp.stack(
        [jnp.where(odd_level, operator[5], operator[6]), jnp.where(odd_level, operator[6], operator[5])]
    )
    upper = lax.axis_index("gx") % 2 == 1
    mine = jnp.where(upper, along_z, along_t_x)
    theirs = swap(jnp.where(upper, along_t_x, along_z), mate)
    inside = jnp.concatenate([own_form(operator[0], dim), -real_form(operator[3] + operator[4], dim)], 1)
    around = jnp.stack(
        [
            jnp.concatenate([-real_form(part[0], dim), -real_form(part[1], dim)], 1)
            for part in (mine, theirs)
        ]
    )

    pair = jnp.stack([half, swap(half, mate)])
    for sweep_id in range(ITERS - 1):
        moved = [swap(pair, first), swap(pair, second)]
        kept = half + apply(jnp.concatenate([pair[0], pair[1]], 1), inside)
        if sweep_id == 1:
            rows, clover, kept = lax.optimization_barrier((*held, kept))
            local = local_term(rows, clover)
        part = lax.dot_general(
            jnp.concatenate(moved, 2), around, (((2,), (2,)), ((0,), (0,))), precision=exact
        )
        part = part + jnp.stack([kept, jnp.zeros_like(kept)])
        if sweep_id < ITERS - 2:
            other = swap(part, mate)
            pair = part + jnp.stack([other[1], other[0]])
    return part[0] + swap(part[1], mate), local


def body(residual, null_vectors, clover_inverse, coarse_op, vector_count):
    rhs_count = residual.shape[0]
    vec_total = null_vectors.shape[1]
    coarse_dim = 2 * vec_total
    sites = residual.shape[3]
    in_use = (lax.iota(jnp.int32, vec_total)[None, :] < vector_count[:, None]).astype(jnp.float32)[0]
    used = jnp.tile(in_use, 4)
    used, fine = lax.optimization_barrier((used, residual))

    parts = fine.transpose(1, 2, 0, 3).reshape(2, 2, 6, rhs_count, sites)
    fine_rows = jnp.stack(
        [jnp.concatenate([parts[0], parts[1]], 2), jnp.concatenate([parts[1], -parts[0]], 2)]
    )
    vectors = null_vectors.transpose(0, 2, 1, 3).reshape(2, 2, 6, vec_total, sites)
    product = jnp.einsum("pxcrs,pxcks->xrk", fine_rows, vectors, preferred_element_type=jnp.float32)
    pieces = [product[chi, part * rhs_count : (part + 1) * rhs_count] for part in range(2) for chi in range(2)]
    half = omega_step * (jnp.concatenate(pieces, 1) * used)

    operator = coarse_op.reshape(9, 2, coarse_dim * coarse_dim)
    held = (residual, clover_inverse)
    if shares_chip():
        coarse, local = sweep_in_pairs(half, operator, coarse_dim, held)
    else:
        coarse, local = sweep_alone(half, operator, coarse_dim, held)
    local_real, local_imag = local

    rounded = coarse * used
    cut = [rounded[:, p * vec_total : (p + 1) * vec_total] for p in range(4)]
    by_real = jnp.stack([jnp.concatenate([cut[chi], cut[2 + chi]], 0) for chi in range(2)])
    by_imag = jnp.stack([jnp.concatenate([-cut[2 + chi], cut[chi]], 0) for chi in range(2)])
    weights = jnp.stack([by_real, by_imag]).astype(jnp.bfloat16)
    lift = jnp.einsum("pxrk,pxcks->xcrs", weights, vectors, preferred_element_type=jnp.float32)
    lift = lift.reshape(2, 6, 2, rhs_count, sites).transpose(3, 2, 0, 1, 4)
    result = jnp.stack([local_real, local_imag], 1) + lift
    return result.reshape(rhs_count, 2, 12, sites).astype(jnp.bfloat16)


def solution(mesh):
    in_specs = (
        P(None, None, None, ("gx", "gz", "ta")),
        P(None, None, None, ("gx", "gz", "ta")),
        P(None, None, None, None, ("gx", "gz", "ta")),
        P(("gx", "gz", "ta"), None, None, None),
        P(("gx", "gz", "ta")),
    )
    out_specs = P(None, None, None, ("gx", "gz", "ta"))
    return jax.shard_map(body, mesh=mesh, in_specs=in_specs, out_specs=out_specs, check_vma=False)
```

```python
import jax
import jax.numpy as jnp
from jax import lax
from jax.experimental import pallas as pl
from jax.experimental.pallas import tpu as pltpu
from jax.sharding import PartitionSpec as P

ITERS = 5


omega_step = 0.5
exact = lax.Precision.HIGHEST
axes = ("gx", "gz", "ta")


def routes():
    total = lax.axis_size("gx")
    plane_y = min(8, total // 2)
    plane_x = total // plane_y

    def ring(count):
        up = [(i + 1) % count for i in range(count)]
        down = [(i - 1) % count for i in range(count)]
        if count % 2:
            return up, down, False
        even = [(up if i % 2 == 0 else down)[i] for i in range(count)]
        odd = [(down if i % 2 == 0 else up)[i] for i in range(count)]
        return even, odd, True

    links = []
    first, second, paired = ring(plane_x)
    links.append(
        [("gx", tuple(way[g // plane_y] * plane_y + g % plane_y for g in range(total))) for way in (first, second)]
        + [paired, lax.axis_index("gx") // plane_y]
    )
    first, second, paired = ring(plane_y)
    links.append(
        [("gx", tuple((g // plane_y) * plane_y + way[g % plane_y] for g in range(total))) for way in (first, second)]
        + [paired, lax.axis_index("gx") % plane_y]
    )
    for axis in ("gz", "ta"):
        first, second, paired = ring(lax.axis_size(axis))
        links.append([(axis, tuple(first)), (axis, tuple(second)), paired, lax.axis_index(axis)])
    return links


def fetch(block, link):
    axis, sources = link
    return lax.ppermute(block, axis, [(source, i) for i, source in enumerate(sources)])


def local_term(residual, clover_inverse):
    rhs_count, _, _, sites = residual.shape
    rows = residual.reshape(rhs_count, 2, 2, 6, sites).astype(jnp.float32)
    clover = clover_inverse.astype(jnp.float32)

    def local_apply(left, right):
        return sum(left[:, :, b][None] * right[:, :, b][:, :, None] for b in range(6))

    local_real = local_apply(clover[0], rows[:, 0]) - local_apply(clover[1], rows[:, 1])
    local_imag = local_apply(clover[0], rows[:, 1]) + local_apply(clover[1], rows[:, 0])
    return local_real, local_imag


def real_form(matrix, dim):
    matrix = matrix.reshape(2, dim, dim)
    upper = jnp.concatenate([matrix[0], -matrix[1]], 1)
    lower = jnp.concatenate([matrix[1], matrix[0]], 1)
    return omega_step * jnp.concatenate([upper, lower], 0)


def apply(vector, matrix):
    return lax.dot_general(vector, matrix, (((1,), (1,)), ((), ())), precision=exact)


def own_form(operator, dim):
    return jnp.eye(2 * dim, dtype=jnp.float32) - real_form(operator, dim)


def sweep_alone(half, operator, dim, held):
    grouped = {}
    for way, (first, second, paired, place) in enumerate(routes()):
        plus, minus = operator[2 * way + 1], operator[2 * way + 2]
        if first == second:
            grouped[first] = plus + minus
        else:
            swap = (place % 2 == 1) & paired
            grouped[first] = jnp.where(swap, minus, plus)
            grouped[second] = jnp.where(swap, plus, minus)

    def reach(link):
        axis, sources = link
        return ("gz", "ta", "gx").index(axis), -max(abs(source - i) for i, source in enumerate(sources))

    order = sorted(grouped, key=reach)
    own = own_form(operator[0], dim)
    around = jnp.concatenate([-real_form(grouped[link], dim) for link in order], 1)
    coarse = half
    for sweep_id in range(ITERS - 1):
        moved = [fetch(coarse, link) for link in order]
        kept = half + apply(coarse, own)
        if sweep_id == 1:
            rows, clover, kept = lax.optimization_barrier((*held, kept))
            local = local_term(rows, clover)
        coarse = kept + apply(jnp.concatenate(moved, 1), around)
    return coarse, local


def shares_chip():
    total, depth, slabs = (lax.axis_size(axis) for axis in axes)
    return total == 4 and depth == 4 and slabs == 2


def pair_routes():
    total, depth, slabs = (lax.axis_size(axis) for axis in axes)

    def device_at(group, level, slab):
        return (group * depth + level) * slabs + slab

    first, second, mate = [], [], []
    for group in range(total):
        for level in range(depth):
            for slab in range(slabs):
                step = 1 if level % 2 == 0 else -1
                if group % 2 == 0:
                    first.append(device_at(group, level, 1 - slab))
                    second.append(device_at(group ^ 2, level, slab))
                else:
                    first.append(device_at(group, (level - step) % depth, slab))
                    second.append(device_at(group, (level + step) % depth, slab))
                mate.append(device_at(group ^ 1, level, slab))
    return first, second, mate


def real_blocks(flat, dim, has_own):
    blocks = flat.shape[0]

    def kernel(flat_ref, out_ref, rows_ref):
        packed = jnp.concatenate([flat_ref[block, link] for block in range(blocks) for link in range(2)], 0)
        for i in range(dim):
            rows_ref[pl.ds(i, 4 * blocks, stride=dim), :] = packed[:, i * dim : (i + 1) * dim]
        row = lax.broadcasted_iota(jnp.int32, (dim, dim), 0)
        col = lax.broadcasted_iota(jnp.int32, (dim, dim), 1)
        for block in range(blocks):
            for link in range(2):
                base = (2 * block + link) * 2 * dim
                real = -omega_step * rows_ref[base : base + dim]
                imag = omega_step * rows_ref[base + dim : base + 2 * dim]
                if has_own and link == 0:
                    real = real + jnp.where(row == col, 1.0, 0.0)
                place, left = ((block,), 2 * dim * link) if has_own else ((block, link), 0)
                low, high = pl.ds(0, dim), pl.ds(dim, dim)
                near, beyond = pl.ds(left, dim), pl.ds(left + dim, dim)
                out_ref[(*place, low, near)] = real
                out_ref[(*place, low, beyond)] = imag
                out_ref[(*place, high, near)] = -imag
                out_ref[(*place, high, beyond)] = real

    shape = (blocks, 2 * dim, 4 * dim) if has_own else (blocks, 2, 2 * dim, 2 * dim)
    return pl.pallas_call(
        kernel,
        out_shape=jax.ShapeDtypeStruct(shape, jnp.float32),
        in_specs=[pl.BlockSpec(memory_space=pltpu.VMEM)],
        out_specs=pl.BlockSpec(memory_space=pltpu.VMEM),
        scratch_shapes=[pltpu.VMEM((4 * blocks * dim, dim), jnp.float32)],
        compiler_params=pltpu.CompilerParams(vmem_limit_bytes=8 * 2**20),
        cost_estimate=pl.CostEstimate(flops=10**5, bytes_accessed=10**5, transcendentals=0),
    )(flat)


def sweep_in_pairs(half, operator, dim, held):
    first, second, mate = pair_routes()

    def swap(block, sources):
        return lax.ppermute(block, axes, [(source, i) for i, source in enumerate(sources)])

    along_t_x = jnp.stack([operator[7] + operator[8], operator[1] + operator[2]])
    odd_level = lax.axis_index("gz") % 2 == 1
    along_z = jnp.stack(
        [jnp.where(odd_level, operator[5], operator[6]), jnp.where(odd_level, operator[6], operator[5])]
    )
    upper = lax.axis_index("gx") % 2 == 1
    mine = jnp.where(upper, along_z, along_t_x)
    theirs = swap(jnp.where(upper, along_t_x, along_z), mate)
    inside = real_blocks(jnp.stack([operator[0], operator[3] + operator[4]])[None], dim, True)[0]
    around = real_blocks(jnp.stack([mine, theirs]), dim, False)

    pair = jnp.stack([half, swap(half, mate)])
    for sweep_id in range(ITERS - 1):
        moved = [swap(pair, first), swap(pair, second)]
        kept = half + apply(jnp.concatenate([pair[0], pair[1]], 1), inside)
        if sweep_id == 1:
            rows, clover, kept = lax.optimization_barrier((*held, kept))
            local = local_term(rows, clover)
        part = jnp.stack([kept, jnp.zeros_like(kept)])
        for link, vectors in enumerate(moved):
            part = part + lax.dot_general(
                vectors, around[:, link], (((2,), (2,)), ((0,), (0,))), precision=exact
            )
        if sweep_id < ITERS - 2:
            other = swap(part, mate)
            pair = part + jnp.stack([other[1], other[0]])
    return part[0] + swap(part[1], mate), local


def body(residual, null_vectors, clover_inverse, coarse_op, vector_count):
    rhs_count = residual.shape[0]
    vec_total = null_vectors.shape[1]
    coarse_dim = 2 * vec_total
    sites = residual.shape[3]
    in_use = (lax.iota(jnp.int32, vec_total)[None, :] < vector_count[:, None]).astype(jnp.float32)[0]
    used = jnp.tile(in_use, 4)
    used, fine = lax.optimization_barrier((used, residual))

    parts = fine.transpose(1, 2, 0, 3).reshape(2, 2, 6, rhs_count, sites)
    fine_rows = jnp.stack(
        [jnp.concatenate([parts[0], parts[1]], 2), jnp.concatenate([parts[1], -parts[0]], 2)]
    )
    vectors = null_vectors.transpose(0, 2, 1, 3).reshape(2, 2, 6, vec_total, sites)
    product = jnp.einsum("pxcrs,pxcks->xrk", fine_rows, vectors, preferred_element_type=jnp.float32)
    pieces = [product[chi, part * rhs_count : (part + 1) * rhs_count] for part in range(2) for chi in range(2)]
    half = omega_step * (jnp.concatenate(pieces, 1) * used)

    operator = coarse_op.reshape(9, 2, coarse_dim * coarse_dim)
    held = (residual, clover_inverse)
    if shares_chip():
        coarse, local = sweep_in_pairs(half, operator, coarse_dim, held)
    else:
        coarse, local = sweep_alone(half, operator, coarse_dim, held)
    local_real, local_imag = local

    rounded = coarse * used
    cut = [rounded[:, p * vec_total : (p + 1) * vec_total] for p in range(4)]
    by_real = jnp.stack([jnp.concatenate([cut[chi], cut[2 + chi]], 0) for chi in range(2)])
    by_imag = jnp.stack([jnp.concatenate([-cut[2 + chi], cut[chi]], 0) for chi in range(2)])
    weights = jnp.stack([by_real, by_imag]).astype(jnp.bfloat16)
    lift = jnp.einsum("pxrk,pxcks->xcrs", weights, vectors, preferred_element_type=jnp.float32)
    lift = lift.reshape(2, 6, 2, rhs_count, sites).transpose(3, 2, 0, 1, 4)
    result = jnp.stack([local_real, local_imag], 1) + lift
    return result.reshape(rhs_count, 2, 12, sites).astype(jnp.bfloat16)


def solution(mesh):
    in_specs = (
        P(None, None, None, ("gx", "gz", "ta")),
        P(None, None, None, ("gx", "gz", "ta")),
        P(None, None, None, None, ("gx", "gz", "ta")),
        P(("gx", "gz", "ta"), None, None, None),
        P(("gx", "gz", "ta")),
    )
    out_specs = P(None, None, None, ("gx", "gz", "ta"))
    return jax.shard_map(body, mesh=mesh, in_specs=in_specs, out_specs=out_specs, check_vma=False)
```

```python
import jax
import jax.numpy as jnp
from jax import lax
from jax.experimental import pallas as pl
from jax.experimental.pallas import tpu as pltpu
from jax.sharding import PartitionSpec as P

ITERS = 5


omega_step = 0.5
exact = lax.Precision.HIGHEST
axes = ("gx", "gz", "ta")


def routes():
    total = lax.axis_size("gx")
    plane_y = min(8, total // 2)
    plane_x = total // plane_y

    def ring(count):
        up = [(i + 1) % count for i in range(count)]
        down = [(i - 1) % count for i in range(count)]
        if count % 2:
            return up, down, False
        even = [(up if i % 2 == 0 else down)[i] for i in range(count)]
        odd = [(down if i % 2 == 0 else up)[i] for i in range(count)]
        return even, odd, True

    links = []
    first, second, paired = ring(plane_x)
    links.append(
        [("gx", tuple(way[g // plane_y] * plane_y + g % plane_y for g in range(total))) for way in (first, second)]
        + [paired, lax.axis_index("gx") // plane_y]
    )
    first, second, paired = ring(plane_y)
    links.append(
        [("gx", tuple((g // plane_y) * plane_y + way[g % plane_y] for g in range(total))) for way in (first, second)]
        + [paired, lax.axis_index("gx") % plane_y]
    )
    for axis in ("gz", "ta"):
        first, second, paired = ring(lax.axis_size(axis))
        links.append([(axis, tuple(first)), (axis, tuple(second)), paired, lax.axis_index(axis)])
    return links


def fetch(block, link):
    axis, sources = link
    return lax.ppermute(block, axis, [(source, i) for i, source in enumerate(sources)])


def restrict_kernel(
    count_ref, rows_hbm, vectors_hbm, out_ref, used_ref, rows_ref, vectors_ref, scratch, sems
):
    rhs, parts, _, sites = rows_ref.shape
    vecs = vectors_ref.shape[2]
    half = parts // 2
    copies = []
    for chi in range(2):
        span = pl.ds(half * chi, half)
        copies.append(
            [
                pltpu.make_async_copy(rows_hbm.at[:, span], rows_ref.at[:, span], sems.at[2 * chi]),
                pltpu.make_async_copy(vectors_hbm.at[:, span], vectors_ref.at[:, span], sems.at[2 * chi + 1]),
            ]
        )
    for copy in copies[0] + copies[1]:
        copy.start()
    for chi in range(2):
        for copy in copies[chi]:
            copy.wait()
        total = jnp.zeros((2 * rhs, 2 * vecs), jnp.float32)
        for c in range(half * chi, half * chi + half):
            rows = rows_ref[:, c].reshape(2 * rhs, sites)
            vectors = jnp.concatenate([vectors_ref[0, c], vectors_ref[1, c]], 0)
            total += lax.dot_general(
                rows, vectors, (((1,), (1,)), ((), ())), preferred_element_type=jnp.float32
            )
        scratch[chi, :, : 2 * vecs] = total
    real, imag = [], []
    for chi in range(2):
        even = scratch[chi, pl.ds(0, rhs, stride=2), :]
        odd = scratch[chi, pl.ds(1, rhs, stride=2), :]
        real.append(even[:, :vecs] + odd[:, vecs : 2 * vecs])
        imag.append(odd[:, :vecs] - even[:, vecs : 2 * vecs])
    lane = lax.broadcasted_iota(jnp.int32, (rhs, vecs), 1)
    used = jnp.where(lane < count_ref[0], 1.0, 0.0)
    out_ref[...] = jnp.concatenate([omega_step * part * used for part in real + imag], 1)
    used_ref[...] = jnp.concatenate([used] * 4, 1)


def restrict(count, rows, vectors):
    rhs, vecs = rows.shape[0], vectors.shape[2]
    in_vmem = pl.BlockSpec(memory_space=pltpu.VMEM)
    in_hbm = pl.BlockSpec(memory_space=pltpu.HBM)
    return pl.pallas_call(
        restrict_kernel,
        out_shape=[jax.ShapeDtypeStruct((rhs, 4 * vecs), jnp.float32)] * 2,
        in_specs=[pl.BlockSpec(memory_space=pltpu.SMEM), in_hbm, in_hbm],
        out_specs=[in_vmem, in_vmem],
        scratch_shapes=[
            pltpu.VMEM(rows.shape, rows.dtype),
            pltpu.VMEM(vectors.shape, vectors.dtype),
            pltpu.VMEM((2, 2 * rhs, 128), jnp.float32),
            pltpu.SemaphoreType.DMA((4,)),
        ],
        compiler_params=pltpu.CompilerParams(vmem_limit_bytes=55168 * 2**10),
        cost_estimate=pl.CostEstimate(flops=10**7, bytes_accessed=5 * 10**5, transcendentals=0),
    )(count, rows, vectors)


def local_term(residual, clover_inverse):
    rhs_count, _, _, sites = residual.shape
    rows = residual.reshape(rhs_count, 2, 2, 6, sites).astype(jnp.float32)
    clover = clover_inverse.astype(jnp.float32)

    def local_apply(left, right):
        return sum(left[:, :, b][None] * right[:, :, b][:, :, None] for b in range(6))

    local_real = local_apply(clover[0], rows[:, 0]) - local_apply(clover[1], rows[:, 1])
    local_imag = local_apply(clover[0], rows[:, 1]) + local_apply(clover[1], rows[:, 0])
    return local_real, local_imag


def real_form(matrix, dim):
    matrix = matrix.reshape(2, dim, dim)
    upper = jnp.concatenate([matrix[0], -matrix[1]], 1)
    lower = jnp.concatenate([matrix[1], matrix[0]], 1)
    return omega_step * jnp.concatenate([upper, lower], 0)


def apply(vector, matrix):
    return lax.dot_general(vector, matrix, (((1,), (1,)), ((), ())), precision=exact)


def own_form(operator, dim):
    return jnp.eye(2 * dim, dtype=jnp.float32) - real_form(operator, dim)


def sweep_alone(half, operator, dim, held):
    grouped = {}
    for way, (first, second, paired, place) in enumerate(routes()):
        plus, minus = operator[2 * way + 1], operator[2 * way + 2]
        if first == second:
            grouped[first] = plus + minus
        else:
            swap = (place % 2 == 1) & paired
            grouped[first] = jnp.where(swap, minus, plus)
            grouped[second] = jnp.where(swap, plus, minus)

    def reach(link):
        axis, sources = link
        return ("gz", "ta", "gx").index(axis), -max(abs(source - i) for i, source in enumerate(sources))

    order = sorted(grouped, key=reach)
    own = own_form(operator[0], dim)
    around = jnp.concatenate([-real_form(grouped[link], dim) for link in order], 1)
    coarse = half
    for sweep_id in range(ITERS - 1):
        moved = [fetch(coarse, link) for link in order]
        kept = half + apply(coarse, own)
        if sweep_id == 1:
            rows, clover, kept = lax.optimization_barrier((*held, kept))
            local = local_term(rows, clover)
        coarse = kept + apply(jnp.concatenate(moved, 1), around)
    return coarse, local


def shares_chip():
    total, depth, slabs = (lax.axis_size(axis) for axis in axes)
    return total == 4 and depth == 4 and slabs == 2


def pair_routes():
    total, depth, slabs = (lax.axis_size(axis) for axis in axes)

    def device_at(group, level, slab):
        return (group * depth + level) * slabs + slab

    first, second, mate = [], [], []
    for group in range(total):
        for level in range(depth):
            for slab in range(slabs):
                step = 1 if level % 2 == 0 else -1
                if group % 2 == 0:
                    first.append(device_at(group, level, 1 - slab))
                    second.append(device_at(group ^ 2, level, slab))
                else:
                    first.append(device_at(group, (level - step) % depth, slab))
                    second.append(device_at(group, (level + step) % depth, slab))
                mate.append(device_at(group ^ 1, level, slab))
    return first, second, mate


def real_blocks(flat, dim, has_own):
    blocks = flat.shape[0]

    def kernel(flat_ref, out_ref, rows_ref):
        packed = jnp.concatenate([flat_ref[block, link] for block in range(blocks) for link in range(2)], 0)
        for i in range(dim):
            rows_ref[pl.ds(i, 4 * blocks, stride=dim), :] = packed[:, i * dim : (i + 1) * dim]
        row = lax.broadcasted_iota(jnp.int32, (dim, dim), 0)
        col = lax.broadcasted_iota(jnp.int32, (dim, dim), 1)
        for block in range(blocks):
            for link in range(2):
                base = (2 * block + link) * 2 * dim
                real = -omega_step * rows_ref[base : base + dim]
                imag = omega_step * rows_ref[base + dim : base + 2 * dim]
                if has_own and link == 0:
                    real = real + jnp.where(row == col, 1.0, 0.0)
                place, left = ((block,), 2 * dim * link) if has_own else ((block, link), 0)
                low, high = pl.ds(0, dim), pl.ds(dim, dim)
                near, beyond = pl.ds(left, dim), pl.ds(left + dim, dim)
                out_ref[(*place, low, near)] = real
                out_ref[(*place, low, beyond)] = imag
                out_ref[(*place, high, near)] = -imag
                out_ref[(*place, high, beyond)] = real

    shape = (blocks, 2 * dim, 4 * dim) if has_own else (blocks, 2, 2 * dim, 2 * dim)
    return pl.pallas_call(
        kernel,
        out_shape=jax.ShapeDtypeStruct(shape, jnp.float32),
        in_specs=[pl.BlockSpec(memory_space=pltpu.VMEM)],
        out_specs=pl.BlockSpec(memory_space=pltpu.VMEM),
        scratch_shapes=[pltpu.VMEM((4 * blocks * dim, dim), jnp.float32)],
        compiler_params=pltpu.CompilerParams(vmem_limit_bytes=8 * 2**20),
        cost_estimate=pl.CostEstimate(flops=10**5, bytes_accessed=10**5, transcendentals=0),
    )(flat)


def sweep_in_pairs(half, operator, dim, held):
    first, second, mate = pair_routes()

    def swap(block, sources):
        return lax.ppermute(block, axes, [(source, i) for i, source in enumerate(sources)])

    along_t_x = jnp.stack([operator[7] + operator[8], operator[1] + operator[2]])
    odd_level = lax.axis_index("gz") % 2 == 1
    along_z = jnp.stack(
        [jnp.where(odd_level, operator[5], operator[6]), jnp.where(odd_level, operator[6], operator[5])]
    )
    upper = lax.axis_index("gx") % 2 == 1
    mine = jnp.where(upper, along_z, along_t_x)
    theirs = swap(jnp.where(upper, along_t_x, along_z), mate)
    inside = real_blocks(jnp.stack([operator[0], operator[3] + operator[4]])[None], dim, True)[0]
    around = real_blocks(jnp.stack([mine, theirs]), dim, False)

    pair = jnp.stack([half, swap(half, mate)])
    for sweep_id in range(ITERS - 1):
        moved = [swap(pair, first), swap(pair, second)]
        kept = half + apply(jnp.concatenate([pair[0], pair[1]], 1), inside)
        if sweep_id == 1:
            rows, clover, kept = lax.optimization_barrier((*held, kept))
            local = local_term(rows, clover)
        part = jnp.stack([kept, jnp.zeros_like(kept)])
        for link, vectors in enumerate(moved):
            part = part + lax.dot_general(
                vectors, around[:, link], (((2,), (2,)), ((0,), (0,))), precision=exact
            )
        if sweep_id < ITERS - 2:
            other = swap(part, mate)
            pair = part + jnp.stack([other[1], other[0]])
    return part[0] + swap(part[1], mate), local


def body(residual, null_vectors, clover_inverse, coarse_op, vector_count):
    rhs_count = residual.shape[0]
    vec_total = null_vectors.shape[1]
    coarse_dim = 2 * vec_total
    sites = residual.shape[3]
    rows = residual.transpose(0, 2, 1, 3)
    stored = null_vectors.transpose(0, 2, 1, 3)
    half, used = restrict(vector_count, rows, stored)
    vectors = stored.reshape(2, 2, 6, vec_total, sites)

    coarse_op, half = lax.optimization_barrier((coarse_op, half))
    operator = coarse_op.reshape(9, 2, coarse_dim * coarse_dim)
    held = (residual, clover_inverse)
    if shares_chip():
        coarse, local = sweep_in_pairs(half, operator, coarse_dim, held)
    else:
        coarse, local = sweep_alone(half, operator, coarse_dim, held)
    local_real, local_imag = local

    rounded = coarse * used
    cut = [rounded[:, p * vec_total : (p + 1) * vec_total] for p in range(4)]
    by_real = jnp.stack([jnp.concatenate([cut[chi], cut[2 + chi]], 0) for chi in range(2)])
    by_imag = jnp.stack([jnp.concatenate([-cut[2 + chi], cut[chi]], 0) for chi in range(2)])
    weights = jnp.stack([by_real, by_imag]).astype(jnp.bfloat16)
    lift = jnp.einsum("pxrk,pxcks->xcrs", weights, vectors, preferred_element_type=jnp.float32)
    lift = lift.reshape(2, 6, 2, rhs_count, sites).transpose(3, 2, 0, 1, 4)
    result = jnp.stack([local_real, local_imag], 1) + lift
    return result.reshape(rhs_count, 2, 12, sites).astype(jnp.bfloat16)


def solution(mesh):
    in_specs = (
        P(None, None, None, ("gx", "gz", "ta")),
        P(None, None, None, ("gx", "gz", "ta")),
        P(None, None, None, None, ("gx", "gz", "ta")),
        P(("gx", "gz", "ta"), None, None, None),
        P(("gx", "gz", "ta")),
    )
    out_specs = P(None, None, None, ("gx", "gz", "ta"))
    return jax.shard_map(body, mesh=mesh, in_specs=in_specs, out_specs=out_specs, check_vma=False)
```

```python
import jax
import jax.numpy as jnp
from jax import lax
from jax.experimental import pallas as pl
from jax.experimental.pallas import tpu as pltpu
from jax.sharding import PartitionSpec as P

ITERS = 5


omega_step = 0.5
exact = lax.Precision.HIGHEST
axes = ("gx", "gz", "ta")


def routes():
    total = lax.axis_size("gx")
    plane_y = min(8, total // 2)
    plane_x = total // plane_y

    def ring(count):
        up = [(i + 1) % count for i in range(count)]
        down = [(i - 1) % count for i in range(count)]
        if count % 2:
            return up, down, False
        even = [(up if i % 2 == 0 else down)[i] for i in range(count)]
        odd = [(down if i % 2 == 0 else up)[i] for i in range(count)]
        return even, odd, True

    links = []
    first, second, paired = ring(plane_x)
    links.append(
        [("gx", tuple(way[g // plane_y] * plane_y + g % plane_y for g in range(total))) for way in (first, second)]
        + [paired, lax.axis_index("gx") // plane_y]
    )
    first, second, paired = ring(plane_y)
    links.append(
        [("gx", tuple((g // plane_y) * plane_y + way[g % plane_y] for g in range(total))) for way in (first, second)]
        + [paired, lax.axis_index("gx") % plane_y]
    )
    for axis in ("gz", "ta"):
        first, second, paired = ring(lax.axis_size(axis))
        links.append([(axis, tuple(first)), (axis, tuple(second)), paired, lax.axis_index(axis)])
    return links


def fetch(block, link):
    axis, sources = link
    return lax.ppermute(block, axis, [(source, i) for i, source in enumerate(sources)])


def restrict_kernel(
    count_ref, rows_hbm, vectors_hbm, out_ref, used_ref, rows_ref, vectors_ref, scratch, sems
):
    rhs, parts, _, sites = rows_ref.shape
    vecs = vectors_ref.shape[2]
    half = parts // 2
    copies = []
    for chi in range(2):
        span = pl.ds(half * chi, half)
        copies.append(
            [
                pltpu.make_async_copy(rows_hbm.at[:, span], rows_ref.at[:, span], sems.at[2 * chi]),
                pltpu.make_async_copy(vectors_hbm.at[:, span], vectors_ref.at[:, span], sems.at[2 * chi + 1]),
            ]
        )
    for copy in copies[0] + copies[1]:
        copy.start()
    for chi in range(2):
        for copy in copies[chi]:
            copy.wait()
        total = jnp.zeros((2 * rhs, 2 * vecs), jnp.float32)
        for c in range(half * chi, half * chi + half):
            rows = rows_ref[:, c].reshape(2 * rhs, sites)
            vectors = jnp.concatenate([vectors_ref[0, c], vectors_ref[1, c]], 0)
            total += lax.dot_general(
                rows, vectors, (((1,), (1,)), ((), ())), preferred_element_type=jnp.float32
            )
        scratch[chi, :, : 2 * vecs] = total
    real, imag = [], []
    for chi in range(2):
        even = scratch[chi, pl.ds(0, rhs, stride=2), :]
        odd = scratch[chi, pl.ds(1, rhs, stride=2), :]
        real.append(even[:, :vecs] + odd[:, vecs : 2 * vecs])
        imag.append(odd[:, :vecs] - even[:, vecs : 2 * vecs])
    lane = lax.broadcasted_iota(jnp.int32, (rhs, vecs), 1)
    used = jnp.where(lane < count_ref[0], 1.0, 0.0)
    out_ref[...] = jnp.concatenate([omega_step * part * used for part in real + imag], 1)
    used_ref[...] = jnp.concatenate([used] * 4, 1)


def restrict(count, rows, vectors):
    rhs, vecs = rows.shape[0], vectors.shape[2]
    in_vmem = pl.BlockSpec(memory_space=pltpu.VMEM)
    in_hbm = pl.BlockSpec(memory_space=pltpu.HBM)
    return pl.pallas_call(
        restrict_kernel,
        out_shape=[jax.ShapeDtypeStruct((rhs, 4 * vecs), jnp.float32)] * 2,
        in_specs=[pl.BlockSpec(memory_space=pltpu.SMEM), in_hbm, in_hbm],
        out_specs=[in_vmem, in_vmem],
        scratch_shapes=[
            pltpu.VMEM(rows.shape, rows.dtype),
            pltpu.VMEM(vectors.shape, vectors.dtype),
            pltpu.VMEM((2, 2 * rhs, 128), jnp.float32),
            pltpu.SemaphoreType.DMA((4,)),
        ],
        compiler_params=pltpu.CompilerParams(vmem_limit_bytes=55168 * 2**10),
        cost_estimate=pl.CostEstimate(flops=10**7, bytes_accessed=5 * 10**5, transcendentals=0),
    )(count, rows, vectors)


def extend_kernel(first_ref, second_ref, used_ref, vectors_ref, local_ref, out_hbm, out_ref, scratch, sems):
    rhs, parts, _, sites = out_ref.shape
    vecs = vectors_ref.shape[1] // 2
    half = parts // 2
    coarse = (first_ref[...] + second_ref[...]) * used_ref[...]
    for chi in range(2):
        real = coarse[:, chi * vecs : (chi + 1) * vecs]
        imag = coarse[:, (2 + chi) * vecs : (3 + chi) * vecs]
        scratch[chi, pl.ds(0, rhs, stride=2), : 2 * vecs] = jnp.concatenate([real, -imag], 1)
        scratch[chi, pl.ds(1, rhs, stride=2), : 2 * vecs] = jnp.concatenate([imag, real], 1)
    copies = []
    for chi in range(2):
        weights = scratch[chi, :, : 2 * vecs].astype(jnp.bfloat16)
        for c in range(half * chi, half * chi + half):
            lift = jnp.dot(weights, vectors_ref[c], preferred_element_type=jnp.float32)
            total = (local_ref[c] + lift).astype(jnp.bfloat16)
            out_ref[:, c] = total.reshape(rhs, 2, sites)
        span = pl.ds(half * chi, half)
        copies.append(pltpu.make_async_copy(out_ref.at[:, span], out_hbm.at[:, span], sems.at[chi]))
        copies[-1].start()
    for copy in copies:
        copy.wait()


small = pltpu.CompilerParams(vmem_limit_bytes=8 * 2**20)
in_vmem = pl.BlockSpec(memory_space=pltpu.VMEM)


def extend(summands, used, vectors, local):
    parts, _, sites = vectors.shape
    rhs = used.shape[0]
    shape = (rhs, parts, 2, sites)
    return pl.pallas_call(
        extend_kernel,
        out_shape=jax.ShapeDtypeStruct(shape, jnp.bfloat16),
        in_specs=[in_vmem] * 5,
        out_specs=pl.BlockSpec(memory_space=pltpu.HBM),
        scratch_shapes=[
            pltpu.VMEM(shape, jnp.bfloat16),
            pltpu.VMEM((2, 2 * rhs, 128), jnp.float32),
            pltpu.SemaphoreType.DMA((2,)),
        ],
        compiler_params=small,
        cost_estimate=pl.CostEstimate(flops=10**7, bytes_accessed=10**6, transcendentals=0),
    )(*summands, used, vectors, local)


def hold_kernel(vectors_ref, out_ref):
    vecs = vectors_ref.shape[2]
    for c in range(vectors_ref.shape[1]):
        out_ref[c] = jnp.concatenate([vectors_ref[0, c], vectors_ref[1, c]], 0)


def hold(vectors):
    _, parts, vecs, sites = vectors.shape
    return pl.pallas_call(
        hold_kernel,
        out_shape=jax.ShapeDtypeStruct((parts, 2 * vecs, sites), vectors.dtype),
        in_specs=[in_vmem],
        out_specs=in_vmem,
        compiler_params=small,
        cost_estimate=pl.CostEstimate(flops=10**5, bytes_accessed=10**5, transcendentals=0),
    )(vectors)


def local_kernel(rows_ref, clover_ref, out_ref):
    rhs, parts, _, sites = rows_ref.shape
    half = parts // 2
    row = lax.broadcasted_iota(jnp.int32, (2 * rhs, 2 * rhs), 0)
    col = lax.broadcasted_iota(jnp.int32, (2 * rhs, 2 * rhs), 1)
    turn = jnp.where((row % 2 == 0) & (col == row + 1), -1.0, 0.0)
    turn = jnp.where((row % 2 == 1) & (col == row - 1), 1.0, turn).astype(jnp.bfloat16)
    for chi in range(2):
        for start in range(0, sites, 128):
            lanes = slice(start, start + 128)
            plain, turned = [], []
            for b in range(half):
                rows = rows_ref[:, half * chi + b, :, lanes].reshape(2 * rhs, 128)
                plain.append(rows.astype(jnp.float32))
                turned.append(jnp.dot(turn, rows, preferred_element_type=jnp.float32))
            for a in range(half):
                total = jnp.zeros((2 * rhs, 128), jnp.float32)
                for b in range(half):
                    real = clover_ref[0, a, b, :, lanes].astype(jnp.float32)[chi : chi + 1]
                    imag = clover_ref[1, a, b, :, lanes].astype(jnp.float32)[chi : chi + 1]
                    total += real * plain[b] + imag * turned[b]
                out_ref[half * chi + a, :, lanes] = total


def local_term(rows, clover):
    rhs, parts, _, sites = rows.shape
    return pl.pallas_call(
        local_kernel,
        out_shape=jax.ShapeDtypeStruct((parts, 2 * rhs, sites), jnp.float32),
        in_specs=[in_vmem] * 2,
        out_specs=in_vmem,
        compiler_params=small,
        cost_estimate=pl.CostEstimate(flops=10**5, bytes_accessed=10**5, transcendentals=0),
    )(rows, clover)


def real_form(matrix, dim):
    matrix = matrix.reshape(2, dim, dim)
    upper = jnp.concatenate([matrix[0], -matrix[1]], 1)
    lower = jnp.concatenate([matrix[1], matrix[0]], 1)
    return omega_step * jnp.concatenate([upper, lower], 0)


def apply(vector, matrix):
    return lax.dot_general(vector, matrix, (((1,), (1,)), ((), ())), precision=exact)


def own_form(operator, dim):
    return jnp.eye(2 * dim, dtype=jnp.float32) - real_form(operator, dim)


def sweep_alone(half, operator, dim, held):
    grouped = {}
    for way, (first, second, paired, place) in enumerate(routes()):
        plus, minus = operator[2 * way + 1], operator[2 * way + 2]
        if first == second:
            grouped[first] = plus + minus
        else:
            swap = (place % 2 == 1) & paired
            grouped[first] = jnp.where(swap, minus, plus)
            grouped[second] = jnp.where(swap, plus, minus)

    def reach(link):
        axis, sources = link
        return ("gz", "ta", "gx").index(axis), -max(abs(source - i) for i, source in enumerate(sources))

    order = sorted(grouped, key=reach)
    own = own_form(operator[0], dim)
    around = jnp.concatenate([-real_form(grouped[link], dim) for link in order], 1)
    coarse = half
    for sweep_id in range(ITERS - 1):
        moved = [fetch(coarse, link) for link in order]
        kept = half + apply(coarse, own)
        if sweep_id == 1:
            rows, clover, kept = lax.optimization_barrier((*held[:2], kept))
            local, kept = lax.optimization_barrier((local_term(rows, clover), kept))
        if sweep_id == 2:
            stored, kept = lax.optimization_barrier((held[2], kept))
            vectors, kept = lax.optimization_barrier((hold(stored), kept))
        added = apply(jnp.concatenate(moved, 1), around)
        coarse = kept + added
    return (kept, added), vectors, local


def shares_chip():
    total, depth, slabs = (lax.axis_size(axis) for axis in axes)
    return total == 4 and depth == 4 and slabs == 2


def pair_routes():
    total, depth, slabs = (lax.axis_size(axis) for axis in axes)

    def device_at(group, level, slab):
        return (group * depth + level) * slabs + slab

    first, second, mate = [], [], []
    for group in range(total):
        for level in range(depth):
            for slab in range(slabs):
                step = 1 if level % 2 == 0 else -1
                if group % 2 == 0:
                    first.append(device_at(group, level, 1 - slab))
                    second.append(device_at(group ^ 2, level, slab))
                else:
                    first.append(device_at(group, (level - step) % depth, slab))
                    second.append(device_at(group, (level + step) % depth, slab))
                mate.append(device_at(group ^ 1, level, slab))
    return first, second, mate


def real_blocks(flat, dim, has_own):
    blocks = flat.shape[0]

    def kernel(flat_ref, out_ref, rows_ref):
        packed = jnp.concatenate([flat_ref[block, link] for block in range(blocks) for link in range(2)], 0)
        for i in range(dim):
            rows_ref[pl.ds(i, 4 * blocks, stride=dim), :] = packed[:, i * dim : (i + 1) * dim]
        row = lax.broadcasted_iota(jnp.int32, (dim, dim), 0)
        col = lax.broadcasted_iota(jnp.int32, (dim, dim), 1)
        for block in range(blocks):
            for link in range(2):
                base = (2 * block + link) * 2 * dim
                real = -omega_step * rows_ref[base : base + dim]
                imag = omega_step * rows_ref[base + dim : base + 2 * dim]
                if has_own and link == 0:
                    real = real + jnp.where(row == col, 1.0, 0.0)
                place, left = ((block,), 2 * dim * link) if has_own else ((block, link), 0)
                low, high = pl.ds(0, dim), pl.ds(dim, dim)
                near, beyond = pl.ds(left, dim), pl.ds(left + dim, dim)
                out_ref[(*place, low, near)] = real
                out_ref[(*place, low, beyond)] = imag
                out_ref[(*place, high, near)] = -imag
                out_ref[(*place, high, beyond)] = real

    shape = (blocks, 2 * dim, 4 * dim) if has_own else (blocks, 2, 2 * dim, 2 * dim)
    return pl.pallas_call(
        kernel,
        out_shape=jax.ShapeDtypeStruct(shape, jnp.float32),
        in_specs=[pl.BlockSpec(memory_space=pltpu.VMEM)],
        out_specs=pl.BlockSpec(memory_space=pltpu.VMEM),
        scratch_shapes=[pltpu.VMEM((4 * blocks * dim, dim), jnp.float32)],
        compiler_params=pltpu.CompilerParams(vmem_limit_bytes=8 * 2**20),
        cost_estimate=pl.CostEstimate(flops=10**5, bytes_accessed=10**5, transcendentals=0),
    )(flat)


def sweep_in_pairs(half, operator, dim, held):
    first, second, mate = pair_routes()

    def swap(block, sources):
        return lax.ppermute(block, axes, [(source, i) for i, source in enumerate(sources)])

    along_t_x = jnp.stack([operator[7] + operator[8], operator[1] + operator[2]])
    odd_level = lax.axis_index("gz") % 2 == 1
    along_z = jnp.stack(
        [jnp.where(odd_level, operator[5], operator[6]), jnp.where(odd_level, operator[6], operator[5])]
    )
    upper = lax.axis_index("gx") % 2 == 1
    mine = jnp.where(upper, along_z, along_t_x)
    theirs = swap(jnp.where(upper, along_t_x, along_z), mate)
    inside = real_blocks(jnp.stack([operator[0], operator[3] + operator[4]])[None], dim, True)[0]
    around = real_blocks(jnp.stack([mine, theirs]), dim, False)

    pair = jnp.stack([half, swap(half, mate)])
    for sweep_id in range(ITERS - 1):
        moved = [swap(pair, first), swap(pair, second)]
        kept = half + apply(jnp.concatenate([pair[0], pair[1]], 1), inside)
        if sweep_id == 1:
            rows, clover, kept = lax.optimization_barrier((*held[:2], kept))
            local, kept = lax.optimization_barrier((local_term(rows, clover), kept))
        if sweep_id == 2:
            stored, kept = lax.optimization_barrier((held[2], kept))
            vectors, kept = lax.optimization_barrier((hold(stored), kept))
        part = jnp.stack([kept, jnp.zeros_like(kept)])
        for link, block in enumerate(moved):
            part = part + lax.dot_general(
                block, around[:, link], (((2,), (2,)), ((0,), (0,))), precision=exact
            )
        if sweep_id < ITERS - 2:
            other = swap(part, mate)
            pair = part + jnp.stack([other[1], other[0]])
    return (part[0], swap(part[1], mate)), vectors, local


def body(residual, null_vectors, clover_inverse, coarse_op, vector_count):
    rhs_count = residual.shape[0]
    vec_total = null_vectors.shape[1]
    coarse_dim = 2 * vec_total
    sites = residual.shape[3]
    rows = residual.transpose(0, 2, 1, 3)
    stored = null_vectors.transpose(0, 2, 1, 3)
    half, used = restrict(vector_count, rows, stored)

    coarse_op, half = lax.optimization_barrier((coarse_op, half))
    operator = coarse_op.reshape(9, 2, coarse_dim * coarse_dim)
    held = (rows, clover_inverse.transpose(0, 2, 3, 1, 4), stored)
    if shares_chip():
        summands, vectors, local = sweep_in_pairs(half, operator, coarse_dim, held)
    else:
        summands, vectors, local = sweep_alone(half, operator, coarse_dim, held)
    return extend(summands, used, vectors, local).transpose(0, 2, 1, 3)


def solution(mesh):
    in_specs = (
        P(None, None, None, ("gx", "gz", "ta")),
        P(None, None, None, ("gx", "gz", "ta")),
        P(None, None, None, None, ("gx", "gz", "ta")),
        P(("gx", "gz", "ta"), None, None, None),
        P(("gx", "gz", "ta")),
    )
    out_specs = P(None, None, None, ("gx", "gz", "ta"))
    return jax.shard_map(body, mesh=mesh, in_specs=in_specs, out_specs=out_specs, check_vma=False)
```

```python
import jax
import jax.numpy as jnp
from jax import lax
from jax.experimental import pallas as pl
from jax.experimental.pallas import tpu as pltpu
from jax.sharding import PartitionSpec as P

ITERS = 5


omega_step = 0.5
exact = lax.Precision.HIGHEST
axes = ("gx", "gz", "ta")


def routes():
    total = lax.axis_size("gx")
    plane_y = min(8, total // 2)
    plane_x = total // plane_y

    def ring(count):
        up = [(i + 1) % count for i in range(count)]
        down = [(i - 1) % count for i in range(count)]
        if count % 2:
            return up, down, False
        even = [(up if i % 2 == 0 else down)[i] for i in range(count)]
        odd = [(down if i % 2 == 0 else up)[i] for i in range(count)]
        return even, odd, True

    links = []
    first, second, paired = ring(plane_x)
    links.append(
        [("gx", tuple(way[g // plane_y] * plane_y + g % plane_y for g in range(total))) for way in (first, second)]
        + [paired, lax.axis_index("gx") // plane_y]
    )
    first, second, paired = ring(plane_y)
    links.append(
        [("gx", tuple((g // plane_y) * plane_y + way[g % plane_y] for g in range(total))) for way in (first, second)]
        + [paired, lax.axis_index("gx") % plane_y]
    )
    for axis in ("gz", "ta"):
        first, second, paired = ring(lax.axis_size(axis))
        links.append([(axis, tuple(first)), (axis, tuple(second)), paired, lax.axis_index(axis)])
    return links


def fetch(block, link):
    axis, sources = link
    return lax.ppermute(block, axis, [(source, i) for i, source in enumerate(sources)])


def restrict_kernel(
    count_ref, rows_hbm, vectors_hbm, out_ref, used_ref, rows_ref, vectors_ref, scratch, sems
):
    rhs, parts, _, sites = rows_ref.shape
    vecs = vectors_ref.shape[2]
    half = parts // 2
    copies = []
    for chi in range(2):
        span = pl.ds(half * chi, half)
        copies.append(
            [
                pltpu.make_async_copy(rows_hbm.at[:, span], rows_ref.at[:, span], sems.at[2 * chi]),
                pltpu.make_async_copy(vectors_hbm.at[:, span], vectors_ref.at[:, span], sems.at[2 * chi + 1]),
            ]
        )
    for copy in copies[0] + copies[1]:
        copy.start()
    for chi in range(2):
        for copy in copies[chi]:
            copy.wait()
        total = jnp.zeros((2 * rhs, 2 * vecs), jnp.float32)
        for c in range(half * chi, half * chi + half):
            rows = rows_ref[:, c].reshape(2 * rhs, sites)
            vectors = jnp.concatenate([vectors_ref[0, c], vectors_ref[1, c]], 0)
            total += lax.dot_general(
                rows, vectors, (((1,), (1,)), ((), ())), preferred_element_type=jnp.float32
            )
        scratch[chi, :, : 2 * vecs] = total
    real, imag = [], []
    for chi in range(2):
        even = scratch[chi, pl.ds(0, rhs, stride=2), :]
        odd = scratch[chi, pl.ds(1, rhs, stride=2), :]
        real.append(even[:, :vecs] + odd[:, vecs : 2 * vecs])
        imag.append(odd[:, :vecs] - even[:, vecs : 2 * vecs])
    lane = lax.broadcasted_iota(jnp.int32, (rhs, vecs), 1)
    used = jnp.where(lane < count_ref[0], 1.0, 0.0)
    out_ref[...] = jnp.concatenate([omega_step * part * used for part in real + imag], 1)
    used_ref[...] = jnp.concatenate([used] * 4, 1)


def restrict(count, rows, vectors):
    rhs, vecs = rows.shape[0], vectors.shape[2]
    in_vmem = pl.BlockSpec(memory_space=pltpu.VMEM)
    in_hbm = pl.BlockSpec(memory_space=pltpu.HBM)
    return pl.pallas_call(
        restrict_kernel,
        out_shape=[jax.ShapeDtypeStruct((rhs, 4 * vecs), jnp.float32)] * 2,
        in_specs=[pl.BlockSpec(memory_space=pltpu.SMEM), in_hbm, in_hbm],
        out_specs=[in_vmem, in_vmem],
        scratch_shapes=[
            pltpu.VMEM(rows.shape, rows.dtype),
            pltpu.VMEM(vectors.shape, vectors.dtype),
            pltpu.VMEM((2, 2 * rhs, 128), jnp.float32),
            pltpu.SemaphoreType.DMA((4,)),
        ],
        compiler_params=pltpu.CompilerParams(vmem_limit_bytes=55168 * 2**10),
        cost_estimate=pl.CostEstimate(flops=10**7, bytes_accessed=5 * 10**5, transcendentals=0),
    )(count, rows, vectors)


def extend_kernel(first_ref, second_ref, used_ref, vectors_ref, local_ref, out_hbm, out_ref, scratch, sems):
    rhs, parts, _, sites = out_ref.shape
    vecs = vectors_ref.shape[1] // 2
    half = parts // 2
    coarse = (first_ref[...] + second_ref[...]) * used_ref[...]
    for chi in range(2):
        real = coarse[:, chi * vecs : (chi + 1) * vecs]
        imag = coarse[:, (2 + chi) * vecs : (3 + chi) * vecs]
        scratch[chi, pl.ds(0, rhs, stride=2), : 2 * vecs] = jnp.concatenate([real, -imag], 1)
        scratch[chi, pl.ds(1, rhs, stride=2), : 2 * vecs] = jnp.concatenate([imag, real], 1)
    copies = []
    for chi in range(2):
        weights = scratch[chi, :, : 2 * vecs].astype(jnp.bfloat16)
        for c in range(half * chi, half * chi + half):
            lift = jnp.dot(weights, vectors_ref[c], preferred_element_type=jnp.float32)
            total = (local_ref[c] + lift).astype(jnp.bfloat16)
            out_ref[:, c] = total.reshape(rhs, 2, sites)
        span = pl.ds(half * chi, half)
        copies.append(pltpu.make_async_copy(out_ref.at[:, span], out_hbm.at[:, span], sems.at[chi]))
        copies[-1].start()
    for copy in copies:
        copy.wait()


small = pltpu.CompilerParams(vmem_limit_bytes=8 * 2**20)
in_vmem = pl.BlockSpec(memory_space=pltpu.VMEM)


def extend(summands, used, vectors, local):
    parts, _, sites = vectors.shape
    rhs = used.shape[0]
    shape = (rhs, parts, 2, sites)
    return pl.pallas_call(
        extend_kernel,
        out_shape=jax.ShapeDtypeStruct(shape, jnp.bfloat16),
        in_specs=[in_vmem] * 5,
        out_specs=pl.BlockSpec(memory_space=pltpu.HBM),
        scratch_shapes=[
            pltpu.VMEM(shape, jnp.bfloat16),
            pltpu.VMEM((2, 2 * rhs, 128), jnp.float32),
            pltpu.SemaphoreType.DMA((2,)),
        ],
        compiler_params=small,
        cost_estimate=pl.CostEstimate(flops=10**7, bytes_accessed=10**6, transcendentals=0),
    )(*summands, used, vectors, local)


def hold_kernel(vectors_ref, out_ref):
    vecs = vectors_ref.shape[2]
    for c in range(vectors_ref.shape[1]):
        out_ref[c] = jnp.concatenate([vectors_ref[0, c], vectors_ref[1, c]], 0)


def hold(vectors):
    _, parts, vecs, sites = vectors.shape
    return pl.pallas_call(
        hold_kernel,
        out_shape=jax.ShapeDtypeStruct((parts, 2 * vecs, sites), vectors.dtype),
        in_specs=[in_vmem],
        out_specs=in_vmem,
        compiler_params=small,
        cost_estimate=pl.CostEstimate(flops=10**5, bytes_accessed=10**5, transcendentals=0),
    )(vectors)


def local_kernel(rows_ref, clover_ref, out_ref):
    rhs, parts, _, sites = rows_ref.shape
    half = parts // 2
    row = lax.broadcasted_iota(jnp.int32, (2 * rhs, 2 * rhs), 0)
    col = lax.broadcasted_iota(jnp.int32, (2 * rhs, 2 * rhs), 1)
    turn = jnp.where((row % 2 == 0) & (col == row + 1), -1.0, 0.0)
    turn = jnp.where((row % 2 == 1) & (col == row - 1), 1.0, turn).astype(jnp.bfloat16)
    for chi in range(2):
        for start in range(0, sites, 128):
            lanes = slice(start, start + 128)
            plain, turned = [], []
            for b in range(half):
                rows = rows_ref[:, half * chi + b, :, lanes].reshape(2 * rhs, 128)
                plain.append(rows.astype(jnp.float32))
                turned.append(jnp.dot(turn, rows, preferred_element_type=jnp.float32))
            for a in range(half):
                total = jnp.zeros((2 * rhs, 128), jnp.float32)
                for b in range(half):
                    real = clover_ref[0, a, b, :, lanes].astype(jnp.float32)[chi : chi + 1]
                    imag = clover_ref[1, a, b, :, lanes].astype(jnp.float32)[chi : chi + 1]
                    total += real * plain[b] + imag * turned[b]
                out_ref[half * chi + a, :, lanes] = total


def local_term(rows, clover):
    rhs, parts, _, sites = rows.shape
    return pl.pallas_call(
        local_kernel,
        out_shape=jax.ShapeDtypeStruct((parts, 2 * rhs, sites), jnp.float32),
        in_specs=[in_vmem] * 2,
        out_specs=in_vmem,
        compiler_params=small,
        cost_estimate=pl.CostEstimate(flops=10**5, bytes_accessed=10**5, transcendentals=0),
    )(rows, clover)


def real_form(matrix, dim):
    matrix = matrix.reshape(2, dim, dim)
    upper = jnp.concatenate([matrix[0], -matrix[1]], 1)
    lower = jnp.concatenate([matrix[1], matrix[0]], 1)
    return omega_step * jnp.concatenate([upper, lower], 0)


def apply(vector, matrix):
    return lax.dot_general(vector, matrix, (((1,), (1,)), ((), ())), precision=exact)


def own_form(operator, dim):
    return jnp.eye(2 * dim, dtype=jnp.float32) - real_form(operator, dim)


def sweep_alone(half, operator, dim, held):
    grouped = {}
    for way, (first, second, paired, place) in enumerate(routes()):
        plus, minus = operator[2 * way + 1], operator[2 * way + 2]
        if first == second:
            grouped[first] = plus + minus
        else:
            swap = (place % 2 == 1) & paired
            grouped[first] = jnp.where(swap, minus, plus)
            grouped[second] = jnp.where(swap, plus, minus)

    def reach(link):
        axis, sources = link
        return ("gz", "ta", "gx").index(axis), -max(abs(source - i) for i, source in enumerate(sources))

    order = sorted(grouped, key=reach)
    own = own_form(operator[0], dim)
    around = jnp.concatenate([-real_form(grouped[link], dim) for link in order], 1)
    coarse = half
    for sweep_id in range(ITERS - 1):
        moved = [fetch(coarse, link) for link in order]
        kept = half + apply(coarse, own)
        if sweep_id == 1:
            rows, clover, kept = lax.optimization_barrier((*held[:2], kept))
            local, kept = lax.optimization_barrier((local_term(rows, clover), kept))
        if sweep_id == 2:
            stored, kept = lax.optimization_barrier((held[2], kept))
            vectors, kept = lax.optimization_barrier((hold(stored), kept))
        added = apply(jnp.concatenate(moved, 1), around)
        coarse = kept + added
    return (kept, added), vectors, local


def shares_chip():
    total, depth, slabs = (lax.axis_size(axis) for axis in axes)
    return total == 4 and depth == 4 and slabs == 2


def pair_routes():
    total, depth, slabs = (lax.axis_size(axis) for axis in axes)

    def device_at(group, level, slab):
        return (group * depth + level) * slabs + slab

    first, second, mate = [], [], []
    for group in range(total):
        for level in range(depth):
            for slab in range(slabs):
                step = 1 if level % 2 == 0 else -1
                if group % 2 == 0:
                    first.append(device_at(group, level, 1 - slab))
                    second.append(device_at(group ^ 2, level, slab))
                else:
                    first.append(device_at(group, (level - step) % depth, slab))
                    second.append(device_at(group, (level + step) % depth, slab))
                mate.append(device_at(group ^ 1, level, slab))
    return first, second, mate


def real_blocks(flat, dim, has_own):
    blocks = flat.shape[0]

    def kernel(flat_ref, out_ref, rows_ref):
        packed = jnp.concatenate([flat_ref[block, link] for block in range(blocks) for link in range(2)], 0)
        for i in range(dim):
            rows_ref[pl.ds(i, 4 * blocks, stride=dim), :] = packed[:, i * dim : (i + 1) * dim]
        row = lax.broadcasted_iota(jnp.int32, (dim, dim), 0)
        col = lax.broadcasted_iota(jnp.int32, (dim, dim), 1)
        for block in range(blocks):
            for link in range(2):
                base = (2 * block + link) * 2 * dim
                real = -omega_step * rows_ref[base : base + dim]
                imag = omega_step * rows_ref[base + dim : base + 2 * dim]
                if has_own and link == 0:
                    real = real + jnp.where(row == col, 1.0, 0.0)
                place, left = ((block,), 2 * dim * link) if has_own else ((block, link), 0)
                low, high = pl.ds(0, dim), pl.ds(dim, dim)
                near, beyond = pl.ds(left, dim), pl.ds(left + dim, dim)
                out_ref[(*place, low, near)] = real
                out_ref[(*place, low, beyond)] = imag
                out_ref[(*place, high, near)] = -imag
                out_ref[(*place, high, beyond)] = real

    shape = (blocks, 2 * dim, 4 * dim) if has_own else (blocks, 2, 2 * dim, 2 * dim)
    return pl.pallas_call(
        kernel,
        out_shape=jax.ShapeDtypeStruct(shape, jnp.float32),
        in_specs=[pl.BlockSpec(memory_space=pltpu.VMEM)],
        out_specs=pl.BlockSpec(memory_space=pltpu.VMEM),
        scratch_shapes=[pltpu.VMEM((4 * blocks * dim, dim), jnp.float32)],
        compiler_params=pltpu.CompilerParams(vmem_limit_bytes=8 * 2**20),
        cost_estimate=pl.CostEstimate(flops=10**5, bytes_accessed=10**5, transcendentals=0),
    )(flat)


def sweep_in_pairs(half, operator, dim, held):
    first, second, mate = pair_routes()

    def swap(block, sources):
        return lax.ppermute(block, axes, [(source, i) for i, source in enumerate(sources)])

    along_t_x = jnp.stack([operator[7] + operator[8], operator[1] + operator[2]])
    odd_level = lax.axis_index("gz") % 2 == 1
    along_z = jnp.stack(
        [jnp.where(odd_level, operator[5], operator[6]), jnp.where(odd_level, operator[6], operator[5])]
    )
    upper = lax.axis_index("gx") % 2 == 1
    mine = jnp.where(upper, along_z, along_t_x)
    theirs = swap(jnp.where(upper, along_t_x, along_z), mate)
    inside = real_blocks(jnp.stack([operator[0], operator[3] + operator[4]])[None], dim, True)[0]
    around = real_blocks(jnp.stack([mine, theirs]), dim, False)

    pair = jnp.stack([half, swap(half, mate)])
    for sweep_id in range(ITERS - 1):
        moved = [swap(pair, first), swap(pair, second)]
        kept = half + apply(jnp.concatenate([pair[0], pair[1]], 1), inside)
        if sweep_id == 1:
            rows, clover, kept = lax.optimization_barrier((*held[:2], kept))
            local, kept = lax.optimization_barrier((local_term(rows, clover), kept))
        if sweep_id == 2:
            stored, kept = lax.optimization_barrier((held[2], kept))
            vectors, kept = lax.optimization_barrier((hold(stored), kept))
        def along(link):
            return lax.dot_general(
                moved[link], around[:, link], (((2,), (2,)), ((0,), (0,))), precision=exact
            )

        part = along(1) + (jnp.stack([kept, jnp.zeros_like(kept)]) + along(0))
        if sweep_id < ITERS - 2:
            other = swap(part, mate)
            pair = part + jnp.stack([other[1], other[0]])
    return (part[0], swap(part[1], mate)), vectors, local


def body(residual, null_vectors, clover_inverse, coarse_op, vector_count):
    rhs_count = residual.shape[0]
    vec_total = null_vectors.shape[1]
    coarse_dim = 2 * vec_total
    sites = residual.shape[3]
    rows = residual.transpose(0, 2, 1, 3)
    stored = null_vectors.transpose(0, 2, 1, 3)
    half, used = restrict(vector_count, rows, stored)

    coarse_op, half = lax.optimization_barrier((coarse_op, half))
    operator = coarse_op.reshape(9, 2, coarse_dim * coarse_dim)
    held = (rows, clover_inverse.transpose(0, 2, 3, 1, 4), stored)
    if shares_chip():
        summands, vectors, local = sweep_in_pairs(half, operator, coarse_dim, held)
    else:
        summands, vectors, local = sweep_alone(half, operator, coarse_dim, held)
    return extend(summands, used, vectors, local).transpose(0, 2, 1, 3)


def solution(mesh):
    in_specs = (
        P(None, None, None, ("gx", "gz", "ta")),
        P(None, None, None, ("gx", "gz", "ta")),
        P(None, None, None, None, ("gx", "gz", "ta")),
        P(("gx", "gz", "ta"), None, None, None),
        P(("gx", "gz", "ta")),
    )
    out_specs = P(None, None, None, ("gx", "gz", "ta"))
    return jax.shard_map(body, mesh=mesh, in_specs=in_specs, out_specs=out_specs, check_vma=False)
```

```python
import jax
import jax.numpy as jnp
from jax import lax
from jax.experimental import pallas as pl
from jax.experimental.pallas import tpu as pltpu
from jax.sharding import PartitionSpec as P

ITERS = 5


omega_step = 0.5
exact = lax.Precision.HIGHEST
axes = ("gx", "gz", "ta")


def routes():
    total = lax.axis_size("gx")
    plane_y = min(8, total // 2)
    plane_x = total // plane_y

    def ring(count):
        up = [(i + 1) % count for i in range(count)]
        down = [(i - 1) % count for i in range(count)]
        if count % 2:
            return up, down, False
        even = [(up if i % 2 == 0 else down)[i] for i in range(count)]
        odd = [(down if i % 2 == 0 else up)[i] for i in range(count)]
        return even, odd, True

    links = []
    first, second, paired = ring(plane_x)
    links.append(
        [("gx", tuple(way[g // plane_y] * plane_y + g % plane_y for g in range(total))) for way in (first, second)]
        + [paired, lax.axis_index("gx") // plane_y]
    )
    first, second, paired = ring(plane_y)
    links.append(
        [("gx", tuple((g // plane_y) * plane_y + way[g % plane_y] for g in range(total))) for way in (first, second)]
        + [paired, lax.axis_index("gx") % plane_y]
    )
    for axis in ("gz", "ta"):
        first, second, paired = ring(lax.axis_size(axis))
        links.append([(axis, tuple(first)), (axis, tuple(second)), paired, lax.axis_index(axis)])
    return links


def fetch(block, link):
    axis, sources = link
    return lax.ppermute(block, axis, [(source, i) for i, source in enumerate(sources)])


def restrict_kernel(
    count_ref, rows_hbm, vectors_hbm, out_ref, used_ref, rows_ref, vectors_ref, scratch, sems
):
    rhs, parts, _, sites = rows_ref.shape
    vecs = vectors_ref.shape[2]
    half = parts // 2
    copies = []
    for chi in range(2):
        span = pl.ds(half * chi, half)
        copies.append(
            [
                pltpu.make_async_copy(rows_hbm.at[:, span], rows_ref.at[:, span], sems.at[2 * chi]),
                pltpu.make_async_copy(vectors_hbm.at[:, span], vectors_ref.at[:, span], sems.at[2 * chi + 1]),
            ]
        )
    for copy in copies[0] + copies[1]:
        copy.start()
    for chi in range(2):
        for copy in copies[chi]:
            copy.wait()
        total = jnp.zeros((2 * rhs, 2 * vecs), jnp.float32)
        for c in range(half * chi, half * chi + half):
            rows = rows_ref[:, c].reshape(2 * rhs, sites)
            vectors = jnp.concatenate([vectors_ref[0, c], vectors_ref[1, c]], 0)
            total += lax.dot_general(
                rows, vectors, (((1,), (1,)), ((), ())), preferred_element_type=jnp.float32
            )
        scratch[chi, :, : 2 * vecs] = total
    real, imag = [], []
    for chi in range(2):
        even = scratch[chi, pl.ds(0, rhs, stride=2), :]
        odd = scratch[chi, pl.ds(1, rhs, stride=2), :]
        real.append(even[:, :vecs] + odd[:, vecs : 2 * vecs])
        imag.append(odd[:, :vecs] - even[:, vecs : 2 * vecs])
    lane = lax.broadcasted_iota(jnp.int32, (rhs, vecs), 1)
    used = jnp.where(lane < count_ref[0], 1.0, 0.0)
    out_ref[...] = jnp.concatenate([omega_step * part * used for part in real + imag], 1)
    used_ref[...] = jnp.concatenate([used] * 4, 1)


def restrict(count, rows, vectors):
    rhs, vecs = rows.shape[0], vectors.shape[2]
    in_vmem = pl.BlockSpec(memory_space=pltpu.VMEM)
    in_hbm = pl.BlockSpec(memory_space=pltpu.HBM)
    return pl.pallas_call(
        restrict_kernel,
        out_shape=[jax.ShapeDtypeStruct((rhs, 4 * vecs), jnp.float32)] * 2,
        in_specs=[pl.BlockSpec(memory_space=pltpu.SMEM), in_hbm, in_hbm],
        out_specs=[in_vmem, in_vmem],
        scratch_shapes=[
            pltpu.VMEM(rows.shape, rows.dtype),
            pltpu.VMEM(vectors.shape, vectors.dtype),
            pltpu.VMEM((2, 2 * rhs, 128), jnp.float32),
            pltpu.SemaphoreType.DMA((4,)),
        ],
        compiler_params=pltpu.CompilerParams(vmem_limit_bytes=55168 * 2**10),
        cost_estimate=pl.CostEstimate(flops=10**7, bytes_accessed=5 * 10**5, transcendentals=0),
    )(count, rows, vectors)


def extend_kernel(first_ref, second_ref, used_ref, vectors_ref, local_ref, out_hbm, out_ref, scratch, sems):
    rhs, parts, _, sites = out_ref.shape
    vecs = vectors_ref.shape[1] // 2
    half = parts // 2
    coarse = (first_ref[...] + second_ref[...]) * used_ref[...]
    for chi in range(2):
        real = coarse[:, chi * vecs : (chi + 1) * vecs]
        imag = coarse[:, (2 + chi) * vecs : (3 + chi) * vecs]
        scratch[chi, pl.ds(0, rhs, stride=2), : 2 * vecs] = jnp.concatenate([real, -imag], 1)
        scratch[chi, pl.ds(1, rhs, stride=2), : 2 * vecs] = jnp.concatenate([imag, real], 1)
    copies = []
    for chi in range(2):
        weights = scratch[chi, :, : 2 * vecs].astype(jnp.bfloat16)
        for c in range(half * chi, half * chi + half):
            lift = jnp.dot(weights, vectors_ref[c], preferred_element_type=jnp.float32)
            total = (local_ref[c] + lift).astype(jnp.bfloat16)
            out_ref[:, c] = total.reshape(rhs, 2, sites)
        span = pl.ds(half * chi, half)
        copies.append(pltpu.make_async_copy(out_ref.at[:, span], out_hbm.at[:, span], sems.at[chi]))
        copies[-1].start()
    for copy in copies:
        copy.wait()


small = pltpu.CompilerParams(vmem_limit_bytes=8 * 2**20)
in_vmem = pl.BlockSpec(memory_space=pltpu.VMEM)


def extend(summands, used, vectors, local):
    parts, _, sites = vectors.shape
    rhs = used.shape[0]
    shape = (rhs, parts, 2, sites)
    return pl.pallas_call(
        extend_kernel,
        out_shape=jax.ShapeDtypeStruct(shape, jnp.bfloat16),
        in_specs=[in_vmem] * 5,
        out_specs=pl.BlockSpec(memory_space=pltpu.HBM),
        scratch_shapes=[
            pltpu.VMEM(shape, jnp.bfloat16),
            pltpu.VMEM((2, 2 * rhs, 128), jnp.float32),
            pltpu.SemaphoreType.DMA((2,)),
        ],
        compiler_params=small,
        cost_estimate=pl.CostEstimate(flops=10**7, bytes_accessed=10**6, transcendentals=0),
    )(*summands, used, vectors, local)


def hold_kernel(vectors_ref, out_ref):
    vecs = vectors_ref.shape[2]
    for c in range(vectors_ref.shape[1]):
        out_ref[c] = jnp.concatenate([vectors_ref[0, c], vectors_ref[1, c]], 0)


def hold(vectors):
    _, parts, vecs, sites = vectors.shape
    return pl.pallas_call(
        hold_kernel,
        out_shape=jax.ShapeDtypeStruct((parts, 2 * vecs, sites), vectors.dtype),
        in_specs=[in_vmem],
        out_specs=in_vmem,
        compiler_params=small,
        cost_estimate=pl.CostEstimate(flops=10**5, bytes_accessed=10**5, transcendentals=0),
    )(vectors)


def local_kernel(rows_ref, clover_ref, out_ref):
    rhs, parts, _, sites = rows_ref.shape
    half = parts // 2
    row = lax.broadcasted_iota(jnp.int32, (2 * rhs, 2 * rhs), 0)
    col = lax.broadcasted_iota(jnp.int32, (2 * rhs, 2 * rhs), 1)
    turn = jnp.where((row % 2 == 0) & (col == row + 1), -1.0, 0.0)
    turn = jnp.where((row % 2 == 1) & (col == row - 1), 1.0, turn).astype(jnp.bfloat16)
    for chi in range(2):
        for start in range(0, sites, 128):
            lanes = slice(start, start + 128)
            plain, turned = [], []
            for b in range(half):
                rows = rows_ref[:, half * chi + b, :, lanes].reshape(2 * rhs, 128)
                plain.append(rows.astype(jnp.float32))
                turned.append(jnp.dot(turn, rows, preferred_element_type=jnp.float32))
            for a in range(half):
                total = jnp.zeros((2 * rhs, 128), jnp.float32)
                for b in range(half):
                    real = clover_ref[0, a, b, :, lanes].astype(jnp.float32)[chi : chi + 1]
                    imag = clover_ref[1, a, b, :, lanes].astype(jnp.float32)[chi : chi + 1]
                    total += real * plain[b] + imag * turned[b]
                out_ref[half * chi + a, :, lanes] = total


def local_term(rows, clover):
    rhs, parts, _, sites = rows.shape
    return pl.pallas_call(
        local_kernel,
        out_shape=jax.ShapeDtypeStruct((parts, 2 * rhs, sites), jnp.float32),
        in_specs=[in_vmem] * 2,
        out_specs=in_vmem,
        compiler_params=small,
        cost_estimate=pl.CostEstimate(flops=10**5, bytes_accessed=10**5, transcendentals=0),
    )(rows, clover)


def real_form(matrix, dim):
    matrix = matrix.reshape(2, dim, dim)
    upper = jnp.concatenate([matrix[0], -matrix[1]], 1)
    lower = jnp.concatenate([matrix[1], matrix[0]], 1)
    return omega_step * jnp.concatenate([upper, lower], 0)


def apply(vector, matrix):
    return lax.dot_general(vector, matrix, (((1,), (1,)), ((), ())), precision=exact)


def own_form(operator, dim):
    return jnp.eye(2 * dim, dtype=jnp.float32) - real_form(operator, dim)


def sweep_alone(half, operator, dim, held):
    grouped = {}
    for way, (first, second, paired, place) in enumerate(routes()):
        plus, minus = operator[2 * way + 1], operator[2 * way + 2]
        if first == second:
            grouped[first] = plus + minus
        else:
            swap = (place % 2 == 1) & paired
            grouped[first] = jnp.where(swap, minus, plus)
            grouped[second] = jnp.where(swap, plus, minus)

    def reach(link):
        axis, sources = link
        return ("gz", "ta", "gx").index(axis), -max(abs(source - i) for i, source in enumerate(sources))

    order = sorted(grouped, key=reach)
    own = own_form(operator[0], dim)
    around = jnp.concatenate([-real_form(grouped[link], dim) for link in order], 1)
    coarse = half
    for sweep_id in range(ITERS - 1):
        moved = [fetch(coarse, link) for link in order]
        kept = half + apply(coarse, own)
        if sweep_id == 1:
            rows, clover, kept = lax.optimization_barrier((*held[:2], kept))
            local, kept = lax.optimization_barrier((local_term(rows, clover), kept))
        if sweep_id == 2:
            stored, kept = lax.optimization_barrier((held[2], kept))
            vectors, kept = lax.optimization_barrier((hold(stored), kept))
        added = apply(jnp.concatenate(moved, 1), around)
        coarse = kept + added
    return (kept, added), vectors, local


def shares_chip():
    total, depth, slabs = (lax.axis_size(axis) for axis in axes)
    return total == 4 and depth == 4 and slabs == 2


def pair_routes():
    total, depth, slabs = (lax.axis_size(axis) for axis in axes)

    def device_at(group, level, slab):
        return (group * depth + level) * slabs + slab

    first, second, mate = [], [], []
    for group in range(total):
        for level in range(depth):
            for slab in range(slabs):
                step = 1 if level % 2 == 0 else -1
                if group % 2 == 0:
                    first.append(device_at(group, level, 1 - slab))
                    second.append(device_at(group ^ 2, level, slab))
                else:
                    first.append(device_at(group, (level - step) % depth, slab))
                    second.append(device_at(group, (level + step) % depth, slab))
                mate.append(device_at(group ^ 1, level, slab))
    return first, second, mate


def real_blocks(flat, dim, has_own):
    blocks = flat.shape[0]

    def kernel(flat_ref, out_ref, rows_ref):
        packed = jnp.concatenate([flat_ref[block, link] for block in range(blocks) for link in range(2)], 0)
        for i in range(dim):
            rows_ref[pl.ds(i, 4 * blocks, stride=dim), :] = packed[:, i * dim : (i + 1) * dim]
        row = lax.broadcasted_iota(jnp.int32, (dim, dim), 0)
        col = lax.broadcasted_iota(jnp.int32, (dim, dim), 1)
        for block in range(blocks):
            for link in range(2):
                base = (2 * block + link) * 2 * dim
                real = -omega_step * rows_ref[base : base + dim]
                imag = omega_step * rows_ref[base + dim : base + 2 * dim]
                if has_own and link == 0:
                    real = real + jnp.where(row == col, 1.0, 0.0)
                left = 2 * dim * link
                low, high = pl.ds(0, dim), pl.ds(dim, dim)
                near, beyond = pl.ds(left, dim), pl.ds(left + dim, dim)
                out_ref[block, low, near] = real
                out_ref[block, low, beyond] = imag
                out_ref[block, high, near] = -imag
                out_ref[block, high, beyond] = real

    shape = (blocks, 2 * dim, 4 * dim)
    return pl.pallas_call(
        kernel,
        out_shape=jax.ShapeDtypeStruct(shape, jnp.float32),
        in_specs=[pl.BlockSpec(memory_space=pltpu.VMEM)],
        out_specs=pl.BlockSpec(memory_space=pltpu.VMEM),
        scratch_shapes=[pltpu.VMEM((4 * blocks * dim, dim), jnp.float32)],
        compiler_params=pltpu.CompilerParams(vmem_limit_bytes=8 * 2**20),
        cost_estimate=pl.CostEstimate(flops=10**5, bytes_accessed=10**5, transcendentals=0),
    )(flat)


def sweep_in_pairs(half, operator, dim, held):
    first, second, mate = pair_routes()

    def swap(block, sources):
        return lax.ppermute(block, axes, [(source, i) for i, source in enumerate(sources)])

    along_x_t = jnp.stack([operator[1] + operator[2], operator[7] + operator[8]])
    odd_level = lax.axis_index("gz") % 2 == 1
    along_z = jnp.stack(
        [jnp.where(odd_level, operator[6], operator[5]), jnp.where(odd_level, operator[5], operator[6])]
    )
    upper = lax.axis_index("gx") % 2 == 1
    mine = jnp.where(upper, along_z, along_x_t)
    theirs = swap(jnp.where(upper, along_x_t, along_z), mate)
    inside = real_blocks(jnp.stack([operator[0], operator[3] + operator[4]])[None], dim, True)[0]
    around = real_blocks(jnp.stack([mine, theirs]), dim, False)

    pair = jnp.stack([half, swap(half, mate)])
    for sweep_id in range(ITERS - 1):
        moved = [swap(pair, second), swap(pair, first)]
        kept = half + apply(jnp.concatenate([pair[0], pair[1]], 1), inside)
        if sweep_id == 1:
            rows, clover, kept = lax.optimization_barrier((*held[:2], kept))
            local, kept = lax.optimization_barrier((local_term(rows, clover), kept))
        if sweep_id == 2:
            stored, kept = lax.optimization_barrier((held[2], kept))
            vectors, kept = lax.optimization_barrier((hold(stored), kept))
        part = lax.dot_general(
            jnp.concatenate(moved, 2), around, (((2,), (2,)), ((0,), (0,))), precision=exact
        )
        part = part + jnp.stack([kept, jnp.zeros_like(kept)])
        if sweep_id < ITERS - 2:
            other = swap(part, mate)
            pair = part + jnp.stack([other[1], other[0]])
    return (part[0], swap(part[1], mate)), vectors, local


def body(residual, null_vectors, clover_inverse, coarse_op, vector_count):
    rhs_count = residual.shape[0]
    vec_total = null_vectors.shape[1]
    coarse_dim = 2 * vec_total
    sites = residual.shape[3]
    rows = residual.transpose(0, 2, 1, 3)
    stored = null_vectors.transpose(0, 2, 1, 3)
    half, used = restrict(vector_count, rows, stored)

    coarse_op, half = lax.optimization_barrier((coarse_op, half))
    operator = coarse_op.reshape(9, 2, coarse_dim * coarse_dim)
    held = (rows, clover_inverse.transpose(0, 2, 3, 1, 4), stored)
    if shares_chip():
        summands, vectors, local = sweep_in_pairs(half, operator, coarse_dim, held)
    else:
        summands, vectors, local = sweep_alone(half, operator, coarse_dim, held)
    return extend(summands, used, vectors, local).transpose(0, 2, 1, 3)


def solution(mesh):
    in_specs = (
        P(None, None, None, ("gx", "gz", "ta")),
        P(None, None, None, ("gx", "gz", "ta")),
        P(None, None, None, None, ("gx", "gz", "ta")),
        P(("gx", "gz", "ta"), None, None, None),
        P(("gx", "gz", "ta")),
    )
    out_specs = P(None, None, None, ("gx", "gz", "ta"))
    return jax.shard_map(body, mesh=mesh, in_specs=in_specs, out_specs=out_specs, check_vma=False)
```

```python
import jax
import jax.numpy as jnp
from jax import lax
from jax.experimental import pallas as pl
from jax.experimental.pallas import tpu as pltpu
from jax.sharding import PartitionSpec as P

ITERS = 5


omega_step = 0.5
exact = lax.Precision.HIGHEST
axes = ("gx", "gz", "ta")


def routes():
    total = lax.axis_size("gx")
    plane_y = min(8, total // 2)
    plane_x = total // plane_y

    def ring(count):
        up = [(i + 1) % count for i in range(count)]
        down = [(i - 1) % count for i in range(count)]
        if count % 2:
            return up, down, False
        even = [(up if i % 2 == 0 else down)[i] for i in range(count)]
        odd = [(down if i % 2 == 0 else up)[i] for i in range(count)]
        return even, odd, True

    links = []
    first, second, paired = ring(plane_x)
    links.append(
        [("gx", tuple(way[g // plane_y] * plane_y + g % plane_y for g in range(total))) for way in (first, second)]
        + [paired, lax.axis_index("gx") // plane_y]
    )
    first, second, paired = ring(plane_y)
    links.append(
        [("gx", tuple((g // plane_y) * plane_y + way[g % plane_y] for g in range(total))) for way in (first, second)]
        + [paired, lax.axis_index("gx") % plane_y]
    )
    for axis in ("gz", "ta"):
        first, second, paired = ring(lax.axis_size(axis))
        links.append([(axis, tuple(first)), (axis, tuple(second)), paired, lax.axis_index(axis)])
    return links


def fetch(block, link):
    axis, sources = link
    return lax.ppermute(block, axis, [(source, i) for i, source in enumerate(sources)])


def restrict_kernel(
    count_ref, rows_hbm, vectors_hbm, out_ref, used_ref, rows_ref, vectors_ref, scratch, sems
):
    rhs, parts, _, sites = rows_ref.shape
    vecs = vectors_ref.shape[2]
    half = parts // 2
    step = half // 2
    copies = []
    for piece in range(4):
        span = pl.ds(step * piece, step)
        copies.append(
            [
                pltpu.make_async_copy(rows_hbm.at[:, span], rows_ref.at[:, span], sems.at[2 * piece]),
                pltpu.make_async_copy(vectors_hbm.at[:, span], vectors_ref.at[:, span], sems.at[2 * piece + 1]),
            ]
        )
        for copy in copies[-1]:
            copy.start()
    for chi in range(2):
        total = jnp.zeros((2 * rhs, 2 * vecs), jnp.float32)
        for piece in (2 * chi, 2 * chi + 1):
            for copy in copies[piece]:
                copy.wait()
            for c in range(step * piece, step * piece + step):
                rows = rows_ref[:, c].reshape(2 * rhs, sites)
                vectors = jnp.concatenate([vectors_ref[0, c], vectors_ref[1, c]], 0)
                total += lax.dot_general(
                    rows, vectors, (((1,), (1,)), ((), ())), preferred_element_type=jnp.float32
                )
        scratch[chi, :, : 2 * vecs] = total
    real, imag = [], []
    for chi in range(2):
        even = scratch[chi, pl.ds(0, rhs, stride=2), :]
        odd = scratch[chi, pl.ds(1, rhs, stride=2), :]
        real.append(even[:, :vecs] + odd[:, vecs : 2 * vecs])
        imag.append(odd[:, :vecs] - even[:, vecs : 2 * vecs])
    lane = lax.broadcasted_iota(jnp.int32, (rhs, vecs), 1)
    used = jnp.where(lane < count_ref[0], 1.0, 0.0)
    out_ref[...] = jnp.concatenate([omega_step * part * used for part in real + imag], 1)
    used_ref[...] = jnp.concatenate([used] * 4, 1)


def restrict(count, rows, vectors):
    rhs, vecs = rows.shape[0], vectors.shape[2]
    in_vmem = pl.BlockSpec(memory_space=pltpu.VMEM)
    in_hbm = pl.BlockSpec(memory_space=pltpu.HBM)
    return pl.pallas_call(
        restrict_kernel,
        out_shape=[jax.ShapeDtypeStruct((rhs, 4 * vecs), jnp.float32)] * 2,
        in_specs=[pl.BlockSpec(memory_space=pltpu.SMEM), in_hbm, in_hbm],
        out_specs=[in_vmem, in_vmem],
        scratch_shapes=[
            pltpu.VMEM(rows.shape, rows.dtype),
            pltpu.VMEM(vectors.shape, vectors.dtype),
            pltpu.VMEM((2, 2 * rhs, 128), jnp.float32),
            pltpu.SemaphoreType.DMA((8,)),
        ],
        compiler_params=pltpu.CompilerParams(vmem_limit_bytes=55168 * 2**10),
        cost_estimate=pl.CostEstimate(flops=10**7, bytes_accessed=5 * 10**5, transcendentals=0),
    )(count, rows, vectors)


def extend_kernel(first_ref, second_ref, used_ref, vectors_ref, local_ref, out_hbm, out_ref, scratch, sems):
    rhs, parts, _, sites = out_ref.shape
    vecs = vectors_ref.shape[1] // 2
    half = parts // 2
    coarse = (first_ref[...] + second_ref[...]) * used_ref[...]
    for chi in range(2):
        real = coarse[:, chi * vecs : (chi + 1) * vecs]
        imag = coarse[:, (2 + chi) * vecs : (3 + chi) * vecs]
        scratch[chi, pl.ds(0, rhs, stride=2), : 2 * vecs] = jnp.concatenate([real, -imag], 1)
        scratch[chi, pl.ds(1, rhs, stride=2), : 2 * vecs] = jnp.concatenate([imag, real], 1)
    copies = []
    step = half // 2
    for piece in range(4):
        weights = scratch[piece // 2, :, : 2 * vecs].astype(jnp.bfloat16)
        for c in range(step * piece, step * piece + step):
            lift = jnp.dot(weights, vectors_ref[c], preferred_element_type=jnp.float32)
            total = (local_ref[c] + lift).astype(jnp.bfloat16)
            out_ref[:, c] = total.reshape(rhs, 2, sites)
        span = pl.ds(step * piece, step)
        copies.append(pltpu.make_async_copy(out_ref.at[:, span], out_hbm.at[:, span], sems.at[piece]))
        copies[-1].start()
    for copy in copies:
        copy.wait()


small = pltpu.CompilerParams(vmem_limit_bytes=8 * 2**20)
in_vmem = pl.BlockSpec(memory_space=pltpu.VMEM)


def extend(summands, used, vectors, local):
    parts, _, sites = vectors.shape
    rhs = used.shape[0]
    shape = (rhs, parts, 2, sites)
    return pl.pallas_call(
        extend_kernel,
        out_shape=jax.ShapeDtypeStruct(shape, jnp.bfloat16),
        in_specs=[in_vmem] * 5,
        out_specs=pl.BlockSpec(memory_space=pltpu.HBM),
        scratch_shapes=[
            pltpu.VMEM(shape, jnp.bfloat16),
            pltpu.VMEM((2, 2 * rhs, 128), jnp.float32),
            pltpu.SemaphoreType.DMA((4,)),
        ],
        compiler_params=small,
        cost_estimate=pl.CostEstimate(flops=10**7, bytes_accessed=10**6, transcendentals=0),
    )(*summands, used, vectors, local)


def hold_kernel(vectors_ref, out_ref):
    vecs = vectors_ref.shape[2]
    for c in range(vectors_ref.shape[1]):
        out_ref[c] = jnp.concatenate([vectors_ref[0, c], vectors_ref[1, c]], 0)


def hold(vectors):
    _, parts, vecs, sites = vectors.shape
    return pl.pallas_call(
        hold_kernel,
        out_shape=jax.ShapeDtypeStruct((parts, 2 * vecs, sites), vectors.dtype),
        in_specs=[in_vmem],
        out_specs=in_vmem,
        compiler_params=small,
        cost_estimate=pl.CostEstimate(flops=10**5, bytes_accessed=10**5, transcendentals=0),
    )(vectors)


def local_kernel(rows_ref, clover_ref, out_ref):
    rhs, parts, _, sites = rows_ref.shape
    half = parts // 2
    row = lax.broadcasted_iota(jnp.int32, (2 * rhs, 2 * rhs), 0)
    col = lax.broadcasted_iota(jnp.int32, (2 * rhs, 2 * rhs), 1)
    turn = jnp.where((row % 2 == 0) & (col == row + 1), -1.0, 0.0)
    turn = jnp.where((row % 2 == 1) & (col == row - 1), 1.0, turn).astype(jnp.bfloat16)
    for chi in range(2):
        for start in range(0, sites, 128):
            lanes = slice(start, start + 128)
            plain, turned = [], []
            for b in range(half):
                rows = rows_ref[:, half * chi + b, :, lanes].reshape(2 * rhs, 128)
                plain.append(rows.astype(jnp.float32))
                turned.append(jnp.dot(turn, rows, preferred_element_type=jnp.float32))
            for a in range(half):
                total = jnp.zeros((2 * rhs, 128), jnp.float32)
                for b in range(half):
                    real = clover_ref[0, a, b, :, lanes].astype(jnp.float32)[chi : chi + 1]
                    imag = clover_ref[1, a, b, :, lanes].astype(jnp.float32)[chi : chi + 1]
                    total += real * plain[b] + imag * turned[b]
                out_ref[half * chi + a, :, lanes] = total


def local_term(rows, clover):
    rhs, parts, _, sites = rows.shape
    return pl.pallas_call(
        local_kernel,
        out_shape=jax.ShapeDtypeStruct((parts, 2 * rhs, sites), jnp.float32),
        in_specs=[in_vmem] * 2,
        out_specs=in_vmem,
        compiler_params=small,
        cost_estimate=pl.CostEstimate(flops=10**5, bytes_accessed=10**5, transcendentals=0),
    )(rows, clover)


def real_form(matrix, dim):
    matrix = matrix.reshape(2, dim, dim)
    upper = jnp.concatenate([matrix[0], -matrix[1]], 1)
    lower = jnp.concatenate([matrix[1], matrix[0]], 1)
    return omega_step * jnp.concatenate([upper, lower], 0)


def apply(vector, matrix, precision=exact):
    return lax.dot_general(vector, matrix, (((1,), (1,)), ((), ())), precision=precision)


def own_form(operator, dim):
    return jnp.eye(2 * dim, dtype=jnp.float32) - real_form(operator, dim)


def sweep_alone(half, operator, dim, held):
    grouped = {}
    for way, (first, second, paired, place) in enumerate(routes()):
        plus, minus = operator[2 * way + 1], operator[2 * way + 2]
        if first == second:
            grouped[first] = plus + minus
        else:
            swap = (place % 2 == 1) & paired
            grouped[first] = jnp.where(swap, minus, plus)
            grouped[second] = jnp.where(swap, plus, minus)

    def reach(link):
        axis, sources = link
        return ("gz", "ta", "gx").index(axis), -max(abs(source - i) for i, source in enumerate(sources))

    order = sorted(grouped, key=reach)
    own = own_form(operator[0], dim)
    around = jnp.concatenate([-real_form(grouped[link], dim) for link in order], 1)
    coarse = half
    for sweep_id in range(ITERS - 1):
        moved = [fetch(coarse, link) for link in order]
        kept = half + apply(coarse, own)
        if sweep_id == 1:
            rows, clover, kept = lax.optimization_barrier((*held[:2], kept))
            local, kept = lax.optimization_barrier((local_term(rows, clover), kept))
        if sweep_id == 2:
            stored, kept = lax.optimization_barrier((held[2], kept))
            vectors, kept = lax.optimization_barrier((hold(stored), kept))
        added = apply(jnp.concatenate(moved, 1), around)
        coarse = kept + added
    return (kept, added), vectors, local


def shares_chip():
    total, depth, slabs = (lax.axis_size(axis) for axis in axes)
    return total == 4 and depth == 4 and slabs == 2


def pair_routes():
    total, depth, slabs = (lax.axis_size(axis) for axis in axes)

    def device_at(group, level, slab):
        return (group * depth + level) * slabs + slab

    first, second, mate = [], [], []
    for group in range(total):
        for level in range(depth):
            for slab in range(slabs):
                step = 1 if level % 2 == 0 else -1
                if group % 2 == 0:
                    first.append(device_at(group, level, 1 - slab))
                    second.append(device_at(group ^ 2, level, slab))
                else:
                    first.append(device_at(group, (level - step) % depth, slab))
                    second.append(device_at(group, (level + step) % depth, slab))
                mate.append(device_at(group ^ 1, level, slab))
    return first, second, mate


def real_blocks(flat, dim, has_own):
    blocks = flat.shape[0]

    def kernel(flat_ref, out_ref, rows_ref):
        packed = jnp.concatenate([flat_ref[block, link] for block in range(blocks) for link in range(2)], 0)
        for i in range(dim):
            rows_ref[pl.ds(i, 4 * blocks, stride=dim), :] = packed[:, i * dim : (i + 1) * dim]
        row = lax.broadcasted_iota(jnp.int32, (dim, dim), 0)
        col = lax.broadcasted_iota(jnp.int32, (dim, dim), 1)
        for block in range(blocks):
            for link in range(2):
                base = (2 * block + link) * 2 * dim
                real = -omega_step * rows_ref[base : base + dim]
                imag = omega_step * rows_ref[base + dim : base + 2 * dim]
                if has_own and link == 0:
                    real = real + jnp.where(row == col, 1.0, 0.0)
                place, left = ((block,), 2 * dim * link) if has_own else ((block, link), 0)
                low, high = pl.ds(0, dim), pl.ds(dim, dim)
                near, beyond = pl.ds(left, dim), pl.ds(left + dim, dim)
                out_ref[(*place, low, near)] = real
                out_ref[(*place, low, beyond)] = imag
                out_ref[(*place, high, near)] = -imag
                out_ref[(*place, high, beyond)] = real

    shape = (blocks, 2 * dim, 4 * dim) if has_own else (blocks, 2, 2 * dim, 2 * dim)
    return pl.pallas_call(
        kernel,
        out_shape=jax.ShapeDtypeStruct(shape, jnp.float32),
        in_specs=[pl.BlockSpec(memory_space=pltpu.VMEM)],
        out_specs=pl.BlockSpec(memory_space=pltpu.VMEM),
        scratch_shapes=[pltpu.VMEM((4 * blocks * dim, dim), jnp.float32)],
        compiler_params=pltpu.CompilerParams(vmem_limit_bytes=8 * 2**20),
        cost_estimate=pl.CostEstimate(flops=10**5, bytes_accessed=10**5, transcendentals=0),
    )(flat)


def sweep_in_pairs(half, operator, dim, held):
    first, second, mate = pair_routes()

    def swap(block, sources):
        return lax.ppermute(block, axes, [(source, i) for i, source in enumerate(sources)])

    along_t_x = jnp.stack([operator[7] + operator[8], operator[1] + operator[2]])
    odd_level = lax.axis_index("gz") % 2 == 1
    along_z = jnp.stack(
        [jnp.where(odd_level, operator[5], operator[6]), jnp.where(odd_level, operator[6], operator[5])]
    )
    upper = lax.axis_index("gx") % 2 == 1
    mine = jnp.where(upper, along_z, along_t_x)
    theirs = swap(jnp.where(upper, along_t_x, along_z), mate)
    inside = real_blocks(jnp.stack([operator[0], operator[3] + operator[4]])[None], dim, True)[0]
    around = real_blocks(jnp.stack([mine, theirs]), dim, False)

    pair = jnp.stack([half, swap(half, mate)])
    for sweep_id in range(ITERS - 1):
        moved = [swap(pair, first), swap(pair, second)]
        kept = half + apply(jnp.concatenate([pair[0], pair[1]], 1), inside, lax.Precision.HIGH)
        if sweep_id == 1:
            rows, clover, kept = lax.optimization_barrier((*held[:2], kept))
            local, kept = lax.optimization_barrier((local_term(rows, clover), kept))
        if sweep_id == 2:
            stored, kept = lax.optimization_barrier((held[2], kept))
            vectors, kept = lax.optimization_barrier((hold(stored), kept))
        def along(link):
            return lax.dot_general(
                moved[link], around[:, link], (((2,), (2,)), ((0,), (0,))), precision=lax.Precision.HIGH
            )

        part = along(1) + (jnp.stack([kept, jnp.zeros_like(kept)]) + along(0))
        if sweep_id < ITERS - 2:
            other = swap(part, mate)
            pair = part + jnp.stack([other[1], other[0]])
    return (part[0], swap(part[1], mate)), vectors, local


def body(residual, null_vectors, clover_inverse, coarse_op, vector_count):
    rhs_count = residual.shape[0]
    vec_total = null_vectors.shape[1]
    coarse_dim = 2 * vec_total
    sites = residual.shape[3]
    rows = residual.transpose(0, 2, 1, 3)
    stored = null_vectors.transpose(0, 2, 1, 3)
    half, used = restrict(vector_count, rows, stored)

    coarse_op, half = lax.optimization_barrier((coarse_op, half))
    operator = coarse_op.reshape(9, 2, coarse_dim * coarse_dim)
    held = (rows, clover_inverse.transpose(0, 2, 3, 1, 4), stored)
    if shares_chip():
        summands, vectors, local = sweep_in_pairs(half, operator, coarse_dim, held)
    else:
        summands, vectors, local = sweep_alone(half, operator, coarse_dim, held)
    return extend(summands, used, vectors, local).transpose(0, 2, 1, 3)


def solution(mesh):
    in_specs = (
        P(None, None, None, ("gx", "gz", "ta")),
        P(None, None, None, ("gx", "gz", "ta")),
        P(None, None, None, None, ("gx", "gz", "ta")),
        P(("gx", "gz", "ta"), None, None, None),
        P(("gx", "gz", "ta")),
    )
    out_specs = P(None, None, None, ("gx", "gz", "ta"))
    return jax.shard_map(body, mesh=mesh, in_specs=in_specs, out_specs=out_specs, check_vma=False)
```

```python
import jax
import jax.numpy as jnp
from jax import lax
from jax.experimental import pallas as pl
from jax.experimental.pallas import tpu as pltpu
from jax.sharding import PartitionSpec as P

ITERS = 5


omega_step = 0.5
exact = lax.Precision.HIGHEST
axes = ("gx", "gz", "ta")


def routes():
    total = lax.axis_size("gx")
    plane_y = min(8, total // 2)
    plane_x = total // plane_y

    def ring(count):
        up = [(i + 1) % count for i in range(count)]
        down = [(i - 1) % count for i in range(count)]
        if count % 2:
            return up, down, False
        even = [(up if i % 2 == 0 else down)[i] for i in range(count)]
        odd = [(down if i % 2 == 0 else up)[i] for i in range(count)]
        return even, odd, True

    links = []
    first, second, paired = ring(plane_x)
    links.append(
        [("gx", tuple(way[g // plane_y] * plane_y + g % plane_y for g in range(total))) for way in (first, second)]
        + [paired, lax.axis_index("gx") // plane_y]
    )
    first, second, paired = ring(plane_y)
    links.append(
        [("gx", tuple((g // plane_y) * plane_y + way[g % plane_y] for g in range(total))) for way in (first, second)]
        + [paired, lax.axis_index("gx") % plane_y]
    )
    for axis in ("gz", "ta"):
        first, second, paired = ring(lax.axis_size(axis))
        links.append([(axis, tuple(first)), (axis, tuple(second)), paired, lax.axis_index(axis)])
    return links


def fetch(block, link):
    axis, sources = link
    return lax.ppermute(block, axis, [(source, i) for i, source in enumerate(sources)])


def restrict_kernel(
    count_ref, rows_hbm, vectors_hbm, out_ref, used_ref, rows_ref, vectors_ref, scratch, sems
):
    rhs, parts, _, sites = rows_ref.shape
    vecs = vectors_ref.shape[2]
    half = parts // 2
    copies = []
    for chi in range(2):
        span = pl.ds(half * chi, half)
        copies.append(
            [
                pltpu.make_async_copy(rows_hbm.at[:, span], rows_ref.at[:, span], sems.at[2 * chi]),
                pltpu.make_async_copy(vectors_hbm.at[:, span], vectors_ref.at[:, span], sems.at[2 * chi + 1]),
            ]
        )
    for copy in copies[0] + copies[1]:
        copy.start()
    for chi in range(2):
        for copy in copies[chi]:
            copy.wait()
        span = range(half * chi, half * chi + half)
        rows = jnp.concatenate([rows_ref[:, c].reshape(2 * rhs, sites) for c in span], 1)
        for part in range(2):
            vectors = jnp.concatenate([vectors_ref[part, c] for c in span], 1)
            scratch[chi, :, part * vecs : (part + 1) * vecs] = lax.dot_general(
                rows, vectors, (((1,), (1,)), ((), ())), preferred_element_type=jnp.float32
            )
    real, imag = [], []
    for chi in range(2):
        even = scratch[chi, pl.ds(0, rhs, stride=2), :]
        odd = scratch[chi, pl.ds(1, rhs, stride=2), :]
        real.append(even[:, :vecs] + odd[:, vecs : 2 * vecs])
        imag.append(odd[:, :vecs] - even[:, vecs : 2 * vecs])
    lane = lax.broadcasted_iota(jnp.int32, (rhs, vecs), 1)
    used = jnp.where(lane < count_ref[0], 1.0, 0.0)
    out_ref[...] = jnp.concatenate([omega_step * part * used for part in real + imag], 1)
    used_ref[...] = jnp.concatenate([used] * 4, 1)


def restrict(count, rows, vectors):
    rhs, vecs = rows.shape[0], vectors.shape[2]
    in_vmem = pl.BlockSpec(memory_space=pltpu.VMEM)
    in_hbm = pl.BlockSpec(memory_space=pltpu.HBM)
    return pl.pallas_call(
        restrict_kernel,
        out_shape=[jax.ShapeDtypeStruct((rhs, 4 * vecs), jnp.float32)] * 2,
        in_specs=[pl.BlockSpec(memory_space=pltpu.SMEM), in_hbm, in_hbm],
        out_specs=[in_vmem, in_vmem],
        scratch_shapes=[
            pltpu.VMEM(rows.shape, rows.dtype),
            pltpu.VMEM(vectors.shape, vectors.dtype),
            pltpu.VMEM((2, 2 * rhs, 128), jnp.float32),
            pltpu.SemaphoreType.DMA((4,)),
        ],
        compiler_params=pltpu.CompilerParams(vmem_limit_bytes=55168 * 2**10),
        cost_estimate=pl.CostEstimate(flops=10**7, bytes_accessed=5 * 10**5, transcendentals=0),
    )(count, rows, vectors)


def extend_kernel(first_ref, second_ref, used_ref, vectors_ref, local_ref, out_hbm, out_ref, scratch, sems):
    rhs, parts, _, sites = out_ref.shape
    vecs = vectors_ref.shape[1] // 2
    half = parts // 2
    coarse = (first_ref[...] + second_ref[...]) * used_ref[...]
    for chi in range(2):
        real = coarse[:, chi * vecs : (chi + 1) * vecs]
        imag = coarse[:, (2 + chi) * vecs : (3 + chi) * vecs]
        scratch[chi, pl.ds(0, rhs, stride=2), : 2 * vecs] = jnp.concatenate([real, -imag], 1)
        scratch[chi, pl.ds(1, rhs, stride=2), : 2 * vecs] = jnp.concatenate([imag, real], 1)
    copies = []
    step = half // 2
    for piece in range(4):
        weights = scratch[piece // 2, :, : 2 * vecs].astype(jnp.bfloat16)
        for c in range(step * piece, step * piece + step):
            lift = jnp.dot(weights, vectors_ref[c], preferred_element_type=jnp.float32)
            total = (local_ref[c] + lift).astype(jnp.bfloat16)
            out_ref[:, c] = total.reshape(rhs, 2, sites)
        span = pl.ds(step * piece, step)
        copies.append(pltpu.make_async_copy(out_ref.at[:, span], out_hbm.at[:, span], sems.at[piece]))
        copies[-1].start()
    for copy in copies:
        copy.wait()


small = pltpu.CompilerParams(vmem_limit_bytes=8 * 2**20)
in_vmem = pl.BlockSpec(memory_space=pltpu.VMEM)


def extend(summands, used, vectors, local):
    parts, _, sites = vectors.shape
    rhs = used.shape[0]
    shape = (rhs, parts, 2, sites)
    return pl.pallas_call(
        extend_kernel,
        out_shape=jax.ShapeDtypeStruct(shape, jnp.bfloat16),
        in_specs=[in_vmem] * 5,
        out_specs=pl.BlockSpec(memory_space=pltpu.HBM),
        scratch_shapes=[
            pltpu.VMEM(shape, jnp.bfloat16),
            pltpu.VMEM((2, 2 * rhs, 128), jnp.float32),
            pltpu.SemaphoreType.DMA((4,)),
        ],
        compiler_params=small,
        cost_estimate=pl.CostEstimate(flops=10**7, bytes_accessed=10**6, transcendentals=0),
    )(*summands, used, vectors, local)


def hold_kernel(vectors_ref, out_ref):
    vecs = vectors_ref.shape[2]
    for c in range(vectors_ref.shape[1]):
        out_ref[c] = jnp.concatenate([vectors_ref[0, c], vectors_ref[1, c]], 0)


def hold(vectors):
    _, parts, vecs, sites = vectors.shape
    return pl.pallas_call(
        hold_kernel,
        out_shape=jax.ShapeDtypeStruct((parts, 2 * vecs, sites), vectors.dtype),
        in_specs=[in_vmem],
        out_specs=in_vmem,
        compiler_params=small,
        cost_estimate=pl.CostEstimate(flops=10**5, bytes_accessed=10**5, transcendentals=0),
    )(vectors)


def local_kernel(rows_ref, clover_ref, out_ref):
    rhs, parts, _, sites = rows_ref.shape
    half = parts // 2
    row = lax.broadcasted_iota(jnp.int32, (2 * rhs, 2 * rhs), 0)
    col = lax.broadcasted_iota(jnp.int32, (2 * rhs, 2 * rhs), 1)
    turn = jnp.where((row % 2 == 0) & (col == row + 1), -1.0, 0.0)
    turn = jnp.where((row % 2 == 1) & (col == row - 1), 1.0, turn).astype(jnp.bfloat16)
    for chi in range(2):
        for start in range(0, sites, 128):
            lanes = slice(start, start + 128)
            plain, turned = [], []
            for b in range(half):
                rows = rows_ref[:, half * chi + b, :, lanes].reshape(2 * rhs, 128)
                plain.append(rows.astype(jnp.float32))
                turned.append(jnp.dot(turn, rows, preferred_element_type=jnp.float32))
            for a in range(half):
                total = jnp.zeros((2 * rhs, 128), jnp.float32)
                for b in range(half):
                    real = clover_ref[0, a, b, :, lanes].astype(jnp.float32)[chi : chi + 1]
                    imag = clover_ref[1, a, b, :, lanes].astype(jnp.float32)[chi : chi + 1]
                    total += real * plain[b] + imag * turned[b]
                out_ref[half * chi + a, :, lanes] = total


def local_term(rows, clover):
    rhs, parts, _, sites = rows.shape
    return pl.pallas_call(
        local_kernel,
        out_shape=jax.ShapeDtypeStruct((parts, 2 * rhs, sites), jnp.float32),
        in_specs=[in_vmem] * 2,
        out_specs=in_vmem,
        compiler_params=small,
        cost_estimate=pl.CostEstimate(flops=10**5, bytes_accessed=10**5, transcendentals=0),
    )(rows, clover)


def real_form(matrix, dim):
    matrix = matrix.reshape(2, dim, dim)
    upper = jnp.concatenate([matrix[0], -matrix[1]], 1)
    lower = jnp.concatenate([matrix[1], matrix[0]], 1)
    return omega_step * jnp.concatenate([upper, lower], 0)


def apply(vector, matrix, precision=exact):
    return lax.dot_general(vector, matrix, (((1,), (1,)), ((), ())), precision=precision)


def own_form(operator, dim):
    return jnp.eye(2 * dim, dtype=jnp.float32) - real_form(operator, dim)


def sweep_alone(half, operator, dim, held):
    grouped = {}
    for way, (first, second, paired, place) in enumerate(routes()):
        plus, minus = operator[2 * way + 1], operator[2 * way + 2]
        if first == second:
            grouped[first] = plus + minus
        else:
            swap = (place % 2 == 1) & paired
            grouped[first] = jnp.where(swap, minus, plus)
            grouped[second] = jnp.where(swap, plus, minus)

    def reach(link):
        axis, sources = link
        return ("gz", "ta", "gx").index(axis), -max(abs(source - i) for i, source in enumerate(sources))

    order = sorted(grouped, key=reach)
    own = own_form(operator[0], dim)
    around = jnp.concatenate([-real_form(grouped[link], dim) for link in order], 1)
    coarse = half
    for sweep_id in range(ITERS - 1):
        moved = [fetch(coarse, link) for link in order]
        kept = half + apply(coarse, own)
        if sweep_id == 1:
            rows, clover, kept = lax.optimization_barrier((*held[:2], kept))
            local, kept = lax.optimization_barrier((local_term(rows, clover), kept))
        if sweep_id == 2:
            stored, kept = lax.optimization_barrier((held[2], kept))
            vectors, kept = lax.optimization_barrier((hold(stored), kept))
        added = apply(jnp.concatenate(moved, 1), around)
        coarse = kept + added
    return (kept, added), vectors, local


def shares_chip():
    total, depth, slabs = (lax.axis_size(axis) for axis in axes)
    return total == 4 and depth == 4 and slabs == 2


def pair_routes():
    total, depth, slabs = (lax.axis_size(axis) for axis in axes)

    def device_at(group, level, slab):
        return (group * depth + level) * slabs + slab

    first, second, mate = [], [], []
    for group in range(total):
        for level in range(depth):
            for slab in range(slabs):
                step = 1 if level % 2 == 0 else -1
                if group % 2 == 0:
                    first.append(device_at(group, level, 1 - slab))
                    second.append(device_at(group ^ 2, level, slab))
                else:
                    first.append(device_at(group, (level - step) % depth, slab))
                    second.append(device_at(group, (level + step) % depth, slab))
                mate.append(device_at(group ^ 1, level, slab))
    return first, second, mate


def real_blocks(flat, dim, has_own):
    blocks = flat.shape[0]

    def kernel(flat_ref, out_ref, rows_ref):
        packed = jnp.concatenate([flat_ref[block, link] for block in range(blocks) for link in range(2)], 0)
        for i in range(dim):
            rows_ref[pl.ds(i, 4 * blocks, stride=dim), :] = packed[:, i * dim : (i + 1) * dim]
        row = lax.broadcasted_iota(jnp.int32, (dim, dim), 0)
        col = lax.broadcasted_iota(jnp.int32, (dim, dim), 1)
        for block in range(blocks):
            for link in range(2):
                base = (2 * block + link) * 2 * dim
                real = -omega_step * rows_ref[base : base + dim]
                imag = omega_step * rows_ref[base + dim : base + 2 * dim]
                if has_own and link == 0:
                    real = real + jnp.where(row == col, 1.0, 0.0)
                place, left = ((block,), 2 * dim * link) if has_own else ((block, link), 0)
                low, high = pl.ds(0, dim), pl.ds(dim, dim)
                near, beyond = pl.ds(left, dim), pl.ds(left + dim, dim)
                out_ref[(*place, low, near)] = real
                out_ref[(*place, low, beyond)] = imag
                out_ref[(*place, high, near)] = -imag
                out_ref[(*place, high, beyond)] = real

    shape = (blocks, 2 * dim, 4 * dim) if has_own else (blocks, 2, 2 * dim, 2 * dim)
    return pl.pallas_call(
        kernel,
        out_shape=jax.ShapeDtypeStruct(shape, jnp.float32),
        in_specs=[pl.BlockSpec(memory_space=pltpu.VMEM)],
        out_specs=pl.BlockSpec(memory_space=pltpu.VMEM),
        scratch_shapes=[pltpu.VMEM((4 * blocks * dim, dim), jnp.float32)],
        compiler_params=pltpu.CompilerParams(vmem_limit_bytes=8 * 2**20),
        cost_estimate=pl.CostEstimate(flops=10**5, bytes_accessed=10**5, transcendentals=0),
    )(flat)


def sweep_in_pairs(half, operator, dim, held):
    first, second, mate = pair_routes()

    def swap(block, sources):
        return lax.ppermute(block, axes, [(source, i) for i, source in enumerate(sources)])

    along_t_x = jnp.stack([operator[7] + operator[8], operator[1] + operator[2]])
    odd_level = lax.axis_index("gz") % 2 == 1
    along_z = jnp.stack(
        [jnp.where(odd_level, operator[5], operator[6]), jnp.where(odd_level, operator[6], operator[5])]
    )
    upper = lax.axis_index("gx") % 2 == 1
    mine = jnp.where(upper, along_z, along_t_x)
    theirs = swap(jnp.where(upper, along_t_x, along_z), mate)
    inside = real_blocks(jnp.stack([operator[0], operator[3] + operator[4]])[None], dim, True)[0]
    around = real_blocks(jnp.stack([mine, theirs]), dim, False)

    pair = jnp.stack([half, swap(half, mate)])
    for sweep_id in range(ITERS - 1):
        moved = [swap(pair, first), swap(pair, second)]
        kept = half + apply(jnp.concatenate([pair[0], pair[1]], 1), inside, lax.Precision.HIGH)
        if sweep_id == 1:
            rows, clover, kept = lax.optimization_barrier((*held[:2], kept))
            local, kept = lax.optimization_barrier((local_term(rows, clover), kept))
        if sweep_id == 2:
            stored, kept = lax.optimization_barrier((held[2], kept))
            vectors, kept = lax.optimization_barrier((hold(stored), kept))
        def along(link):
            return lax.dot_general(
                moved[link], around[:, link], (((2,), (2,)), ((0,), (0,))), precision=lax.Precision.HIGH
            )

        part = along(1) + (jnp.stack([kept, jnp.zeros_like(kept)]) + along(0))
        if sweep_id < ITERS - 2:
            other = swap(part, mate)
            pair = part + jnp.stack([other[1], other[0]])
    return (part[0], swap(part[1], mate)), vectors, local


def body(residual, null_vectors, clover_inverse, coarse_op, vector_count):
    rhs_count = residual.shape[0]
    vec_total = null_vectors.shape[1]
    coarse_dim = 2 * vec_total
    sites = residual.shape[3]
    rows = residual.transpose(0, 2, 1, 3)
    stored = null_vectors.transpose(0, 2, 1, 3)
    half, used = restrict(vector_count, rows, stored)

    coarse_op, half = lax.optimization_barrier((coarse_op, half))
    operator = coarse_op.reshape(9, 2, coarse_dim * coarse_dim)
    held = (rows, clover_inverse.transpose(0, 2, 3, 1, 4), stored)
    if shares_chip():
        summands, vectors, local = sweep_in_pairs(half, operator, coarse_dim, held)
    else:
        summands, vectors, local = sweep_alone(half, operator, coarse_dim, held)
    return extend(summands, used, vectors, local).transpose(0, 2, 1, 3)


def solution(mesh):
    in_specs = (
        P(None, None, None, ("gx", "gz", "ta")),
        P(None, None, None, ("gx", "gz", "ta")),
        P(None, None, None, None, ("gx", "gz", "ta")),
        P(("gx", "gz", "ta"), None, None, None),
        P(("gx", "gz", "ta")),
    )
    out_specs = P(None, None, None, ("gx", "gz", "ta"))
    return jax.shard_map(body, mesh=mesh, in_specs=in_specs, out_specs=out_specs, check_vma=False)
```

```python
import jax
import jax.numpy as jnp
from jax import lax
from jax.experimental import pallas as pl
from jax.experimental.pallas import tpu as pltpu
from jax.sharding import PartitionSpec as P

ITERS = 5


omega_step = 0.5
exact = lax.Precision.HIGHEST
axes = ("gx", "gz", "ta")


def routes():
    total = lax.axis_size("gx")
    plane_y = min(8, total // 2)
    plane_x = total // plane_y

    def ring(count):
        up = [(i + 1) % count for i in range(count)]
        down = [(i - 1) % count for i in range(count)]
        if count % 2:
            return up, down, False
        even = [(up if i % 2 == 0 else down)[i] for i in range(count)]
        odd = [(down if i % 2 == 0 else up)[i] for i in range(count)]
        return even, odd, True

    links = []
    first, second, paired = ring(plane_x)
    links.append(
        [("gx", tuple(way[g // plane_y] * plane_y + g % plane_y for g in range(total))) for way in (first, second)]
        + [paired, lax.axis_index("gx") // plane_y]
    )
    first, second, paired = ring(plane_y)
    links.append(
        [("gx", tuple((g // plane_y) * plane_y + way[g % plane_y] for g in range(total))) for way in (first, second)]
        + [paired, lax.axis_index("gx") % plane_y]
    )
    for axis in ("gz", "ta"):
        first, second, paired = ring(lax.axis_size(axis))
        links.append([(axis, tuple(first)), (axis, tuple(second)), paired, lax.axis_index(axis)])
    return links


def fetch(block, link):
    axis, sources = link
    return lax.ppermute(block, axis, [(source, i) for i, source in enumerate(sources)])


def restrict_kernel(
    count_ref, rows_hbm, vectors_hbm, out_ref, used_ref, rows_ref, vectors_ref, scratch, sems
):
    rhs, parts, _, sites = rows_ref.shape
    vecs = vectors_ref.shape[2]
    half = parts // 2
    copies = [pltpu.make_async_copy(rows_hbm, rows_ref, sems.at[2])]
    for part in range(2):
        copies.append(pltpu.make_async_copy(vectors_hbm.at[part], vectors_ref.at[part], sems.at[part]))
    for copy in copies:
        copy.start()
    copies[0].wait()
    for part in range(2):
        copies[1 + part].wait()
        for chi in range(2):
            total = jnp.zeros((2 * rhs, vecs), jnp.float32)
            for c in range(half * chi, half * chi + half):
                rows = rows_ref[:, c].reshape(2 * rhs, sites)
                total += lax.dot_general(
                    rows, vectors_ref[part, c], (((1,), (1,)), ((), ())), preferred_element_type=jnp.float32
                )
            scratch[chi, :, part * vecs : (part + 1) * vecs] = total
    real, imag = [], []
    for chi in range(2):
        even = scratch[chi, pl.ds(0, rhs, stride=2), :]
        odd = scratch[chi, pl.ds(1, rhs, stride=2), :]
        real.append(even[:, :vecs] + odd[:, vecs : 2 * vecs])
        imag.append(odd[:, :vecs] - even[:, vecs : 2 * vecs])
    lane = lax.broadcasted_iota(jnp.int32, (rhs, vecs), 1)
    used = jnp.where(lane < count_ref[0], 1.0, 0.0)
    out_ref[...] = jnp.concatenate([omega_step * part * used for part in real + imag], 1)
    used_ref[...] = jnp.concatenate([used] * 4, 1)


def restrict(count, rows, vectors):
    rhs, vecs = rows.shape[0], vectors.shape[2]
    in_vmem = pl.BlockSpec(memory_space=pltpu.VMEM)
    in_hbm = pl.BlockSpec(memory_space=pltpu.HBM)
    return pl.pallas_call(
        restrict_kernel,
        out_shape=[jax.ShapeDtypeStruct((rhs, 4 * vecs), jnp.float32)] * 2,
        in_specs=[pl.BlockSpec(memory_space=pltpu.SMEM), in_hbm, in_hbm],
        out_specs=[in_vmem, in_vmem],
        scratch_shapes=[
            pltpu.VMEM(rows.shape, rows.dtype),
            pltpu.VMEM(vectors.shape, vectors.dtype),
            pltpu.VMEM((2, 2 * rhs, 128), jnp.float32),
            pltpu.SemaphoreType.DMA((3,)),
        ],
        compiler_params=pltpu.CompilerParams(vmem_limit_bytes=55168 * 2**10),
        cost_estimate=pl.CostEstimate(flops=10**7, bytes_accessed=5 * 10**5, transcendentals=0),
    )(count, rows, vectors)


def extend_kernel(first_ref, second_ref, used_ref, vectors_ref, local_ref, out_hbm, out_ref, scratch, sems):
    rhs, parts, _, sites = out_ref.shape
    vecs = vectors_ref.shape[1] // 2
    half = parts // 2
    coarse = (first_ref[...] + second_ref[...]) * used_ref[...]
    for chi in range(2):
        real = coarse[:, chi * vecs : (chi + 1) * vecs]
        imag = coarse[:, (2 + chi) * vecs : (3 + chi) * vecs]
        scratch[chi, pl.ds(0, rhs, stride=2), : 2 * vecs] = jnp.concatenate([real, -imag], 1)
        scratch[chi, pl.ds(1, rhs, stride=2), : 2 * vecs] = jnp.concatenate([imag, real], 1)
    copies = []
    step = half // 2
    for piece in range(4):
        weights = scratch[piece // 2, :, : 2 * vecs].astype(jnp.bfloat16)
        for c in range(step * piece, step * piece + step):
            lift = jnp.dot(weights, vectors_ref[c], preferred_element_type=jnp.float32)
            total = (local_ref[c] + lift).astype(jnp.bfloat16)
            out_ref[:, c] = total.reshape(rhs, 2, sites)
        span = pl.ds(step * piece, step)
        copies.append(pltpu.make_async_copy(out_ref.at[:, span], out_hbm.at[:, span], sems.at[piece]))
        copies[-1].start()
    for copy in copies:
        copy.wait()


small = pltpu.CompilerParams(vmem_limit_bytes=8 * 2**20)
in_vmem = pl.BlockSpec(memory_space=pltpu.VMEM)


def extend(summands, used, vectors, local):
    parts, _, sites = vectors.shape
    rhs = used.shape[0]
    shape = (rhs, parts, 2, sites)
    return pl.pallas_call(
        extend_kernel,
        out_shape=jax.ShapeDtypeStruct(shape, jnp.bfloat16),
        in_specs=[in_vmem] * 5,
        out_specs=pl.BlockSpec(memory_space=pltpu.HBM),
        scratch_shapes=[
            pltpu.VMEM(shape, jnp.bfloat16),
            pltpu.VMEM((2, 2 * rhs, 128), jnp.float32),
            pltpu.SemaphoreType.DMA((4,)),
        ],
        compiler_params=small,
        cost_estimate=pl.CostEstimate(flops=10**7, bytes_accessed=10**6, transcendentals=0),
    )(*summands, used, vectors, local)


def hold_kernel(vectors_ref, out_ref):
    vecs = vectors_ref.shape[2]
    for c in range(vectors_ref.shape[1]):
        out_ref[c] = jnp.concatenate([vectors_ref[0, c], vectors_ref[1, c]], 0)


def hold(vectors):
    _, parts, vecs, sites = vectors.shape
    return pl.pallas_call(
        hold_kernel,
        out_shape=jax.ShapeDtypeStruct((parts, 2 * vecs, sites), vectors.dtype),
        in_specs=[in_vmem],
        out_specs=in_vmem,
        compiler_params=small,
        cost_estimate=pl.CostEstimate(flops=10**5, bytes_accessed=10**5, transcendentals=0),
    )(vectors)


def local_kernel(rows_ref, clover_ref, out_ref):
    rhs, parts, _, sites = rows_ref.shape
    half = parts // 2
    row = lax.broadcasted_iota(jnp.int32, (2 * rhs, 2 * rhs), 0)
    col = lax.broadcasted_iota(jnp.int32, (2 * rhs, 2 * rhs), 1)
    turn = jnp.where((row % 2 == 0) & (col == row + 1), -1.0, 0.0)
    turn = jnp.where((row % 2 == 1) & (col == row - 1), 1.0, turn).astype(jnp.bfloat16)
    for chi in range(2):
        for start in range(0, sites, 128):
            lanes = slice(start, start + 128)
            plain, turned = [], []
            for b in range(half):
                rows = rows_ref[:, half * chi + b, :, lanes].reshape(2 * rhs, 128)
                plain.append(rows.astype(jnp.float32))
                turned.append(jnp.dot(turn, rows, preferred_element_type=jnp.float32))
            for a in range(half):
                total = jnp.zeros((2 * rhs, 128), jnp.float32)
                for b in range(half):
                    real = clover_ref[0, a, b, :, lanes].astype(jnp.float32)[chi : chi + 1]
                    imag = clover_ref[1, a, b, :, lanes].astype(jnp.float32)[chi : chi + 1]
                    total += real * plain[b] + imag * turned[b]
                out_ref[half * chi + a, :, lanes] = total


def local_term(rows, clover):
    rhs, parts, _, sites = rows.shape
    return pl.pallas_call(
        local_kernel,
        out_shape=jax.ShapeDtypeStruct((parts, 2 * rhs, sites), jnp.float32),
        in_specs=[in_vmem] * 2,
        out_specs=in_vmem,
        compiler_params=small,
        cost_estimate=pl.CostEstimate(flops=10**5, bytes_accessed=10**5, transcendentals=0),
    )(rows, clover)


def real_form(matrix, dim):
    matrix = matrix.reshape(2, dim, dim)
    upper = jnp.concatenate([matrix[0], -matrix[1]], 1)
    lower = jnp.concatenate([matrix[1], matrix[0]], 1)
    return omega_step * jnp.concatenate([upper, lower], 0)


def apply(vector, matrix, precision=exact):
    return lax.dot_general(vector, matrix, (((1,), (1,)), ((), ())), precision=precision)


def own_form(operator, dim):
    return jnp.eye(2 * dim, dtype=jnp.float32) - real_form(operator, dim)


def sweep_alone(half, operator, dim, held):
    grouped = {}
    for way, (first, second, paired, place) in enumerate(routes()):
        plus, minus = operator[2 * way + 1], operator[2 * way + 2]
        if first == second:
            grouped[first] = plus + minus
        else:
            swap = (place % 2 == 1) & paired
            grouped[first] = jnp.where(swap, minus, plus)
            grouped[second] = jnp.where(swap, plus, minus)

    def reach(link):
        axis, sources = link
        return ("gz", "ta", "gx").index(axis), -max(abs(source - i) for i, source in enumerate(sources))

    order = sorted(grouped, key=reach)
    own = own_form(operator[0], dim)
    around = jnp.concatenate([-real_form(grouped[link], dim) for link in order], 1)
    coarse = half
    for sweep_id in range(ITERS - 1):
        moved = [fetch(coarse, link) for link in order]
        kept = half + apply(coarse, own)
        if sweep_id == 1:
            rows, clover, kept = lax.optimization_barrier((*held[:2], kept))
            local, kept = lax.optimization_barrier((local_term(rows, clover), kept))
        if sweep_id == 2:
            stored, kept = lax.optimization_barrier((held[2], kept))
            vectors, kept = lax.optimization_barrier((hold(stored), kept))
        added = apply(jnp.concatenate(moved, 1), around)
        coarse = kept + added
    return (kept, added), vectors, local


def shares_chip():
    total, depth, slabs = (lax.axis_size(axis) for axis in axes)
    return total == 4 and depth == 4 and slabs == 2


def pair_routes():
    total, depth, slabs = (lax.axis_size(axis) for axis in axes)

    def device_at(group, level, slab):
        return (group * depth + level) * slabs + slab

    first, second, mate = [], [], []
    for group in range(total):
        for level in range(depth):
            for slab in range(slabs):
                step = 1 if level % 2 == 0 else -1
                if group % 2 == 0:
                    first.append(device_at(group, level, 1 - slab))
                    second.append(device_at(group ^ 2, level, slab))
                else:
                    first.append(device_at(group, (level - step) % depth, slab))
                    second.append(device_at(group, (level + step) % depth, slab))
                mate.append(device_at(group ^ 1, level, slab))
    return first, second, mate


def real_blocks(flat, dim, has_own):
    blocks = flat.shape[0]

    def kernel(flat_ref, out_ref, rows_ref):
        packed = jnp.concatenate([flat_ref[block, link] for block in range(blocks) for link in range(2)], 0)
        for i in range(dim):
            rows_ref[pl.ds(i, 4 * blocks, stride=dim), :] = packed[:, i * dim : (i + 1) * dim]
        row = lax.broadcasted_iota(jnp.int32, (dim, dim), 0)
        col = lax.broadcasted_iota(jnp.int32, (dim, dim), 1)
        for block in range(blocks):
            for link in range(2):
                base = (2 * block + link) * 2 * dim
                real = -omega_step * rows_ref[base : base + dim]
                imag = omega_step * rows_ref[base + dim : base + 2 * dim]
                if has_own and link == 0:
                    real = real + jnp.where(row == col, 1.0, 0.0)
                place, left = ((block,), 2 * dim * link) if has_own else ((block, link), 0)
                low, high = pl.ds(0, dim), pl.ds(dim, dim)
                near, beyond = pl.ds(left, dim), pl.ds(left + dim, dim)
                out_ref[(*place, low, near)] = real
                out_ref[(*place, low, beyond)] = imag
                out_ref[(*place, high, near)] = -imag
                out_ref[(*place, high, beyond)] = real

    shape = (blocks, 2 * dim, 4 * dim) if has_own else (blocks, 2, 2 * dim, 2 * dim)
    return pl.pallas_call(
        kernel,
        out_shape=jax.ShapeDtypeStruct(shape, jnp.float32),
        in_specs=[pl.BlockSpec(memory_space=pltpu.VMEM)],
        out_specs=pl.BlockSpec(memory_space=pltpu.VMEM),
        scratch_shapes=[pltpu.VMEM((4 * blocks * dim, dim), jnp.float32)],
        compiler_params=pltpu.CompilerParams(vmem_limit_bytes=8 * 2**20),
        cost_estimate=pl.CostEstimate(flops=10**5, bytes_accessed=10**5, transcendentals=0),
    )(flat)


def sweep_in_pairs(half, operator, dim, held):
    first, second, mate = pair_routes()

    def swap(block, sources):
        return lax.ppermute(block, axes, [(source, i) for i, source in enumerate(sources)])

    along_t_x = jnp.stack([operator[7] + operator[8], operator[1] + operator[2]])
    odd_level = lax.axis_index("gz") % 2 == 1
    along_z = jnp.stack(
        [jnp.where(odd_level, operator[5], operator[6]), jnp.where(odd_level, operator[6], operator[5])]
    )
    upper = lax.axis_index("gx") % 2 == 1
    mine = jnp.where(upper, along_z, along_t_x)
    theirs = swap(jnp.where(upper, along_t_x, along_z), mate)
    inside = real_blocks(jnp.stack([operator[0], operator[3] + operator[4]])[None], dim, True)[0]
    around = real_blocks(jnp.stack([mine, theirs]), dim, False)

    pair = jnp.stack([half, swap(half, mate)])
    for sweep_id in range(ITERS - 1):
        moved = [swap(pair, first), swap(pair, second)]
        kept = half + apply(jnp.concatenate([pair[0], pair[1]], 1), inside, lax.Precision.HIGH)
        if sweep_id == 1:
            rows, clover, kept = lax.optimization_barrier((*held[:2], kept))
            local, kept = lax.optimization_barrier((local_term(rows, clover), kept))
        if sweep_id == 2:
            stored, kept = lax.optimization_barrier((held[2], kept))
            vectors, kept = lax.optimization_barrier((hold(stored), kept))
        def along(link):
            return lax.dot_general(
                moved[link], around[:, link], (((2,), (2,)), ((0,), (0,))), precision=lax.Precision.HIGH
            )

        part = along(1) + (jnp.stack([kept, jnp.zeros_like(kept)]) + along(0))
        if sweep_id < ITERS - 2:
            other = swap(part, mate)
            pair = part + jnp.stack([other[1], other[0]])
    return (part[0], swap(part[1], mate)), vectors, local


def body(residual, null_vectors, clover_inverse, coarse_op, vector_count):
    rhs_count = residual.shape[0]
    vec_total = null_vectors.shape[1]
    coarse_dim = 2 * vec_total
    sites = residual.shape[3]
    rows = residual.transpose(0, 2, 1, 3)
    stored = null_vectors.transpose(0, 2, 1, 3)
    half, used = restrict(vector_count, rows, stored)

    coarse_op, half = lax.optimization_barrier((coarse_op, half))
    operator = coarse_op.reshape(9, 2, coarse_dim * coarse_dim)
    held = (rows, clover_inverse.transpose(0, 2, 3, 1, 4), stored)
    if shares_chip():
        summands, vectors, local = sweep_in_pairs(half, operator, coarse_dim, held)
    else:
        summands, vectors, local = sweep_alone(half, operator, coarse_dim, held)
    return extend(summands, used, vectors, local).transpose(0, 2, 1, 3)


def solution(mesh):
    in_specs = (
        P(None, None, None, ("gx", "gz", "ta")),
        P(None, None, None, ("gx", "gz", "ta")),
        P(None, None, None, None, ("gx", "gz", "ta")),
        P(("gx", "gz", "ta"), None, None, None),
        P(("gx", "gz", "ta")),
    )
    out_specs = P(None, None, None, ("gx", "gz", "ta"))
    return jax.shard_map(body, mesh=mesh, in_specs=in_specs, out_specs=out_specs, check_vma=False)
```

```python
import jax
import jax.numpy as jnp
from jax import lax
from jax.experimental import pallas as pl
from jax.experimental.pallas import tpu as pltpu
from jax.sharding import PartitionSpec as P

ITERS = 5


omega_step = 0.5
exact = lax.Precision.HIGHEST
axes = ("gx", "gz", "ta")


def routes():
    total = lax.axis_size("gx")
    plane_y = min(8, total // 2)
    plane_x = total // plane_y

    def ring(count):
        up = [(i + 1) % count for i in range(count)]
        down = [(i - 1) % count for i in range(count)]
        if count % 2:
            return up, down, False
        even = [(up if i % 2 == 0 else down)[i] for i in range(count)]
        odd = [(down if i % 2 == 0 else up)[i] for i in range(count)]
        return even, odd, True

    links = []
    first, second, paired = ring(plane_x)
    links.append(
        [("gx", tuple(way[g // plane_y] * plane_y + g % plane_y for g in range(total))) for way in (first, second)]
        + [paired, lax.axis_index("gx") // plane_y]
    )
    first, second, paired = ring(plane_y)
    links.append(
        [("gx", tuple((g // plane_y) * plane_y + way[g % plane_y] for g in range(total))) for way in (first, second)]
        + [paired, lax.axis_index("gx") % plane_y]
    )
    for axis in ("gz", "ta"):
        first, second, paired = ring(lax.axis_size(axis))
        links.append([(axis, tuple(first)), (axis, tuple(second)), paired, lax.axis_index(axis)])
    return links


def fetch(block, link):
    axis, sources = link
    return lax.ppermute(block, axis, [(source, i) for i, source in enumerate(sources)])


def restrict_kernel(
    count_ref, rows_hbm, vectors_hbm, out_ref, used_ref, rows_ref, vectors_ref, scratch, sems
):
    rhs, parts, _, sites = rows_ref.shape
    vecs = vectors_ref.shape[2]
    half = parts // 2
    copies = []
    for chi in range(2):
        span = pl.ds(half * chi, half)
        copies.append(
            [
                pltpu.make_async_copy(rows_hbm.at[:, span], rows_ref.at[:, span], sems.at[2 * chi]),
                pltpu.make_async_copy(vectors_hbm.at[:, span], vectors_ref.at[:, span], sems.at[2 * chi + 1]),
            ]
        )
    for copy in copies[0] + copies[1]:
        copy.start()
    for chi in range(2):
        for copy in copies[chi]:
            copy.wait()
        total = jnp.zeros((2 * rhs, 2 * vecs), jnp.float32)
        for c in range(half * chi, half * chi + half):
            rows = rows_ref[:, c].reshape(2 * rhs, sites)
            vectors = jnp.concatenate([vectors_ref[0, c], vectors_ref[1, c]], 0)
            total += lax.dot_general(
                rows, vectors, (((1,), (1,)), ((), ())), preferred_element_type=jnp.float32
            )
        scratch[chi, :, : 2 * vecs] = total
    real, imag = [], []
    for chi in range(2):
        even = scratch[chi, pl.ds(0, rhs, stride=2), :]
        odd = scratch[chi, pl.ds(1, rhs, stride=2), :]
        real.append(even[:, :vecs] + odd[:, vecs : 2 * vecs])
        imag.append(odd[:, :vecs] - even[:, vecs : 2 * vecs])
    lane = lax.broadcasted_iota(jnp.int32, (rhs, vecs), 1)
    used = jnp.where(lane < count_ref[0], 1.0, 0.0)
    out_ref[...] = jnp.concatenate([omega_step * part * used for part in real + imag], 1)
    used_ref[...] = jnp.concatenate([used] * 4, 1)


def restrict(count, rows, vectors):
    rhs, vecs = rows.shape[0], vectors.shape[2]
    in_vmem = pl.BlockSpec(memory_space=pltpu.VMEM)
    in_hbm = pl.BlockSpec(memory_space=pltpu.HBM)
    return pl.pallas_call(
        restrict_kernel,
        out_shape=[jax.ShapeDtypeStruct((rhs, 4 * vecs), jnp.float32)] * 2,
        in_specs=[pl.BlockSpec(memory_space=pltpu.SMEM), in_hbm, in_hbm],
        out_specs=[in_vmem, in_vmem],
        scratch_shapes=[
            pltpu.VMEM(rows.shape, rows.dtype),
            pltpu.VMEM(vectors.shape, vectors.dtype),
            pltpu.VMEM((2, 2 * rhs, 128), jnp.float32),
            pltpu.SemaphoreType.DMA((4,)),
        ],
        compiler_params=pltpu.CompilerParams(vmem_limit_bytes=55168 * 2**10),
        cost_estimate=pl.CostEstimate(flops=10**7, bytes_accessed=5 * 10**5, transcendentals=0),
    )(count, rows, vectors)


def extend_kernel(first_ref, second_ref, used_ref, vectors_ref, local_ref, out_hbm, out_ref, scratch, sems):
    rhs, parts, _, sites = out_ref.shape
    vecs = vectors_ref.shape[1] // 2
    half = parts // 2
    coarse = (first_ref[...] + second_ref[...]) * used_ref[...]
    for chi in range(2):
        real = coarse[:, chi * vecs : (chi + 1) * vecs]
        imag = coarse[:, (2 + chi) * vecs : (3 + chi) * vecs]
        scratch[chi, pl.ds(0, rhs, stride=2), : 2 * vecs] = jnp.concatenate([real, -imag], 1)
        scratch[chi, pl.ds(1, rhs, stride=2), : 2 * vecs] = jnp.concatenate([imag, real], 1)
    copies = []
    step = half // 2
    for piece in range(4):
        weights = scratch[piece // 2, :, : 2 * vecs].astype(jnp.bfloat16)
        for c in range(step * piece, step * piece + step):
            lift = jnp.dot(weights, vectors_ref[c], preferred_element_type=jnp.float32)
            total = (local_ref[c] + lift).astype(jnp.bfloat16)
            out_ref[:, c] = total.reshape(rhs, 2, sites)
        span = pl.ds(step * piece, step)
        copies.append(pltpu.make_async_copy(out_ref.at[:, span], out_hbm.at[:, span], sems.at[piece]))
        copies[-1].start()
    for copy in copies:
        copy.wait()


small = pltpu.CompilerParams(vmem_limit_bytes=8 * 2**20)
in_vmem = pl.BlockSpec(memory_space=pltpu.VMEM)


def extend(summands, used, vectors, local):
    parts, _, sites = vectors.shape
    rhs = used.shape[0]
    shape = (rhs, parts, 2, sites)
    return pl.pallas_call(
        extend_kernel,
        out_shape=jax.ShapeDtypeStruct(shape, jnp.bfloat16),
        in_specs=[in_vmem] * 5,
        out_specs=pl.BlockSpec(memory_space=pltpu.HBM),
        scratch_shapes=[
            pltpu.VMEM(shape, jnp.bfloat16),
            pltpu.VMEM((2, 2 * rhs, 128), jnp.float32),
            pltpu.SemaphoreType.DMA((4,)),
        ],
        compiler_params=small,
        cost_estimate=pl.CostEstimate(flops=10**7, bytes_accessed=10**6, transcendentals=0),
    )(*summands, used, vectors, local)


def hold_kernel(vectors_ref, out_ref):
    vecs = vectors_ref.shape[2]
    for c in range(vectors_ref.shape[1]):
        out_ref[c] = jnp.concatenate([vectors_ref[0, c], vectors_ref[1, c]], 0)


def hold(vectors):
    _, parts, vecs, sites = vectors.shape
    return pl.pallas_call(
        hold_kernel,
        out_shape=jax.ShapeDtypeStruct((parts, 2 * vecs, sites), vectors.dtype),
        in_specs=[in_vmem],
        out_specs=in_vmem,
        compiler_params=small,
        cost_estimate=pl.CostEstimate(flops=10**5, bytes_accessed=10**5, transcendentals=0),
    )(vectors)


def local_kernel(rows_ref, clover_ref, out_ref):
    rhs, parts, _, sites = rows_ref.shape
    half = parts // 2
    row = lax.broadcasted_iota(jnp.int32, (2 * rhs, 2 * rhs), 0)
    col = lax.broadcasted_iota(jnp.int32, (2 * rhs, 2 * rhs), 1)
    turn = jnp.where((row % 2 == 0) & (col == row + 1), -1.0, 0.0)
    turn = jnp.where((row % 2 == 1) & (col == row - 1), 1.0, turn).astype(jnp.bfloat16)
    for chi in range(2):
        for start in range(0, sites, 128):
            lanes = slice(start, start + 128)
            plain, turned = [], []
            for b in range(half):
                rows = rows_ref[:, half * chi + b, :, lanes].reshape(2 * rhs, 128)
                plain.append(rows.astype(jnp.float32))
                turned.append(jnp.dot(turn, rows, preferred_element_type=jnp.float32))
            for a in range(half):
                total = jnp.zeros((2 * rhs, 128), jnp.float32)
                for b in range(half):
                    real = clover_ref[0, a, b, :, lanes].astype(jnp.float32)[chi : chi + 1]
                    imag = clover_ref[1, a, b, :, lanes].astype(jnp.float32)[chi : chi + 1]
                    total += real * plain[b] + imag * turned[b]
                out_ref[half * chi + a, :, lanes] = total


def local_term(rows, clover):
    rhs, parts, _, sites = rows.shape
    return pl.pallas_call(
        local_kernel,
        out_shape=jax.ShapeDtypeStruct((parts, 2 * rhs, sites), jnp.float32),
        in_specs=[in_vmem] * 2,
        out_specs=in_vmem,
        compiler_params=small,
        cost_estimate=pl.CostEstimate(flops=10**5, bytes_accessed=10**5, transcendentals=0),
    )(rows, clover)


def real_form(matrix, dim):
    matrix = matrix.reshape(2, dim, dim)
    upper = jnp.concatenate([matrix[0], -matrix[1]], 1)
    lower = jnp.concatenate([matrix[1], matrix[0]], 1)
    return omega_step * jnp.concatenate([upper, lower], 0)


def apply(vector, matrix, precision=exact):
    return lax.dot_general(vector, matrix, (((1,), (1,)), ((), ())), precision=precision)


def own_form(operator, dim):
    return jnp.eye(2 * dim, dtype=jnp.float32) - real_form(operator, dim)


def sweep_alone(half, operator, dim, held):
    grouped = {}
    for way, (first, second, paired, place) in enumerate(routes()):
        plus, minus = operator[2 * way + 1], operator[2 * way + 2]
        if first == second:
            grouped[first] = plus + minus
        else:
            swap = (place % 2 == 1) & paired
            grouped[first] = jnp.where(swap, minus, plus)
            grouped[second] = jnp.where(swap, plus, minus)

    def reach(link):
        axis, sources = link
        return ("gz", "ta", "gx").index(axis), -max(abs(source - i) for i, source in enumerate(sources))

    order = sorted(grouped, key=reach)
    own = own_form(operator[0], dim)
    around = jnp.concatenate([-real_form(grouped[link], dim) for link in order], 1)
    coarse = half
    for sweep_id in range(ITERS - 1):
        moved = [fetch(coarse, link) for link in order]
        kept = half + apply(coarse, own)
        if sweep_id == 1:
            rows, clover, kept = lax.optimization_barrier((*held[:2], kept))
            local, kept = lax.optimization_barrier((local_term(rows, clover), kept))
        if sweep_id == 2:
            stored, kept = lax.optimization_barrier((held[2], kept))
            vectors, kept = lax.optimization_barrier((hold(stored), kept))
        added = apply(jnp.concatenate(moved, 1), around)
        coarse = kept + added
    return (kept, added), vectors, local


def shares_chip():
    total, depth, slabs = (lax.axis_size(axis) for axis in axes)
    return total == 4 and depth == 4 and slabs == 2


def pair_routes():
    total, depth, slabs = (lax.axis_size(axis) for axis in axes)

    def device_at(group, level, slab):
        return (group * depth + level) * slabs + slab

    first, second, mate = [], [], []
    for group in range(total):
        for level in range(depth):
            for slab in range(slabs):
                step = 1 if level % 2 == 0 else -1
                if group % 2 == 0:
                    first.append(device_at(group, level, 1 - slab))
                    second.append(device_at(group ^ 2, level, slab))
                else:
                    first.append(device_at(group, (level - step) % depth, slab))
                    second.append(device_at(group, (level + step) % depth, slab))
                mate.append(device_at(group ^ 1, level, slab))
    return first, second, mate


def real_blocks(flat, dim, has_own):
    blocks = flat.shape[0]

    def kernel(flat_ref, out_ref, rows_ref):
        packed = jnp.concatenate([flat_ref[block, link] for block in range(blocks) for link in range(2)], 0)
        for i in range(dim):
            rows_ref[pl.ds(i, 4 * blocks, stride=dim), :] = packed[:, i * dim : (i + 1) * dim]
        row = lax.broadcasted_iota(jnp.int32, (dim, dim), 0)
        col = lax.broadcasted_iota(jnp.int32, (dim, dim), 1)
        for block in range(blocks):
            for link in range(2):
                base = (2 * block + link) * 2 * dim
                real = -omega_step * rows_ref[base : base + dim]
                imag = omega_step * rows_ref[base + dim : base + 2 * dim]
                if has_own and link == 0:
                    real = real + jnp.where(row == col, 1.0, 0.0)
                place, left = ((block,), 2 * dim * link) if has_own else ((block, link), 0)
                low, high = pl.ds(0, dim), pl.ds(dim, dim)
                near, beyond = pl.ds(left, dim), pl.ds(left + dim, dim)
                out_ref[(*place, low, near)] = real
                out_ref[(*place, low, beyond)] = imag
                out_ref[(*place, high, near)] = -imag
                out_ref[(*place, high, beyond)] = real

    shape = (blocks, 2 * dim, 4 * dim) if has_own else (blocks, 2, 2 * dim, 2 * dim)
    return pl.pallas_call(
        kernel,
        out_shape=jax.ShapeDtypeStruct(shape, jnp.float32),
        in_specs=[pl.BlockSpec(memory_space=pltpu.VMEM)],
        out_specs=pl.BlockSpec(memory_space=pltpu.VMEM),
        scratch_shapes=[pltpu.VMEM((4 * blocks * dim, dim), jnp.float32)],
        compiler_params=pltpu.CompilerParams(vmem_limit_bytes=8 * 2**20),
        cost_estimate=pl.CostEstimate(flops=10**5, bytes_accessed=10**5, transcendentals=0),
    )(flat)


def sweep_in_pairs(half, operator, dim, held):
    first, second, mate = pair_routes()

    def swap(block, sources):
        return lax.ppermute(block, axes, [(source, i) for i, source in enumerate(sources)])

    along_t_x = jnp.stack([operator[7] + operator[8], operator[1] + operator[2]])
    odd_level = lax.axis_index("gz") % 2 == 1
    along_z = jnp.stack(
        [jnp.where(odd_level, operator[5], operator[6]), jnp.where(odd_level, operator[6], operator[5])]
    )
    upper = lax.axis_index("gx") % 2 == 1
    mine = jnp.where(upper, along_z, along_t_x)
    theirs = swap(jnp.where(upper, along_t_x, along_z), mate)
    inside = real_blocks(jnp.stack([operator[0], operator[3] + operator[4]])[None], dim, True)[0]
    around = real_blocks(jnp.stack([mine, theirs]), dim, False)

    pair = jnp.stack([half, swap(half, mate)])
    for sweep_id in range(ITERS - 1):
        moved = [swap(pair, first), swap(pair, second)]
        kept = half + apply(jnp.concatenate([pair[0], pair[1]], 1), inside, lax.Precision.HIGH)
        if sweep_id == 1:
            rows, clover, kept = lax.optimization_barrier((*held[:2], kept))
            local, kept = lax.optimization_barrier((local_term(rows, clover), kept))
        if sweep_id == 2:
            stored, kept = lax.optimization_barrier((held[2], kept))
            vectors, kept = lax.optimization_barrier((hold(stored), kept))
        def along(link):
            return lax.dot_general(
                moved[link], around[:, link], (((2,), (2,)), ((0,), (0,))), precision=lax.Precision.HIGH
            )

        part = along(1) + (jnp.stack([kept, jnp.zeros_like(kept)]) + along(0))
        if sweep_id < ITERS - 2:
            other = swap(part, mate)
            pair = part + jnp.stack([other[1], other[0]])
    return (part[0], swap(part[1], mate)), vectors, local


def body(residual, null_vectors, clover_inverse, coarse_op, vector_count):
    rhs_count = residual.shape[0]
    vec_total = null_vectors.shape[1]
    coarse_dim = 2 * vec_total
    sites = residual.shape[3]
    rows = residual.transpose(0, 2, 1, 3)
    stored = null_vectors.transpose(0, 2, 1, 3)
    half, used = restrict(vector_count, rows, stored)

    coarse_op, half = lax.optimization_barrier((coarse_op, half))
    operator = coarse_op.reshape(9, 2, coarse_dim * coarse_dim)
    held = (rows, clover_inverse.transpose(0, 2, 3, 1, 4), stored)
    if shares_chip():
        summands, vectors, local = sweep_in_pairs(half, operator, coarse_dim, held)
    else:
        summands, vectors, local = sweep_alone(half, operator, coarse_dim, held)
    return extend(summands, used, vectors, local).transpose(0, 2, 1, 3)


def solution(mesh):
    in_specs = (
        P(None, None, None, ("gx", "gz", "ta")),
        P(None, None, None, ("gx", "gz", "ta")),
        P(None, None, None, None, ("gx", "gz", "ta")),
        P(("gx", "gz", "ta"), None, None, None),
        P(("gx", "gz", "ta")),
    )
    out_specs = P(None, None, None, ("gx", "gz", "ta"))
    return jax.shard_map(body, mesh=mesh, in_specs=in_specs, out_specs=out_specs, check_vma=False)
```

```python
import jax
import jax.numpy as jnp
from jax import lax
from jax.experimental import pallas as pl
from jax.experimental.pallas import tpu as pltpu
from jax.sharding import PartitionSpec as P

ITERS = 5


omega_step = 0.5
exact = lax.Precision.HIGHEST
axes = ("gx", "gz", "ta")


def routes():
    total = lax.axis_size("gx")
    plane_y = min(8, total // 2)
    plane_x = total // plane_y

    def ring(count):
        up = [(i + 1) % count for i in range(count)]
        down = [(i - 1) % count for i in range(count)]
        if count % 2:
            return up, down, False
        even = [(up if i % 2 == 0 else down)[i] for i in range(count)]
        odd = [(down if i % 2 == 0 else up)[i] for i in range(count)]
        return even, odd, True

    links = []
    first, second, paired = ring(plane_x)
    links.append(
        [("gx", tuple(way[g // plane_y] * plane_y + g % plane_y for g in range(total))) for way in (first, second)]
        + [paired, lax.axis_index("gx") // plane_y]
    )
    first, second, paired = ring(plane_y)
    links.append(
        [("gx", tuple((g // plane_y) * plane_y + way[g % plane_y] for g in range(total))) for way in (first, second)]
        + [paired, lax.axis_index("gx") % plane_y]
    )
    for axis in ("gz", "ta"):
        first, second, paired = ring(lax.axis_size(axis))
        links.append([(axis, tuple(first)), (axis, tuple(second)), paired, lax.axis_index(axis)])
    return links


def fetch(block, link):
    axis, sources = link
    return lax.ppermute(block, axis, [(source, i) for i, source in enumerate(sources)])


def restrict_kernel(
    count_ref, rows_hbm, vectors_hbm, out_ref, used_ref, rows_ref, vectors_ref, scratch, sems
):
    rhs, parts, _, sites = rows_ref.shape
    vecs = vectors_ref.shape[2]
    half = parts // 2
    copies = []
    for chi in range(2):
        span = pl.ds(half * chi, half)
        copies.append(
            [
                pltpu.make_async_copy(rows_hbm.at[:, span], rows_ref.at[:, span], sems.at[2 * chi]),
                pltpu.make_async_copy(vectors_hbm.at[:, span], vectors_ref.at[:, span], sems.at[2 * chi + 1]),
            ]
        )
    for copy in copies[0][::-1] + copies[1][::-1]:
        copy.start()
    for chi in range(2):
        for copy in copies[chi]:
            copy.wait()
        total = jnp.zeros((2 * rhs, 2 * vecs), jnp.float32)
        for c in range(half * chi, half * chi + half):
            rows = rows_ref[:, c].reshape(2 * rhs, sites)
            vectors = jnp.concatenate([vectors_ref[0, c], vectors_ref[1, c]], 0)
            total += lax.dot_general(
                rows, vectors, (((1,), (1,)), ((), ())), preferred_element_type=jnp.float32
            )
        scratch[chi, :, : 2 * vecs] = total
    real, imag = [], []
    for chi in range(2):
        even = scratch[chi, pl.ds(0, rhs, stride=2), :]
        odd = scratch[chi, pl.ds(1, rhs, stride=2), :]
        real.append(even[:, :vecs] + odd[:, vecs : 2 * vecs])
        imag.append(odd[:, :vecs] - even[:, vecs : 2 * vecs])
    lane = lax.broadcasted_iota(jnp.int32, (rhs, vecs), 1)
    used = jnp.where(lane < count_ref[0], 1.0, 0.0)
    out_ref[...] = jnp.concatenate([omega_step * part * used for part in real + imag], 1)
    used_ref[...] = jnp.concatenate([used] * 4, 1)


def restrict(count, rows, vectors):
    rhs, vecs = rows.shape[0], vectors.shape[2]
    in_vmem = pl.BlockSpec(memory_space=pltpu.VMEM)
    in_hbm = pl.BlockSpec(memory_space=pltpu.HBM)
    return pl.pallas_call(
        restrict_kernel,
        out_shape=[jax.ShapeDtypeStruct((rhs, 4 * vecs), jnp.float32)] * 2,
        in_specs=[pl.BlockSpec(memory_space=pltpu.SMEM), in_hbm, in_hbm],
        out_specs=[in_vmem, in_vmem],
        scratch_shapes=[
            pltpu.VMEM(rows.shape, rows.dtype),
            pltpu.VMEM(vectors.shape, vectors.dtype),
            pltpu.VMEM((2, 2 * rhs, 128), jnp.float32),
            pltpu.SemaphoreType.DMA((4,)),
        ],
        compiler_params=pltpu.CompilerParams(vmem_limit_bytes=55168 * 2**10),
        cost_estimate=pl.CostEstimate(flops=10**7, bytes_accessed=5 * 10**5, transcendentals=0),
    )(count, rows, vectors)


def extend_kernel(first_ref, second_ref, used_ref, vectors_ref, local_ref, out_hbm, out_ref, scratch, sems):
    rhs, parts, _, sites = out_ref.shape
    vecs = vectors_ref.shape[1] // 2
    half = parts // 2
    coarse = (first_ref[...] + second_ref[...]) * used_ref[...]
    for chi in range(2):
        real = coarse[:, chi * vecs : (chi + 1) * vecs]
        imag = coarse[:, (2 + chi) * vecs : (3 + chi) * vecs]
        scratch[chi, pl.ds(0, rhs, stride=2), : 2 * vecs] = jnp.concatenate([real, -imag], 1)
        scratch[chi, pl.ds(1, rhs, stride=2), : 2 * vecs] = jnp.concatenate([imag, real], 1)
    copies = []
    step = half // 2
    for piece in range(4):
        weights = scratch[piece // 2, :, : 2 * vecs].astype(jnp.bfloat16)
        for c in range(step * piece, step * piece + step):
            lift = jnp.dot(weights, vectors_ref[c], preferred_element_type=jnp.float32)
            total = (local_ref[c] + lift).astype(jnp.bfloat16)
            out_ref[:, c] = total.reshape(rhs, 2, sites)
        span = pl.ds(step * piece, step)
        copies.append(pltpu.make_async_copy(out_ref.at[:, span], out_hbm.at[:, span], sems.at[piece]))
        copies[-1].start()
    for copy in copies:
        copy.wait()


small = pltpu.CompilerParams(vmem_limit_bytes=8 * 2**20)
in_vmem = pl.BlockSpec(memory_space=pltpu.VMEM)


def extend(summands, used, vectors, local):
    parts, _, sites = vectors.shape
    rhs = used.shape[0]
    shape = (rhs, parts, 2, sites)
    return pl.pallas_call(
        extend_kernel,
        out_shape=jax.ShapeDtypeStruct(shape, jnp.bfloat16),
        in_specs=[in_vmem] * 5,
        out_specs=pl.BlockSpec(memory_space=pltpu.HBM),
        scratch_shapes=[
            pltpu.VMEM(shape, jnp.bfloat16),
            pltpu.VMEM((2, 2 * rhs, 128), jnp.float32),
            pltpu.SemaphoreType.DMA((4,)),
        ],
        compiler_params=small,
        cost_estimate=pl.CostEstimate(flops=10**7, bytes_accessed=10**6, transcendentals=0),
    )(*summands, used, vectors, local)


def hold_kernel(vectors_ref, out_ref):
    vecs = vectors_ref.shape[2]
    for c in range(vectors_ref.shape[1]):
        out_ref[c] = jnp.concatenate([vectors_ref[0, c], vectors_ref[1, c]], 0)


def hold(vectors):
    _, parts, vecs, sites = vectors.shape
    return pl.pallas_call(
        hold_kernel,
        out_shape=jax.ShapeDtypeStruct((parts, 2 * vecs, sites), vectors.dtype),
        in_specs=[in_vmem],
        out_specs=in_vmem,
        compiler_params=small,
        cost_estimate=pl.CostEstimate(flops=10**5, bytes_accessed=10**5, transcendentals=0),
    )(vectors)


def local_kernel(rows_ref, clover_ref, out_ref):
    rhs, parts, _, sites = rows_ref.shape
    half = parts // 2
    row = lax.broadcasted_iota(jnp.int32, (2 * rhs, 2 * rhs), 0)
    col = lax.broadcasted_iota(jnp.int32, (2 * rhs, 2 * rhs), 1)
    turn = jnp.where((row % 2 == 0) & (col == row + 1), -1.0, 0.0)
    turn = jnp.where((row % 2 == 1) & (col == row - 1), 1.0, turn).astype(jnp.bfloat16)
    for chi in range(2):
        for start in range(0, sites, 128):
            lanes = slice(start, start + 128)
            plain, turned = [], []
            for b in range(half):
                rows = rows_ref[:, half * chi + b, :, lanes].reshape(2 * rhs, 128)
                plain.append(rows.astype(jnp.float32))
                turned.append(jnp.dot(turn, rows, preferred_element_type=jnp.float32))
            for a in range(half):
                total = jnp.zeros((2 * rhs, 128), jnp.float32)
                for b in range(half):
                    real = clover_ref[0, a, b, :, lanes].astype(jnp.float32)[chi : chi + 1]
                    imag = clover_ref[1, a, b, :, lanes].astype(jnp.float32)[chi : chi + 1]
                    total += real * plain[b] + imag * turned[b]
                out_ref[half * chi + a, :, lanes] = total


def local_term(rows, clover):
    rhs, parts, _, sites = rows.shape
    return pl.pallas_call(
        local_kernel,
        out_shape=jax.ShapeDtypeStruct((parts, 2 * rhs, sites), jnp.float32),
        in_specs=[in_vmem] * 2,
        out_specs=in_vmem,
        compiler_params=small,
        cost_estimate=pl.CostEstimate(flops=10**5, bytes_accessed=10**5, transcendentals=0),
    )(rows, clover)


def real_form(matrix, dim):
    matrix = matrix.reshape(2, dim, dim)
    upper = jnp.concatenate([matrix[0], -matrix[1]], 1)
    lower = jnp.concatenate([matrix[1], matrix[0]], 1)
    return omega_step * jnp.concatenate([upper, lower], 0)


def apply(vector, matrix, precision=exact):
    return lax.dot_general(vector, matrix, (((1,), (1,)), ((), ())), precision=precision)


def own_form(operator, dim):
    return jnp.eye(2 * dim, dtype=jnp.float32) - real_form(operator, dim)


def sweep_alone(half, operator, dim, held):
    grouped = {}
    for way, (first, second, paired, place) in enumerate(routes()):
        plus, minus = operator[2 * way + 1], operator[2 * way + 2]
        if first == second:
            grouped[first] = plus + minus
        else:
            swap = (place % 2 == 1) & paired
            grouped[first] = jnp.where(swap, minus, plus)
            grouped[second] = jnp.where(swap, plus, minus)

    def reach(link):
        axis, sources = link
        return ("gz", "ta", "gx").index(axis), -max(abs(source - i) for i, source in enumerate(sources))

    order = sorted(grouped, key=reach)
    own = own_form(operator[0], dim)
    around = jnp.concatenate([-real_form(grouped[link], dim) for link in order], 1)
    coarse = half
    for sweep_id in range(ITERS - 1):
        moved = [fetch(coarse, link) for link in order]
        kept = half + apply(coarse, own)
        if sweep_id == 1:
            rows, clover, kept = lax.optimization_barrier((*held[:2], kept))
            local, kept = lax.optimization_barrier((local_term(rows, clover), kept))
        if sweep_id == 2:
            stored, kept = lax.optimization_barrier((held[2], kept))
            vectors, kept = lax.optimization_barrier((hold(stored), kept))
        added = apply(jnp.concatenate(moved, 1), around)
        coarse = kept + added
    return (kept, added), vectors, local


def shares_chip():
    total, depth, slabs = (lax.axis_size(axis) for axis in axes)
    return total == 4 and depth == 4 and slabs == 2


def pair_routes():
    total, depth, slabs = (lax.axis_size(axis) for axis in axes)

    def device_at(group, level, slab):
        return (group * depth + level) * slabs + slab

    first, second, mate = [], [], []
    for group in range(total):
        for level in range(depth):
            for slab in range(slabs):
                step = 1 if level % 2 == 0 else -1
                if group % 2 == 0:
                    first.append(device_at(group, level, 1 - slab))
                    second.append(device_at(group ^ 2, level, slab))
                else:
                    first.append(device_at(group, (level - step) % depth, slab))
                    second.append(device_at(group, (level + step) % depth, slab))
                mate.append(device_at(group ^ 1, level, slab))
    return first, second, mate


def real_blocks(flat, dim, has_own):
    blocks = flat.shape[0]

    def kernel(flat_ref, out_ref, rows_ref):
        packed = jnp.concatenate([flat_ref[block, link] for block in range(blocks) for link in range(2)], 0)
        for i in range(dim):
            rows_ref[pl.ds(i, 4 * blocks, stride=dim), :] = packed[:, i * dim : (i + 1) * dim]
        row = lax.broadcasted_iota(jnp.int32, (dim, dim), 0)
        col = lax.broadcasted_iota(jnp.int32, (dim, dim), 1)
        for block in range(blocks):
            for link in range(2):
                base = (2 * block + link) * 2 * dim
                real = -omega_step * rows_ref[base : base + dim]
                imag = omega_step * rows_ref[base + dim : base + 2 * dim]
                if has_own and link == 0:
                    real = real + jnp.where(row == col, 1.0, 0.0)
                place, left = ((block,), 2 * dim * link) if has_own else ((block, link), 0)
                low, high = pl.ds(0, dim), pl.ds(dim, dim)
                near, beyond = pl.ds(left, dim), pl.ds(left + dim, dim)
                out_ref[(*place, low, near)] = real
                out_ref[(*place, low, beyond)] = imag
                out_ref[(*place, high, near)] = -imag
                out_ref[(*place, high, beyond)] = real

    shape = (blocks, 2 * dim, 4 * dim) if has_own else (blocks, 2, 2 * dim, 2 * dim)
    return pl.pallas_call(
        kernel,
        out_shape=jax.ShapeDtypeStruct(shape, jnp.float32),
        in_specs=[pl.BlockSpec(memory_space=pltpu.VMEM)],
        out_specs=pl.BlockSpec(memory_space=pltpu.VMEM),
        scratch_shapes=[pltpu.VMEM((4 * blocks * dim, dim), jnp.float32)],
        compiler_params=pltpu.CompilerParams(vmem_limit_bytes=8 * 2**20),
        cost_estimate=pl.CostEstimate(flops=10**5, bytes_accessed=10**5, transcendentals=0),
    )(flat)


def sweep_in_pairs(half, operator, dim, held):
    first, second, mate = pair_routes()

    def swap(block, sources):
        return lax.ppermute(block, axes, [(source, i) for i, source in enumerate(sources)])

    along_t_x = jnp.stack([operator[7] + operator[8], operator[1] + operator[2]])
    odd_level = lax.axis_index("gz") % 2 == 1
    along_z = jnp.stack(
        [jnp.where(odd_level, operator[5], operator[6]), jnp.where(odd_level, operator[6], operator[5])]
    )
    upper = lax.axis_index("gx") % 2 == 1
    mine = jnp.where(upper, along_z, along_t_x)
    theirs = swap(jnp.where(upper, along_t_x, along_z), mate)
    inside = real_blocks(jnp.stack([operator[0], operator[3] + operator[4]])[None], dim, True)[0]
    around = real_blocks(jnp.stack([mine, theirs]), dim, False)

    pair = jnp.stack([half, swap(half, mate)])
    for sweep_id in range(ITERS - 1):
        moved = [swap(pair, first), swap(pair, second)]
        kept = half + apply(jnp.concatenate([pair[0], pair[1]], 1), inside, lax.Precision.HIGH)
        if sweep_id == 1:
            rows, clover, kept = lax.optimization_barrier((*held[:2], kept))
            local, kept = lax.optimization_barrier((local_term(rows, clover), kept))
        if sweep_id == 2:
            stored, kept = lax.optimization_barrier((held[2], kept))
            vectors, kept = lax.optimization_barrier((hold(stored), kept))
        def along(link):
            return lax.dot_general(
                moved[link], around[:, link], (((2,), (2,)), ((0,), (0,))), precision=lax.Precision.HIGH
            )

        part = along(1) + (jnp.stack([kept, jnp.zeros_like(kept)]) + along(0))
        if sweep_id < ITERS - 2:
            other = swap(part, mate)
            pair = part + jnp.stack([other[1], other[0]])
    return (part[0], swap(part[1], mate)), vectors, local


def body(residual, null_vectors, clover_inverse, coarse_op, vector_count):
    rhs_count = residual.shape[0]
    vec_total = null_vectors.shape[1]
    coarse_dim = 2 * vec_total
    sites = residual.shape[3]
    rows = residual.transpose(0, 2, 1, 3)
    stored = null_vectors.transpose(0, 2, 1, 3)
    half, used = restrict(vector_count, rows, stored)

    coarse_op, half = lax.optimization_barrier((coarse_op, half))
    operator = coarse_op.reshape(9, 2, coarse_dim * coarse_dim)
    held = (rows, clover_inverse.transpose(0, 2, 3, 1, 4), stored)
    if shares_chip():
        summands, vectors, local = sweep_in_pairs(half, operator, coarse_dim, held)
    else:
        summands, vectors, local = sweep_alone(half, operator, coarse_dim, held)
    return extend(summands, used, vectors, local).transpose(0, 2, 1, 3)


def solution(mesh):
    in_specs = (
        P(None, None, None, ("gx", "gz", "ta")),
        P(None, None, None, ("gx", "gz", "ta")),
        P(None, None, None, None, ("gx", "gz", "ta")),
        P(("gx", "gz", "ta"), None, None, None),
        P(("gx", "gz", "ta")),
    )
    out_specs = P(None, None, None, ("gx", "gz", "ta"))
    return jax.shard_map(body, mesh=mesh, in_specs=in_specs, out_specs=out_specs, check_vma=False)
```

```python
import jax
import jax.numpy as jnp
from jax import lax
from jax.experimental import pallas as pl
from jax.experimental.pallas import tpu as pltpu
from jax.sharding import PartitionSpec as P

ITERS = 5


omega_step = 0.5
exact = lax.Precision.HIGHEST
axes = ("gx", "gz", "ta")


def routes():
    total = lax.axis_size("gx")
    plane_y = min(8, total // 2)
    plane_x = total // plane_y

    def ring(count):
        up = [(i + 1) % count for i in range(count)]
        down = [(i - 1) % count for i in range(count)]
        if count % 2:
            return up, down, False
        even = [(up if i % 2 == 0 else down)[i] for i in range(count)]
        odd = [(down if i % 2 == 0 else up)[i] for i in range(count)]
        return even, odd, True

    links = []
    first, second, paired = ring(plane_x)
    links.append(
        [("gx", tuple(way[g // plane_y] * plane_y + g % plane_y for g in range(total))) for way in (first, second)]
        + [paired, lax.axis_index("gx") // plane_y]
    )
    first, second, paired = ring(plane_y)
    links.append(
        [("gx", tuple((g // plane_y) * plane_y + way[g % plane_y] for g in range(total))) for way in (first, second)]
        + [paired, lax.axis_index("gx") % plane_y]
    )
    for axis in ("gz", "ta"):
        first, second, paired = ring(lax.axis_size(axis))
        links.append([(axis, tuple(first)), (axis, tuple(second)), paired, lax.axis_index(axis)])
    return links


def fetch(block, link):
    axis, sources = link
    return lax.ppermute(block, axis, [(source, i) for i, source in enumerate(sources)])


def restrict_kernel(
    count_ref, rows_hbm, vectors_hbm, out_ref, used_ref, rows_ref, vectors_ref, scratch, sems
):
    rhs, parts, _, sites = rows_ref.shape
    vecs = vectors_ref.shape[2]
    half = parts // 2
    copies = []
    for chi in range(2):
        span = pl.ds(half * chi, half)
        copies.append(
            [
                pltpu.make_async_copy(rows_hbm.at[:, span], rows_ref.at[:, span], sems.at[2 * chi]),
                pltpu.make_async_copy(vectors_hbm.at[:, span], vectors_ref.at[:, span], sems.at[2 * chi + 1]),
            ]
        )
    for copy in copies[0] + copies[1]:
        copy.start()
    for chi in range(2):
        for copy in copies[chi]:
            copy.wait()
        total = jnp.zeros((2 * rhs, 2 * vecs), jnp.float32)
        for c in range(half * chi, half * chi + half):
            rows = rows_ref[:, c].reshape(2 * rhs, sites)
            vectors = jnp.concatenate([vectors_ref[0, c], vectors_ref[1, c]], 0)
            total += lax.dot_general(
                rows, vectors, (((1,), (1,)), ((), ())), preferred_element_type=jnp.float32
            )
        scratch[chi, :, : 2 * vecs] = total
    real, imag = [], []
    for chi in range(2):
        even = scratch[chi, pl.ds(0, rhs, stride=2), :]
        odd = scratch[chi, pl.ds(1, rhs, stride=2), :]
        real.append(even[:, :vecs] + odd[:, vecs : 2 * vecs])
        imag.append(odd[:, :vecs] - even[:, vecs : 2 * vecs])
    lane = lax.broadcasted_iota(jnp.int32, (rhs, vecs), 1)
    used = jnp.where(lane < count_ref[0], 1.0, 0.0)
    out_ref[...] = jnp.concatenate([omega_step * part * used for part in real + imag], 1)
    used_ref[...] = jnp.concatenate([used] * 4, 1)


def restrict(count, rows, vectors):
    rhs, vecs = rows.shape[0], vectors.shape[2]
    in_vmem = pl.BlockSpec(memory_space=pltpu.VMEM)
    in_hbm = pl.BlockSpec(memory_space=pltpu.HBM)
    return pl.pallas_call(
        restrict_kernel,
        out_shape=[jax.ShapeDtypeStruct((rhs, 4 * vecs), jnp.float32)] * 2,
        in_specs=[pl.BlockSpec(memory_space=pltpu.SMEM), in_hbm, in_hbm],
        out_specs=[in_vmem, in_vmem],
        scratch_shapes=[
            pltpu.VMEM(rows.shape, rows.dtype),
            pltpu.VMEM(vectors.shape, vectors.dtype),
            pltpu.VMEM((2, 2 * rhs, 128), jnp.float32),
            pltpu.SemaphoreType.DMA((4,)),
        ],
        compiler_params=pltpu.CompilerParams(vmem_limit_bytes=55168 * 2**10),
        cost_estimate=pl.CostEstimate(flops=10**7, bytes_accessed=5 * 10**5, transcendentals=0),
    )(count, rows, vectors)


def extend_kernel(first_ref, second_ref, used_ref, vectors_ref, local_ref, out_hbm, out_ref, scratch, sems):
    rhs, parts, _, sites = out_ref.shape
    vecs = vectors_ref.shape[1] // 2
    half = parts // 2
    coarse = (first_ref[...] + second_ref[...]) * used_ref[...]
    for chi in range(2):
        real = coarse[:, chi * vecs : (chi + 1) * vecs]
        imag = coarse[:, (2 + chi) * vecs : (3 + chi) * vecs]
        scratch[chi, pl.ds(0, rhs, stride=2), : 2 * vecs] = jnp.concatenate([real, -imag], 1)
        scratch[chi, pl.ds(1, rhs, stride=2), : 2 * vecs] = jnp.concatenate([imag, real], 1)
    copies = []
    step = half // 3
    for piece in range(6):
        weights = scratch[piece // 3, :, : 2 * vecs].astype(jnp.bfloat16)
        for c in range(step * piece, step * piece + step):
            lift = jnp.dot(weights, vectors_ref[c], preferred_element_type=jnp.float32)
            total = (local_ref[c] + lift).astype(jnp.bfloat16)
            out_ref[:, c] = total.reshape(rhs, 2, sites)
        span = pl.ds(step * piece, step)
        copies.append(pltpu.make_async_copy(out_ref.at[:, span], out_hbm.at[:, span], sems.at[piece]))
        copies[-1].start()
    for copy in copies:
        copy.wait()


small = pltpu.CompilerParams(vmem_limit_bytes=8 * 2**20)
in_vmem = pl.BlockSpec(memory_space=pltpu.VMEM)


def extend(summands, used, vectors, local):
    parts, _, sites = vectors.shape
    rhs = used.shape[0]
    shape = (rhs, parts, 2, sites)
    return pl.pallas_call(
        extend_kernel,
        out_shape=jax.ShapeDtypeStruct(shape, jnp.bfloat16),
        in_specs=[in_vmem] * 5,
        out_specs=pl.BlockSpec(memory_space=pltpu.HBM),
        scratch_shapes=[
            pltpu.VMEM(shape, jnp.bfloat16),
            pltpu.VMEM((2, 2 * rhs, 128), jnp.float32),
            pltpu.SemaphoreType.DMA((6,)),
        ],
        compiler_params=small,
        cost_estimate=pl.CostEstimate(flops=10**7, bytes_accessed=10**6, transcendentals=0),
    )(*summands, used, vectors, local)


def hold_kernel(vectors_ref, out_ref):
    vecs = vectors_ref.shape[2]
    for c in range(vectors_ref.shape[1]):
        out_ref[c] = jnp.concatenate([vectors_ref[0, c], vectors_ref[1, c]], 0)


def hold(vectors):
    _, parts, vecs, sites = vectors.shape
    return pl.pallas_call(
        hold_kernel,
        out_shape=jax.ShapeDtypeStruct((parts, 2 * vecs, sites), vectors.dtype),
        in_specs=[in_vmem],
        out_specs=in_vmem,
        compiler_params=small,
        cost_estimate=pl.CostEstimate(flops=10**5, bytes_accessed=10**5, transcendentals=0),
    )(vectors)


def local_kernel(rows_ref, clover_ref, out_ref):
    rhs, parts, _, sites = rows_ref.shape
    half = parts // 2
    row = lax.broadcasted_iota(jnp.int32, (2 * rhs, 2 * rhs), 0)
    col = lax.broadcasted_iota(jnp.int32, (2 * rhs, 2 * rhs), 1)
    turn = jnp.where((row % 2 == 0) & (col == row + 1), -1.0, 0.0)
    turn = jnp.where((row % 2 == 1) & (col == row - 1), 1.0, turn).astype(jnp.bfloat16)
    for chi in range(2):
        for start in range(0, sites, 128):
            lanes = slice(start, start + 128)
            plain, turned = [], []
            for b in range(half):
                rows = rows_ref[:, half * chi + b, :, lanes].reshape(2 * rhs, 128)
                plain.append(rows.astype(jnp.float32))
                turned.append(jnp.dot(turn, rows, preferred_element_type=jnp.float32))
            for a in range(half):
                total = jnp.zeros((2 * rhs, 128), jnp.float32)
                for b in range(half):
                    real = clover_ref[0, a, b, :, lanes].astype(jnp.float32)[chi : chi + 1]
                    imag = clover_ref[1, a, b, :, lanes].astype(jnp.float32)[chi : chi + 1]
                    total += real * plain[b] + imag * turned[b]
                out_ref[half * chi + a, :, lanes] = total


def local_term(rows, clover):
    rhs, parts, _, sites = rows.shape
    return pl.pallas_call(
        local_kernel,
        out_shape=jax.ShapeDtypeStruct((parts, 2 * rhs, sites), jnp.float32),
        in_specs=[in_vmem] * 2,
        out_specs=in_vmem,
        compiler_params=small,
        cost_estimate=pl.CostEstimate(flops=10**5, bytes_accessed=10**5, transcendentals=0),
    )(rows, clover)


def real_form(matrix, dim):
    matrix = matrix.reshape(2, dim, dim)
    upper = jnp.concatenate([matrix[0], -matrix[1]], 1)
    lower = jnp.concatenate([matrix[1], matrix[0]], 1)
    return omega_step * jnp.concatenate([upper, lower], 0)


def apply(vector, matrix, precision=exact):
    return lax.dot_general(vector, matrix, (((1,), (1,)), ((), ())), precision=precision)


def own_form(operator, dim):
    return jnp.eye(2 * dim, dtype=jnp.float32) - real_form(operator, dim)


def sweep_alone(half, operator, dim, held):
    grouped = {}
    for way, (first, second, paired, place) in enumerate(routes()):
        plus, minus = operator[2 * way + 1], operator[2 * way + 2]
        if first == second:
            grouped[first] = plus + minus
        else:
            swap = (place % 2 == 1) & paired
            grouped[first] = jnp.where(swap, minus, plus)
            grouped[second] = jnp.where(swap, plus, minus)

    def reach(link):
        axis, sources = link
        return ("gz", "ta", "gx").index(axis), -max(abs(source - i) for i, source in enumerate(sources))

    order = sorted(grouped, key=reach)
    own = own_form(operator[0], dim)
    around = jnp.concatenate([-real_form(grouped[link], dim) for link in order], 1)
    coarse = half
    for sweep_id in range(ITERS - 1):
        moved = [fetch(coarse, link) for link in order]
        kept = half + apply(coarse, own)
        if sweep_id == 1:
            rows, clover, kept = lax.optimization_barrier((*held[:2], kept))
            local, kept = lax.optimization_barrier((local_term(rows, clover), kept))
        if sweep_id == 2:
            stored, kept = lax.optimization_barrier((held[2], kept))
            vectors, kept = lax.optimization_barrier((hold(stored), kept))
        added = apply(jnp.concatenate(moved, 1), around)
        coarse = kept + added
    return (kept, added), vectors, local


def shares_chip():
    total, depth, slabs = (lax.axis_size(axis) for axis in axes)
    return total == 4 and depth == 4 and slabs == 2


def pair_routes():
    total, depth, slabs = (lax.axis_size(axis) for axis in axes)

    def device_at(group, level, slab):
        return (group * depth + level) * slabs + slab

    first, second, mate = [], [], []
    for group in range(total):
        for level in range(depth):
            for slab in range(slabs):
                step = 1 if level % 2 == 0 else -1
                if group % 2 == 0:
                    first.append(device_at(group, level, 1 - slab))
                    second.append(device_at(group ^ 2, level, slab))
                else:
                    first.append(device_at(group, (level - step) % depth, slab))
                    second.append(device_at(group, (level + step) % depth, slab))
                mate.append(device_at(group ^ 1, level, slab))
    return first, second, mate


def real_blocks(flat, dim, has_own):
    blocks = flat.shape[0]

    def kernel(flat_ref, out_ref, rows_ref):
        packed = jnp.concatenate([flat_ref[block, link] for block in range(blocks) for link in range(2)], 0)
        for i in range(dim):
            rows_ref[pl.ds(i, 4 * blocks, stride=dim), :] = packed[:, i * dim : (i + 1) * dim]
        row = lax.broadcasted_iota(jnp.int32, (dim, dim), 0)
        col = lax.broadcasted_iota(jnp.int32, (dim, dim), 1)
        for block in range(blocks):
            for link in range(2):
                base = (2 * block + link) * 2 * dim
                real = -omega_step * rows_ref[base : base + dim]
                imag = omega_step * rows_ref[base + dim : base + 2 * dim]
                if has_own and link == 0:
                    real = real + jnp.where(row == col, 1.0, 0.0)
                place, left = ((block,), 2 * dim * link) if has_own else ((block, link), 0)
                low, high = pl.ds(0, dim), pl.ds(dim, dim)
                near, beyond = pl.ds(left, dim), pl.ds(left + dim, dim)
                out_ref[(*place, low, near)] = real
                out_ref[(*place, low, beyond)] = imag
                out_ref[(*place, high, near)] = -imag
                out_ref[(*place, high, beyond)] = real

    shape = (blocks, 2 * dim, 4 * dim) if has_own else (blocks, 2, 2 * dim, 2 * dim)
    return pl.pallas_call(
        kernel,
        out_shape=jax.ShapeDtypeStruct(shape, jnp.float32),
        in_specs=[pl.BlockSpec(memory_space=pltpu.VMEM)],
        out_specs=pl.BlockSpec(memory_space=pltpu.VMEM),
        scratch_shapes=[pltpu.VMEM((4 * blocks * dim, dim), jnp.float32)],
        compiler_params=pltpu.CompilerParams(vmem_limit_bytes=8 * 2**20),
        cost_estimate=pl.CostEstimate(flops=10**5, bytes_accessed=10**5, transcendentals=0),
    )(flat)


def sweep_in_pairs(half, operator, dim, held):
    first, second, mate = pair_routes()

    def swap(block, sources):
        return lax.ppermute(block, axes, [(source, i) for i, source in enumerate(sources)])

    along_t_x = jnp.stack([operator[7] + operator[8], operator[1] + operator[2]])
    odd_level = lax.axis_index("gz") % 2 == 1
    along_z = jnp.stack(
        [jnp.where(odd_level, operator[5], operator[6]), jnp.where(odd_level, operator[6], operator[5])]
    )
    upper = lax.axis_index("gx") % 2 == 1
    mine = jnp.where(upper, along_z, along_t_x)
    theirs = swap(jnp.where(upper, along_t_x, along_z), mate)
    inside = real_blocks(jnp.stack([operator[0], operator[3] + operator[4]])[None], dim, True)[0]
    around = real_blocks(jnp.stack([mine, theirs]), dim, False)

    pair = jnp.stack([half, swap(half, mate)])
    for sweep_id in range(ITERS - 1):
        moved = [swap(pair, first), swap(pair, second)]
        kept = half + apply(jnp.concatenate([pair[0], pair[1]], 1), inside, lax.Precision.HIGH)
        if sweep_id == 1:
            rows, clover, kept = lax.optimization_barrier((*held[:2], kept))
            local, kept = lax.optimization_barrier((local_term(rows, clover), kept))
        if sweep_id == 2:
            stored, kept = lax.optimization_barrier((held[2], kept))
            vectors, kept = lax.optimization_barrier((hold(stored), kept))
        def along(link):
            return lax.dot_general(
                moved[link], around[:, link], (((2,), (2,)), ((0,), (0,))), precision=lax.Precision.HIGH
            )

        part = along(1) + (jnp.stack([kept, jnp.zeros_like(kept)]) + along(0))
        if sweep_id < ITERS - 2:
            other = swap(part, mate)
            pair = part + jnp.stack([other[1], other[0]])
    return (part[0], swap(part[1], mate)), vectors, local


def body(residual, null_vectors, clover_inverse, coarse_op, vector_count):
    rhs_count = residual.shape[0]
    vec_total = null_vectors.shape[1]
    coarse_dim = 2 * vec_total
    sites = residual.shape[3]
    rows = residual.transpose(0, 2, 1, 3)
    stored = null_vectors.transpose(0, 2, 1, 3)
    half, used = restrict(vector_count, rows, stored)

    coarse_op, half = lax.optimization_barrier((coarse_op, half))
    operator = coarse_op.reshape(9, 2, coarse_dim * coarse_dim)
    held = (rows, clover_inverse.transpose(0, 2, 3, 1, 4), stored)
    if shares_chip():
        summands, vectors, local = sweep_in_pairs(half, operator, coarse_dim, held)
    else:
        summands, vectors, local = sweep_alone(half, operator, coarse_dim, held)
    return extend(summands, used, vectors, local).transpose(0, 2, 1, 3)


def solution(mesh):
    in_specs = (
        P(None, None, None, ("gx", "gz", "ta")),
        P(None, None, None, ("gx", "gz", "ta")),
        P(None, None, None, None, ("gx", "gz", "ta")),
        P(("gx", "gz", "ta"), None, None, None),
        P(("gx", "gz", "ta")),
    )
    out_specs = P(None, None, None, ("gx", "gz", "ta"))
    return jax.shard_map(body, mesh=mesh, in_specs=in_specs, out_specs=out_specs, check_vma=False)
```
